32 devices in a mesh: seq: 8 (over y, x, core), tp: 4 (over z).
Axes of the slice: x: 2, y: 2, z: 4, core: 2. Of those that a mesh axis runs over, the one named last changes fastest.
Arguments:
- tokens: bfloat16 [8192, 1024], P('seq'), may hold values from -6 to 6
- cotangent: bfloat16 [8192, 1024], P('seq'), may hold values from -6 to 6
- lengths: int32 [8], replicated, may hold values from 1 to 4096, 8192 in all
- retrieve: int32 [8, 8], replicated, may hold values from 0 to 63
- owners: int32 [98], replicated, may hold values from 0 to 103, as said below
- masters: float32 [4, 104, 32, 1024], P('tp', 'seq'), may hold values from -0.1875 to 0.1875
- first_moment: float32 [4, 104, 32, 1024], P('tp', 'seq')
- second_moment: float32 [4, 104, 32, 1024], P('tp', 'seq'), as said below
- averaged: float32 [4, 104, 32, 1024], P('tp', 'seq'), may hold values from -0.1875 to 0.1875
- statistics: float32 [4, 104, 32, 32], P('tp', 'seq'), as said below
- bases: float32 [4, 104, 32, 32], P('tp', 'seq'), as said below
- gains: float32 [2, 1024], replicated, may hold values from 0.5 to 1.5
- gain_first: float32 [2, 1024], replicated, may hold values from -27.1529 to 27.1529
- gain_second: float32 [2, 1024], replicated, may hold values from 106.496 to 409.6
Outputs:
- output: bfloat16 [8192, 1024], P('seq')
- grad_input: float32 [8192, 1024], P('seq')
- new_masters: float32 [4, 104, 32, 1024], P('tp', 'seq')
- new_first: float32 [4, 104, 32, 1024], P('tp', 'seq')
- new_second: float32 [4, 104, 32, 1024], P('tp', 'seq')
- new_average: float32 [4, 104, 32, 1024], P('tp', 'seq')
- new_statistics: float32 [4, 104, 32, 32], P('tp', 'seq')
- new_bases: float32 [4, 104, 32, 32], P('tp', 'seq')
- new_gains: float32 [2, 1024], replicated
- new_gain_first: float32 [2, 1024], replicated
- new_gain_second: float32 [2, 1024], replicated
The draws below stay inside these ranges and needn't reach their ends.
Inputs may be any that keep to these rules, and one draw needn't show every extreme that they name: `owners`: the 98 panels name different slots, and slot 103 is always named. `second_moment`: positive. `statistics`: each slot's matrix is symmetric with a dominant positive diagonal. `bases`: each slot's matrix is orthogonal.
All inputs are finite; a program needn't handle non-finite values.
Results may differ from the reference program's by a relative error of at most 0.011.
Values may be sent and summed in bfloat16 or wider, within the bound.
No kernel may reach another device: no remote copies, remote signals or barrier semaphores. Data moves between devices by JAX's collectives and lax.ppermute only.
A program may use at most 256 MiB of HBM per device.

```python
import math
import jax
import jax.numpy as jnp
import numpy as np
from jax import lax

D = 1024
H = 8
HD = 128
FF = 2816
TOK_DEV = 1024
TOPK = 8
MEMB = 128
NDOC = 8
PW = 32
STEP = 10
TOKENS = 8192
NKB = 64
NP = 98
SLOTS = 104
N_SEQ = 8
N_TP = 4


def grad_size():
    return 0.3 * TOKENS ** 0.5


def draw_owners(key, part):
    key = jax.random.fold_in(key, 5)
    picks = jax.random.permutation(key, SLOTS - 1)[:NP - 1]
    values = jnp.concatenate([picks, jnp.full((1,), SLOTS - 1, jnp.int32)]).astype(jnp.int32)
    order = jax.random.permutation(jax.random.fold_in(key, 6), NP)
    return values[order].astype(jnp.int32)


def draw_first_moment(key, part):
    key = jax.random.fold_in(key, 1)
    scale = 0.1 / 0.9 * grad_size()
    shape = (N_TP, SLOTS, PW, D)
    return (scale * jnp.clip(jax.random.normal(key, shape, jnp.float32), -6.0, 6.0)).astype(jnp.float32)


def draw_second_moment(key, part):
    key = jax.random.fold_in(key, 2)
    base = 0.05 / 0.95 * grad_size() * grad_size()
    spread = jax.random.uniform(key, (N_TP, SLOTS, PW, D), jnp.float32, 0.0, 1.3862944)
    return (base * jnp.exp(spread)).astype(jnp.float32)


def draw_statistics(key, part):
    key = jax.random.fold_in(key, 3)
    base = 0.05 / 0.95 * D * grad_size() * grad_size()
    diagonal = base * jnp.exp(jax.random.uniform(key, (N_TP, SLOTS, PW), jnp.float32, 0.0, 1.3862944))
    other = jax.random.uniform(jax.random.fold_in(key, 7), (N_TP, SLOTS, PW, PW), jnp.float32, -1.0, 1.0)
    other = 0.5 * (other + jnp.swapaxes(other, -1, -2)) * base * 0.5 / PW
    identity = jnp.eye(PW, dtype=jnp.float32)
    return (other * (1.0 - identity) + diagonal[..., None] * identity).astype(jnp.float32)


def draw_bases(key, part):
    key = jax.random.fold_in(key, 4)
    vector = jax.random.normal(key, (N_TP, SLOTS, PW), jnp.float32)
    length = jnp.sum(vector * vector, axis=-1)
    outer = vector[..., :, None] * vector[..., None, :]
    return (jnp.eye(PW, dtype=jnp.float32) - 2.0 * outer / length[..., None, None]).astype(jnp.float32)


def plant(entries, rng, smallest, largest):
    extent = entries.shape
    spot = [jax.random.randint(jax.random.fold_in(rng, axis), (), 0, extent[axis]) for axis in range(len(extent))]
    entries = entries.at[tuple(spot)].set(smallest)
    longest = extent.index(max(extent))
    spot[longest] = (spot[longest] + 1) % extent[longest]
    return entries.at[tuple(spot)].set(largest)


def levels(stream_key, extent, pieces, smallest, high):
    factor_of = 1.0
    for axis_at, parts in pieces:
        heights = jax.random.uniform(jax.random.fold_in(jax.random.fold_in(stream_key, 6), axis_at), (parts,), jnp.float32, smallest / len(pieces), high / len(pieces))
        factor_of = factor_of * jnp.repeat(jnp.exp(heights), extent[axis_at] // parts).reshape((-1,) + (1,) * (len(extent) - 1 - axis_at))
    return factor_of


def split_up(amount, total, bound, skew):
    portions = [(1 << 20) // math.isqrt(grade ** skew) + 1 for grade in range(2, amount + 1)]
    spare, counts = total - bound - (amount - 1), [1] * (amount - 1)
    while spare > 0:
        free = [i for i in range(amount - 1) if counts[i] < bound]
        pool, remaining = sum([portions[i] for i in free]), spare
        for i in free:
            addition = min(bound - counts[i], max(1, remaining * portions[i] // pool), spare)
            counts[i] = counts[i] + addition
            spare = spare - addition
    return np.array([bound] + counts)


def ragged(key, amount, total, limit, lean):
    if amount == 2:
        one = jax.random.randint(key, (), max(1, total - limit), min(limit, total - 1) + 1)
        return jnp.stack([one, total - one])
    sizes = jnp.asarray(split_up(amount, total, limit, lean), jnp.int32)
    twos = (amount - 1) // 2
    source_of, receiver = sizes[1:1 + 2 * twos:2], sizes[2:2 + 2 * twos:2]
    margin = jnp.minimum(source_of - 1, limit - receiver)
    moved = jax.random.randint(jax.random.fold_in(key, 1), (twos,), 0, 1 << 20) % (margin + 1)
    sizes = sizes.at[1:1 + 2 * twos:2].set(source_of - moved).at[2:2 + 2 * twos:2].set(receiver + moved)
    return sizes[jax.random.permutation(jax.random.fold_in(key, 2), amount)]


def centred(rng, extent, scale, bound, pieces=(), kind=jnp.bfloat16):
    loudness = levels(rng, extent, pieces, -0.22, 0.18) if pieces else 1.0
    entries = jax.random.normal(rng, extent, jnp.float32) * scale * loudness
    return jnp.minimum(jnp.maximum(entries, -bound), bound).astype(kind)


def setup_inputs(seed: int = 0) -> dict:
    key_of = jax.random.split(jax.random.key(seed), 15)
    return {
        "tokens": centred(key_of[0], (TOKENS, D), 1.0, 6.0, ((0, 8),)),
        "cotangent": centred(key_of[1], (TOKENS, D), 1.0, 6.0, ((0, 8),)),
        "lengths": ragged(key_of[2], NDOC, TOKENS, TOKENS // 2, 2).astype(jnp.int32),
        "retrieve": plant(jax.random.randint(key_of[3], (N_SEQ, TOPK), 0, NKB), jax.random.fold_in(key_of[3], 1), 0, NKB - 1).astype(jnp.int32),
        "owners": draw_owners(jax.random.fold_in(key_of[14], 71), 0),
        "masters": centred(key_of[5], (N_TP, SLOTS, PW, D), D ** -0.5, 0.1875, ((0, 4), (1, 8)), jnp.float32),
        "first_moment": draw_first_moment(jax.random.fold_in(key_of[14], 71), 0),
        "second_moment": draw_second_moment(jax.random.fold_in(key_of[14], 71), 0),
        "averaged": centred(key_of[8], (N_TP, SLOTS, PW, D), D ** -0.5, 0.1875, ((0, 4), (1, 8)), jnp.float32),
        "statistics": draw_statistics(jax.random.fold_in(key_of[14], 71), 0),
        "bases": draw_bases(jax.random.fold_in(key_of[14], 71), 0),
        "gains": jnp.clip(1.0 + 0.1 * jax.random.normal(key_of[11], (2, D), jnp.float32), 0.5, 1.5),
        "gain_first": centred(key_of[12], (2, D), (0.05 * TOKENS ** 0.5), 27.1529, (), jnp.float32),
        "gain_second": jnp.clip(jnp.exp(jax.random.uniform(key_of[13], (2, D), jnp.float32, math.log(106.496), math.log(409.6))), 106.496, 409.6),
    }


@jax.custom_vjp
def low(v):
    return lax.optimization_barrier(v.astype(jnp.bfloat16)).astype(jnp.float32)

@jax.custom_vjp
def low_back(v):
    return v

def low_keep(v):
    return (low(v), None)

def low_pass(kept, grad):
    return (grad,)

def back_keep(v):
    return (v, None)

def back_low(kept, grad):
    return (low(grad),)
low.defvjp(low_keep, low_pass)
low_back.defvjp(back_keep, back_low)
EPSILON = 1e-06
RATE = 0.02
GAIN_RATE = 0.5
BETA_ONE = 0.9
BETA_TWO = 0.95
ADAM_EPSILON = 1e-08
WEIGHT_DECAY = 0.01
AVERAGE_DECAY = 0.8
NEGATIVE = -1e+30

def document_of(positions, starts):
    return lax.optimization_barrier(jnp.sum((positions[:, None] >= starts[None, :]).astype(jnp.int32), axis=1)) - 1

def visible_mask(query_pos, key_pos, starts, recalled):
    query_doc = document_of(query_pos, starts)
    key_doc = document_of(key_pos, starts)
    member = jnp.any((key_pos // MEMB)[:, None] == recalled[None, :], axis=1)
    same_doc = (query_doc[:, None] == key_doc[None, :]) & (key_pos[None, :] <= query_pos[:, None])
    memory = (key_doc[None, :] < query_doc[:, None]) & member[None, :]
    return same_doc | memory

def orthonormal(matrix):
    columns = []
    for index in range(matrix.shape[-1]):
        vector = matrix[..., index]
        for previous in columns:
            vector = vector - lax.optimization_barrier(jnp.sum(previous * vector, axis=-1, keepdims=True)) * previous
        vector = vector * lax.rsqrt(lax.optimization_barrier(jnp.sum(vector * vector, axis=-1, keepdims=True)))
        columns.append(vector)
    return jnp.stack(columns, axis=-1)

def soap_step(gradient, weight, first_state, second, statistic, basis_old):
    high = lax.Precision.HIGHEST
    new_stat = BETA_TWO * statistic + (1.0 - BETA_TWO) * jnp.einsum('spd,sqd->spq', gradient, gradient, precision=high)
    rotated = jnp.einsum('spq,spd->sqd', basis_old, gradient, precision=high)
    new_first = BETA_ONE * first_state + (1.0 - BETA_ONE) * rotated
    new_second = BETA_TWO * second + (1.0 - BETA_TWO) * rotated * rotated
    direction = new_first / (1.0 - BETA_ONE ** STEP) / (jnp.sqrt(new_second / (1.0 - BETA_TWO ** STEP)) + ADAM_EPSILON)
    update = jnp.einsum('spq,sqd->spd', basis_old, direction, precision=high)
    new_weight = weight - RATE * (update + WEIGHT_DECAY * weight)
    new_basis = orthonormal(jnp.einsum('spq,sqr->spr', new_stat, basis_old, precision=high))
    return (new_weight, new_first, new_second, new_stat, new_basis)

def adam_gain(gradient, weight, first_state, second):
    new_first = BETA_ONE * first_state + (1.0 - BETA_ONE) * gradient
    new_second = BETA_TWO * second + (1.0 - BETA_TWO) * gradient * gradient
    direction = new_first / (1.0 - BETA_ONE ** STEP) / (jnp.sqrt(new_second / (1.0 - BETA_TWO ** STEP)) + ADAM_EPSILON)
    return (weight - GAIN_RATE * direction, new_first, new_second)

def matmul_high(left, right):
    return jnp.dot(left, right, precision=lax.Precision.HIGHEST)

def reference(tokens, cotangent, lengths, retrieve, owners, masters, first_moment, second_moment, averaged, statistics, bases, gains, gain_first, gain_second):
    heads_dev = H // N_TP
    ff_dev = FF // N_TP
    query_width = heads_dev * HD
    starts = jnp.cumsum(lengths) - lengths
    score_scale = HD ** (-0.5)
    key_pos = jnp.arange(TOKENS, dtype=jnp.int32)

    def forward(inputs, weight_all, gain_pair):
        panel_rows = low(weight_all)[:, owners].reshape(N_TP, -1, D)

        def gather_rows(first_row, last_row):
            return panel_rows[:, first_row:last_row].reshape(-1, D)
        w_query = gather_rows(0, query_width)
        w_key = gather_rows(query_width, 2 * query_width)
        w_value = gather_rows(2 * query_width, 3 * query_width)
        w_out = gather_rows(3 * query_width, 4 * query_width)
        base_row = 4 * query_width
        w_gate = gather_rows(base_row, base_row + ff_dev)
        w_up = gather_rows(base_row + ff_dev, base_row + 2 * ff_dev)
        w_down = gather_rows(base_row + 2 * ff_dev, base_row + 3 * ff_dev)
        inverse_one = lax.rsqrt(lax.optimization_barrier(jnp.mean(inputs * inputs, axis=-1, keepdims=True)) + EPSILON)
        normed_one = low(inputs * inverse_one * gain_pair[0])
        queries = low_back(low(matmul_high(normed_one, w_query.T))).reshape(TOKENS, H, HD)
        key_rows = low_back(low(matmul_high(normed_one, w_key.T))).reshape(TOKENS, H, HD)
        value_rows = low_back(low(matmul_high(normed_one, w_value.T))).reshape(TOKENS, H, HD)

        def attend(block_index):
            query_part = lax.dynamic_slice_in_dim(queries, block_index * TOK_DEV, TOK_DEV, 0)
            query_pos = block_index * TOK_DEV + jnp.arange(TOK_DEV, dtype=jnp.int32)
            visible = visible_mask(query_pos, key_pos, starts, retrieve[block_index])
            raw_scores = jnp.einsum('qhd,khd->hqk', query_part, key_rows, precision=lax.Precision.HIGHEST)
            scores = low_back(raw_scores * score_scale)
            masked = jnp.where(visible[None], scores, NEGATIVE)
            probs = jax.nn.softmax(masked, axis=-1)
            return jnp.einsum('hqk,khd->qhd', low(probs), value_rows, precision=lax.Precision.HIGHEST)
        attended = lax.map(jax.checkpoint(attend), jnp.arange(N_SEQ, dtype=jnp.int32))
        attended = low_back(low(attended.reshape(TOKENS, H * HD)))
        branch = low_back(matmul_high(attended, w_out))
        mixed = inputs + branch
        inverse_two = lax.rsqrt(lax.optimization_barrier(jnp.mean(mixed * mixed, axis=-1, keepdims=True)) + EPSILON)
        normed_two = low(mixed * inverse_two * gain_pair[1])
        gate = low_back(matmul_high(normed_two, w_gate.T))
        up_rows = low_back(matmul_high(normed_two, w_up.T))
        hidden = low_back(low(jax.nn.silu(gate) * up_rows))
        return mixed + low_back(matmul_high(hidden, w_down))
    inputs = tokens.astype(jnp.float32)
    result, pullback = jax.vjp(forward, inputs, masters, gains)
    grad_input, grad_masters, grad_gains = pullback(cotangent.astype(jnp.float32))
    shape_slots = (N_TP * SLOTS, PW, D)
    shape_small = (N_TP * SLOTS, PW, PW)
    new_weight, new_first, new_second, new_stat, new_basis = soap_step(grad_masters.reshape(shape_slots), masters.reshape(shape_slots), first_moment.reshape(shape_slots), second_moment.reshape(shape_slots), statistics.reshape(shape_small), bases.reshape(shape_small))
    new_average = AVERAGE_DECAY * averaged.reshape(shape_slots) + (1.0 - AVERAGE_DECAY) * new_weight
    new_gains, new_gain_first, new_gain_second = adam_gain(grad_gains, gains, gain_first, gain_second)
    big_shape = (N_TP, SLOTS, PW, D)
    small_shape = (N_TP, SLOTS, PW, PW)
    return (result.astype(jnp.bfloat16), grad_input, new_weight.reshape(big_shape), new_first.reshape(big_shape), new_second.reshape(big_shape), new_average.reshape(big_shape), new_stat.reshape(small_shape), new_basis.reshape(small_shape), new_gains, new_gain_first, new_gain_second)
```

```python
import functools

import jax
import jax.numpy as jnp
from jax import lax
from jax.experimental import pallas as pl
from jax.experimental.pallas import tpu as pltpu
from jax.sharding import PartitionSpec as P

H = 8
HD = 128
FF = 2816
MEMB = 128
STEP = 10

EPSILON = 1e-06
RATE = 0.02
GAIN_RATE = 0.5
BETA_ONE = 0.9
BETA_TWO = 0.95
ADAM_EPSILON = 1e-08
WEIGHT_DECAY = 0.01
AVERAGE_DECAY = 0.8
NEGATIVE = -1e30
START_TOP = -1e29
LOG2E = 1.4426950408889634

BF = jnp.bfloat16
F32 = jnp.float32
I32 = jnp.int32
HIGH = lax.Precision.HIGHEST
ANY = pl.BlockSpec(memory_space=pl.ANY)
SMEM = pl.BlockSpec(memory_space=pltpu.SMEM)
VMEM = pl.BlockSpec(memory_space=pltpu.VMEM)
VMEM_BYTES = 58 * 2**20

NT = (((1,), (1,)), ((), ()))
NN = (((1,), (0,)), ((), ()))
TN = (((0,), (0,)), ((), ()))


def mm(left, right, dims):
    return lax.dot_general(left, right, dims, preferred_element_type=F32)


def params(**more):
    return pltpu.CompilerParams(vmem_limit_bytes=VMEM_BYTES, **more)


def cost(flops, moved, exps=0):
    return pl.CostEstimate(flops=int(flops), bytes_accessed=int(moved), transcendentals=int(exps))


def routes(count):
    bits = []
    bit = 2
    while bit < count:
        bits.append(bit)
        bit *= 2
    return bits, bits[::-1]


def swap(value, count, bit):
    return lax.ppermute(value, "seq", [(i, i ^ bit) for i in range(count)])


def gather_seq(own, count, order):
    pieces = {0: own}
    for bit in [*order, 1]:
        pieces.update({m | bit: swap(p, count, bit) for m, p in pieces.items()})
    return [pieces[m] for m in range(count)]


def plus(left, right):
    return (left.astype(F32) + right.astype(F32)).astype(left.dtype)


def reduce_seq(parts, count, order):
    parts = dict(enumerate(parts))
    bits = [1, *order[::-1]]
    for at, bit in enumerate(bits):
        stay = [m for m in parts if not m & bit]
        came = {m: swap(parts[m | bit], count, bit) for m in stay}
        if at == len(bits) - 1:
            return parts[0], came[0]
        parts = {m: plus(parts[m], came[m]) for m in stay}
    return None


def ring(value, count, step):
    return lax.ppermute(value, "tp", [(i, (i + step) % count) for i in range(count)])


def gather_tp(own, count):
    pieces = [own]
    for _ in range(count - 1):
        pieces.append(ring(pieces[-1], count, 1))
    return pieces


def reduce_tp(parts, count):
    total = parts[count - 1]
    for k in range(count - 2, -1, -1):
        came = ring(total, count, -1)
        if k == 0:
            return parts[0], came
        total = plus(parts[k], came)
    return None


def sum_all(value, n_seq, n_tp):
    for axis, count in (("seq", n_seq), ("tp", n_tp)):
        bit = 1
        while bit < count:
            value = value + lax.ppermute(value, axis, [(i, i ^ bit) for i in range(count)])
            bit *= 2
    return value


def panel_copies(owners_ref, me, first, amount, slots_dev, split, pieces, view, sem, back):
    def one(i, carry):
        slot = owners_ref[first + i]
        spot = lax.bitwise_xor(slot // slots_dev, me)
        row = slot % slots_dev
        for m, (low, high) in enumerate(pieces):
            for ref, base, size in ((low, 0, split), (high, split, slots_dev - split)):

                @pl.when((spot == m) & (row >= base) & (row < base + size))
                def _(ref=ref, base=base):
                    there = ref.at[row - base]
                    source, target = (view(i), there) if back else (there, view(i))
                    pltpu.make_async_copy(source, target, sem).start()

        return carry

    lax.fori_loop(0, amount, one, 0)


def norm_rows(rows, gain):
    inverse = lax.rsqrt(jnp.mean(rows * rows, axis=-1, keepdims=True) + EPSILON)
    unit = rows * inverse
    return unit, inverse, unit * gain


def project_kernel(cfg, meta, owners, x_ref, gain_ref, *refs):
    n, qw, slots_dev, split, panel = cfg
    low, high = refs[:n], refs[n : 2 * n]
    q_ref, k_ref, v_ref, normed_ref, w_ref, sem = refs[2 * n :]
    amount = 3 * qw // panel

    @pl.when(pl.program_id(0) == 0)
    def _():
        panel_copies(
            owners, meta[0], 0, amount, slots_dev, split, list(zip(low, high, strict=True)),
            lambda i: w_ref.at[i], sem, False,
        )

    _, _, normed = norm_rows(x_ref[...].astype(F32), gain_ref[0:1, :])
    normed = normed.astype(BF)
    normed_ref[...] = normed

    @pl.when(pl.program_id(0) == 0)
    def _():
        pltpu.make_async_copy(w_ref, w_ref, sem).wait()

    for at, out in enumerate((q_ref, k_ref, v_ref)):
        w = w_ref[at * qw // panel : (at + 1) * qw // panel].reshape(qw, x_ref.shape[1])
        out[...] = mm(normed, w, NT).astype(BF)


def project_in(meta, owners, x, gains, pieces, qw, slots_dev, split, panel):
    n = len(pieces)
    tok, d = x.shape
    tile = 256
    out = lambda w: pl.BlockSpec((tile, w), lambda i: (i, 0))
    return pl.pallas_call(
        functools.partial(project_kernel, (n, qw, slots_dev, split, panel)),
        grid=(tok // tile,),
        in_specs=[SMEM, SMEM, out(d), pl.BlockSpec(gains.shape, lambda i: (0, 0))] + [ANY] * (2 * n),
        out_specs=[out(qw), out(qw), out(qw), out(d)],
        out_shape=[jax.ShapeDtypeStruct((tok, qw), BF)] * 3 + [jax.ShapeDtypeStruct((tok, d), BF)],
        scratch_shapes=[pltpu.VMEM((3 * qw // panel, panel, d), BF), pltpu.SemaphoreType.DMA],
        compiler_params=params(),
        cost_estimate=cost(6 * tok * d * qw, 4 * tok * d + 6 * qw * (tok + d)),
        name="project",
    )(meta, owners, x, gains, *[p[0] for p in pieces], *[p[1] for p in pieces])


def weights_kernel(cfg, meta, owners, *refs):
    n, sizes, slots_dev, split = cfg
    pieces = list(zip(refs[:n], refs[n : 2 * n], strict=True))
    outs, sem = refs[2 * n : -1], refs[-1]
    first = 0
    for out, size in zip(outs, sizes, strict=True):
        panel_copies(
            owners, meta[0], first, size, slots_dev, split, pieces,
            lambda i, out=out: out.at[i], sem.at[0], False,
        )
        first += size
    for out in outs:
        pltpu.make_async_copy(out, out, sem.at[0]).wait()


def order_weights(meta, owners, pieces, sizes, slots_dev, split):
    n = len(pieces)
    panel, d = pieces[0][0].shape[1:]
    got = pl.pallas_call(
        functools.partial(weights_kernel, (n, sizes, slots_dev, split)),
        in_specs=[SMEM, SMEM] + [ANY] * (2 * n),
        out_specs=[VMEM] * len(sizes),
        out_shape=[jax.ShapeDtypeStruct((s, panel, d), BF) for s in sizes],
        scratch_shapes=[pltpu.SemaphoreType.DMA((1,))],
        compiler_params=params(),
        cost_estimate=cost(0, 4 * sum(sizes) * panel * d),
        name="order_weights",
    )(meta, owners, *[p[0] for p in pieces], *[p[1] for p in pieces])
    return [g.reshape(-1, d) for g in got]


def doc_start(meta, positions, docs):
    start = jnp.int32(0)
    found = jnp.zeros_like(positions)
    for at in range(docs):
        found = jnp.where(positions >= start, start, found)
        start = start + meta[1 + at]
    return found


def load_pieces(me, pieces, buffer, sem, tok):
    for m, piece in enumerate(pieces):
        owner = lax.bitwise_xor(me, m)
        at = pl.multiple_of(owner * tok, tok)
        pltpu.make_async_copy(piece, buffer.at[pl.ds(at, tok)], sem).start()


def member_table(meta, table, docs, picks, blocks):
    def clear(i, c):
        table[i] = 0
        return c

    lax.fori_loop(0, blocks, clear, 0)
    for e in range(picks):
        table[meta[1 + docs + e]] = 1


def memory_list(meta, blocks_ref, docs, picks, limit):
    count = jnp.int32(0)
    for e in range(picks):
        block = meta[1 + docs + e]
        fresh = (block + 1) * MEMB <= limit
        for other in range(e):
            fresh = fresh & (meta[1 + docs + other] != block)

        @pl.when(fresh)
        def _(count=count, block=block):
            blocks_ref[count] = block

        count = count + fresh.astype(I32)
    return count


def hide(scores, at, table, starts, queries, fill):
    rows = scores.shape[0]
    row = lax.broadcasted_iota(I32, (MEMB, scores.shape[1]), 0)
    kept = []
    for b in range(rows // MEMB):
        base = at + b * MEMB
        lowest = starts * (1 - table[base // MEMB]) - base
        seen = (row >= lowest) & (row <= queries - base)
        kept.append(jnp.where(seen, scores[b * MEMB : (b + 1) * MEMB], fill))
    return jnp.concatenate(kept, axis=0)


def attend_kernel(cfg, meta, q_ref, *refs):
    n, docs, picks, qt, kt = cfg
    keys, values = refs[:n], refs[n : 2 * n]
    out_ref, wide_ref, log_ref, kbuf, vbuf, acc, table, blocks, sems = refs[2 * n :]
    tok, width = q_ref.shape
    me = meta[0]
    factor = HD**-0.5 * LOG2E
    load_pieces(me, keys, kbuf, sems.at[0], tok)
    load_pieces(me, values, vbuf, sems.at[1], tok)
    member_table(meta, table, docs, picks, kbuf.shape[0] // MEMB)
    pltpu.make_async_copy(kbuf, kbuf, sems.at[0]).wait()
    pltpu.make_async_copy(vbuf, vbuf, sems.at[1]).wait()
    for head in range(width // HD):
        cols = slice(head * HD, (head + 1) * HD)

        def query_tile(t, carry, head=head, cols=cols):
            base = pl.multiple_of(t * qt, qt)
            first = me * tok + base
            queries = first + lax.broadcasted_iota(I32, (1, qt), 1)
            starts = doc_start(meta, queries, docs)
            low_tile = doc_start(meta, first, docs) // kt
            high_tile = (first + qt - 1) // kt
            q = q_ref[pl.ds(base, qt), cols]
            acc[...] = jnp.zeros_like(acc)

            def visit(at, rows, state, masked):
                top, total = state
                scores = mm(kbuf[pl.ds(at, rows), cols], q, NT)
                if masked:
                    scores = hide(scores, at, table, starts, queries, NEGATIVE)
                new_top = jnp.maximum(top, jnp.max(scores, axis=0, keepdims=True))
                fade = jnp.exp2((top - new_top) * factor)
                probs = jnp.exp2((scores - new_top) * factor)
                total = total * fade + jnp.sum(probs, axis=0, keepdims=True)
                acc[...] = acc[...] * fade + mm(vbuf[pl.ds(at, rows), cols], probs.astype(BF), TN)
                return new_top, total

            def dense(i, state):
                return visit(pl.multiple_of(i * kt, kt), kt, state, True)

            def memory(i, state):
                return visit(pl.multiple_of(blocks[i] * MEMB, MEMB), MEMB, state, False)

            count = memory_list(meta, blocks, docs, picks, low_tile * kt)
            state = (jnp.full((1, qt), START_TOP, F32), jnp.zeros((1, qt), F32))
            state = lax.fori_loop(low_tile, high_tile + 1, dense, state)
            top, total = lax.fori_loop(0, count, memory, state)
            rows = jnp.transpose(acc[...] * (1.0 / total))
            wide_ref[pl.ds(base, qt), cols] = rows
            out_ref[pl.ds(base, qt), cols] = rows.astype(BF)
            log_ref[head : head + 1, pl.ds(base, qt)] = top * factor + jnp.log2(total)
            return carry

        lax.fori_loop(0, tok // qt, query_tile, 0)


def attend(meta, q, keys, values, docs, picks):
    n = len(keys)
    tok, width = q.shape
    qt, kt = 512, 512
    return pl.pallas_call(
        functools.partial(attend_kernel, (n, docs, picks, qt, kt)),
        in_specs=[SMEM, VMEM] + [ANY] * (2 * n),
        out_specs=[VMEM] * 3,
        out_shape=[
            jax.ShapeDtypeStruct((tok, width), BF),
            jax.ShapeDtypeStruct((tok, width), F32),
            jax.ShapeDtypeStruct((width // HD, tok), F32),
        ],
        scratch_shapes=[
            pltpu.VMEM((n * tok, width), BF),
            pltpu.VMEM((n * tok, width), BF),
            pltpu.VMEM((HD, qt), F32),
            pltpu.SMEM((n * tok // MEMB,), I32),
            pltpu.SMEM((picks,), I32),
            pltpu.SemaphoreType.DMA((2,)),
        ],
        compiler_params=params(),
        cost_estimate=cost(4 * tok * n * tok * width // 2, 4 * n * tok * width, tok * n * tok),
        name="attend",
    )(meta, q, *keys, *values)


def attend_back_kernel(cfg, meta, q_ref, g_ref, wide_ref, log_ref, *refs):
    n, docs, picks, qt, kt = cfg
    keys, values = refs[:n], refs[n : 2 * n]
    dq_ref = refs[2 * n]
    dk_out, dv_out = refs[2 * n + 1 : 3 * n + 1], refs[3 * n + 1 : 4 * n + 1]
    kbuf, vbuf, dk_acc, dv_acc, acc, stage, table, blocks, sems = refs[4 * n + 1 :]
    tok, width = q_ref.shape
    me = meta[0]
    scale = HD**-0.5
    factor = scale * LOG2E
    load_pieces(me, keys, kbuf, sems.at[0], tok)
    load_pieces(me, values, vbuf, sems.at[1], tok)
    member_table(meta, table, docs, picks, kbuf.shape[0] // MEMB)

    def clear(i, c):
        at = pl.ds(pl.multiple_of(i * 256, 256), 256)
        dk_acc[at, :] = jnp.zeros((256, width), F32)
        dv_acc[at, :] = jnp.zeros((256, width), F32)
        return c

    lax.fori_loop(0, kbuf.shape[0] // 256, clear, 0)
    pltpu.make_async_copy(kbuf, kbuf, sems.at[0]).wait()
    pltpu.make_async_copy(vbuf, vbuf, sems.at[1]).wait()
    for head in range(width // HD):
        cols = slice(head * HD, (head + 1) * HD)

        def query_tile(t, carry, head=head, cols=cols):
            base = pl.multiple_of(t * qt, qt)
            first = me * tok + base
            queries = first + lax.broadcasted_iota(I32, (1, qt), 1)
            starts = doc_start(meta, queries, docs)
            low_tile = doc_start(meta, first, docs) // kt
            high_tile = (first + qt - 1) // kt
            q = q_ref[pl.ds(base, qt), cols]
            grad = g_ref[pl.ds(base, qt), cols]
            logs = log_ref[head : head + 1, pl.ds(base, qt)]
            product = grad.astype(F32) * wide_ref[pl.ds(base, qt), cols]
            delta = jnp.sum(jnp.transpose(product), axis=0, keepdims=True)
            acc[...] = jnp.zeros_like(acc)

            def visit(at, rows, masked):
                here = pl.ds(at, rows)
                k = kbuf[here, cols]
                probs = jnp.exp2(mm(k, q, NT) * factor - logs)
                if masked:
                    probs = hide(probs, at, table, starts, queries, 0.0)
                slopes = probs * (mm(vbuf[here, cols], grad, NT) - delta)
                slopes = slopes.astype(BF)
                dv_acc[here, cols] += mm(probs.astype(BF), grad, NN)
                dk_acc[here, cols] += mm(slopes, q, NN)
                acc[...] += mm(k, slopes, TN)

            def dense(i, c):
                visit(pl.multiple_of(i * kt, kt), kt, True)
                return c

            def memory(i, c):
                visit(pl.multiple_of(blocks[i] * MEMB, MEMB), MEMB, False)
                return c

            count = memory_list(meta, blocks, docs, picks, low_tile * kt)
            lax.fori_loop(low_tile, high_tile + 1, dense, 0)
            lax.fori_loop(0, count, memory, 0)
            dq_ref[pl.ds(base, qt), cols] = (jnp.transpose(acc[...]) * scale).astype(BF)
            return carry

        lax.fori_loop(0, tok // qt, query_tile, 0)

    def put(slot, m):
        which, out = (0, dk_out[m]) if slot == 0 else (1, dv_out[m])
        return pltpu.make_async_copy(stage.at[which], out, sems.at[2 + which])

    for m in range(n):
        at = pl.ds(pl.multiple_of(lax.bitwise_xor(me, m) * tok, tok), tok)
        for which in range(2):
            if m:
                put(which, m - 1).wait()
            rows = dk_acc[at, :] * scale if which == 0 else dv_acc[at, :]
            stage[which] = rows.astype(BF)
            put(which, m).start()
    for which in range(2):
        put(which, n - 1).wait()


def attend_back(meta, q, grad, wide, logs, keys, values, docs, picks):
    n = len(keys)
    tok, width = q.shape
    qt, kt = 512, 512
    got = pl.pallas_call(
        functools.partial(attend_back_kernel, (n, docs, picks, qt, kt)),
        in_specs=[SMEM] + [VMEM] * 4 + [ANY] * (2 * n),
        out_specs=[VMEM] + [ANY] * (2 * n),
        out_shape=[jax.ShapeDtypeStruct((tok, width), BF)] * (2 * n + 1),
        scratch_shapes=[
            pltpu.VMEM((n * tok, width), BF),
            pltpu.VMEM((n * tok, width), BF),
            pltpu.VMEM((n * tok, width), F32),
            pltpu.VMEM((n * tok, width), F32),
            pltpu.VMEM((HD, qt), F32),
            pltpu.VMEM((2, tok, width), BF),
            pltpu.SMEM((n * tok // MEMB,), I32),
            pltpu.SMEM((picks,), I32),
            pltpu.SemaphoreType.DMA((4,)),
        ],
        compiler_params=params(),
        cost_estimate=cost(10 * tok * n * tok * width // 2, 8 * n * tok * width, tok * n * tok),
        name="attend_back",
    )(meta, q, grad, wide, logs, *keys, *values)
    return got[0], got[1 : n + 1], got[n + 1 :]


def feed_kernel(cfg, meta, x_ref, g_ref, gain_ref, wg, wu, wd, *refs):
    n = cfg
    heads, wo = refs[:n], refs[n : 2 * n]
    mixed_ref, normed_ref, hidden_ref, dgate_ref, dup_ref, back_ref, feed_ref = refs[2 * n :]
    mixed = x_ref[...].astype(F32)
    for a, w in zip(heads, wo, strict=True):
        mixed = mixed + mm(a[...], w[...], NN)
    mixed_ref[...] = mixed
    _, _, normed = norm_rows(mixed, gain_ref[1:2, :])
    normed = normed.astype(BF)
    normed_ref[...] = normed
    gate = mm(normed, wg[...], NT)
    up = mm(normed, wu[...], NT)
    sigma = jax.nn.sigmoid(gate)
    silu = gate * sigma
    hidden = (silu * up).astype(BF)
    hidden_ref[...] = hidden
    grad = g_ref[...]
    d_hidden = mm(grad, wd[...], NT).astype(BF).astype(F32)
    d_gate = (d_hidden * up * (sigma * (1.0 + gate * (1.0 - sigma)))).astype(BF)
    d_up = (d_hidden * silu).astype(BF)
    dgate_ref[...] = d_gate
    dup_ref[...] = d_up
    back_ref[...] = (mm(d_gate, wg[...], NN) + mm(d_up, wu[...], NN)).astype(BF)
    feed_ref[...] = mm(hidden, wd[...], NN).astype(BF)


def feed_forward(meta, x, grad, gains, wg, wu, wd, heads, wo):
    n = len(heads)
    tok, d = x.shape
    ff, qw = wg.shape[0], wo[0].shape[0]
    tile = tok // n
    rows = lambda w: pl.BlockSpec((tile, w), lambda i, meta: (i, 0))
    turned = lambda w: pl.BlockSpec((tile, w), lambda i, meta: ((meta[0] - i + n) % n, 0))
    whole = lambda a: pl.BlockSpec(a.shape, lambda i, meta: (0, 0))
    shape = lambda w, t: jax.ShapeDtypeStruct((tok, w), t)
    return pl.pallas_call(
        functools.partial(feed_kernel, n),
        grid_spec=pltpu.PrefetchScalarGridSpec(
            num_scalar_prefetch=1,
            grid=(n,),
            in_specs=[rows(d), rows(d), whole(gains), whole(wg), whole(wu), whole(wd)]
            + [rows(qw)] * n + [whole(w) for w in wo],
            out_specs=[rows(d), rows(d), rows(ff), rows(ff), rows(ff), turned(d), turned(d)],
        ),
        out_shape=[shape(d, F32), shape(d, BF), shape(ff, BF), shape(ff, BF), shape(ff, BF), shape(d, BF), shape(d, BF)],
        compiler_params=params(),
        cost_estimate=cost(2 * tok * d * (6 * ff + n * qw), 20 * tok * d, tok * ff),
        name="feed_forward",
    )(meta, x, grad, gains, wg, wu, wd, *heads, *wo)


def place_kernel(n, meta, *refs):
    pieces, out = refs[:n], refs[n]
    rows = pieces[0].shape[0]
    for k, piece in enumerate(pieces):
        block = lax.rem(meta[0] - k + n, n)
        out[pl.ds(pl.multiple_of(block * rows, rows), rows), :] = piece[...].astype(out.dtype)


def place(meta, pieces, kind=BF):
    n = len(pieces)
    rows, d = pieces[0].shape
    return pl.pallas_call(
        functools.partial(place_kernel, n),
        in_specs=[SMEM] + [VMEM] * n,
        out_specs=VMEM,
        out_shape=jax.ShapeDtypeStruct((n * rows, d), kind),
        compiler_params=params(),
        cost_estimate=cost(0, 6 * n * rows * d),
        name="place",
    )(meta, *pieces)


def norm_back(grad_normed, unit_rows, inverse, gain_row):
    scaled = grad_normed * gain_row
    return inverse * (scaled - unit_rows * jnp.mean(scaled * unit_rows, axis=-1, keepdims=True))


def slots_kernel(cfg, meta, owners, *refs):
    n, sizes, slots_dev, split, panel = cfg
    count = len(sizes)
    lefts, rights = refs[:count], refs[count : 2 * count]
    low, high = refs[2 * count : 2 * count + n], refs[2 * count + n : 2 * count + 2 * n]
    stage, zero, named, sem, zero_sem = refs[2 * count + 2 * n :]
    pieces = list(zip(low, high, strict=True))
    me = meta[0]
    panels = sum(sizes)

    def clear(i, c):
        named[i] = 0
        return c

    lax.fori_loop(0, n * slots_dev, clear, 0)

    def mark(i, c):
        named[owners[i]] = 1
        return c

    lax.fori_loop(0, panels, mark, 0)
    zero[...] = jnp.zeros_like(zero)

    def blank(i, c):
        spot = lax.bitwise_xor(i // slots_dev, me)
        row = i % slots_dev
        for m, (a, b) in enumerate(pieces):
            for ref, base, size in ((a, 0, split), (b, split, slots_dev - split)):

                @pl.when((named[i] == 0) & (spot == m) & (row >= base) & (row < base + size))
                def _(ref=ref, base=base):
                    pltpu.make_async_copy(zero, ref.at[row - base], zero_sem).start()

        return c

    lax.fori_loop(0, n * slots_dev, blank, 0)
    first = 0
    for left, right, size in zip(lefts, rights, sizes, strict=True):
        product = mm(left[...], right[...], TN).astype(BF)
        stage[first : first + size] = product.reshape(size, panel, right.shape[1])
        panel_copies(
            owners, me, first, size, slots_dev, split, pieces,
            lambda i, first=first: stage.at[first + i], sem, True,
        )
        first += size
    pltpu.make_async_copy(stage, stage, sem).wait()

    def finish(i, c):
        @pl.when(named[i] == 0)
        def _():
            pltpu.make_async_copy(zero, zero, zero_sem).wait()

        return c

    lax.fori_loop(0, n * slots_dev, finish, 0)


def grads_to_slots(meta, owners, lefts, rights, n, slots_dev, split, panel):
    sizes = tuple(a.shape[1] // panel for a in lefts)
    tok, d = rights[0].shape
    count = len(lefts)
    shape = lambda s: jax.ShapeDtypeStruct((s, panel, d), BF)
    got = pl.pallas_call(
        functools.partial(slots_kernel, (n, sizes, slots_dev, split, panel)),
        in_specs=[SMEM, SMEM] + [VMEM] * (2 * count),
        out_specs=[ANY] * (2 * n),
        out_shape=[shape(split)] * n + [shape(slots_dev - split)] * n,
        scratch_shapes=[
            pltpu.VMEM((sum(sizes), panel, d), BF),
            pltpu.VMEM((panel, d), BF),
            pltpu.SMEM((n * slots_dev,), I32),
            pltpu.SemaphoreType.DMA,
            pltpu.SemaphoreType.DMA,
        ],
        compiler_params=params(),
        cost_estimate=cost(2 * tok * d * sum(sizes) * panel, 4 * sum(sizes) * panel * d + 4 * tok * d),
        name="grads_to_slots",
    )(meta, owners, *lefts, *rights)
    return got[:n], got[n:]


def soap_kernel(g1, g2, weight_ref, first_ref, second_ref, average_ref, stat_ref, basis_ref,
                weight_out, first_out, second_out, average_out, stat_out, turned_out):
    high = functools.partial(lax.dot_general, precision=HIGH, preferred_element_type=F32)
    grad = g1[0].astype(F32) + g2[0].astype(F32)
    basis = basis_ref[0]
    stat = BETA_TWO * stat_ref[0] + (1.0 - BETA_TWO) * high(grad, grad, NT)
    stat_out[0] = stat
    turned_out[0] = high(stat, basis, NN)
    rotated = high(basis, grad, TN)
    first = BETA_ONE * first_ref[0] + (1.0 - BETA_ONE) * rotated
    second = BETA_TWO * second_ref[0] + (1.0 - BETA_TWO) * rotated * rotated
    first_out[0] = first
    second_out[0] = second
    direction = (first / (1.0 - BETA_ONE**STEP)) / (
        jnp.sqrt(second / (1.0 - BETA_TWO**STEP)) + ADAM_EPSILON
    )
    weight = weight_ref[0]
    new_weight = weight - RATE * (high(basis, direction, NN) + WEIGHT_DECAY * weight)
    weight_out[0] = new_weight
    average_out[0] = AVERAGE_DECAY * average_ref[0] + (1.0 - AVERAGE_DECAY) * new_weight


def soap(g1, g2, weight, first, second, average, stat, basis):
    slots, panel, d = weight.shape
    big = pl.BlockSpec((1, panel, d), lambda i: (i, 0, 0))
    small = pl.BlockSpec((1, panel, panel), lambda i: (i, 0, 0))
    shape = jax.ShapeDtypeStruct
    return pl.pallas_call(
        soap_kernel,
        grid=(slots,),
        in_specs=[big] * 6 + [small] * 2,
        out_specs=[big] * 4 + [small] * 2,
        out_shape=[shape((slots, panel, d), F32)] * 4 + [shape((slots, panel, panel), F32)] * 2,
        compiler_params=params(),
        cost_estimate=cost(36 * slots * panel * panel * d, 40 * slots * panel * d),
        name="soap",
    )(g1, g2, weight, first, second, average, stat, basis)


def orthonormal_kernel(columns_ref, out_ref):
    size = columns_ref.shape[0]
    columns = columns_ref[...]
    index = lax.broadcasted_iota(I32, columns.shape, 0)
    out_ref[...] = columns

    def step(i, c):
        vector = out_ref[i]
        vector = vector * lax.rsqrt(jnp.sum(vector * vector, axis=0, keepdims=True))
        rest = out_ref[...]
        share = jnp.sum(rest * vector[None], axis=1, keepdims=True)
        rest = jnp.where(index > i, rest - share * vector[None], rest)
        out_ref[...] = rest
        out_ref[i] = vector
        return c

    lax.fori_loop(0, size, step, 0)


def orthonormal(matrix):
    columns = jnp.transpose(matrix, (2, 1, 0))
    found = pl.pallas_call(
        orthonormal_kernel,
        in_specs=[VMEM],
        out_specs=VMEM,
        out_shape=jax.ShapeDtypeStruct(columns.shape, F32),
        compiler_params=params(),
        name="orthonormal",
    )(columns)
    return jnp.transpose(found, (2, 1, 0))


def adam_gain(gradient, weight, first_state, second):
    new_first = BETA_ONE * first_state + (1.0 - BETA_ONE) * gradient
    new_second = BETA_TWO * second + (1.0 - BETA_TWO) * gradient * gradient
    direction = (
        new_first
        / (1.0 - BETA_ONE**STEP)
        / (jnp.sqrt(new_second / (1.0 - BETA_TWO**STEP)) + ADAM_EPSILON)
    )
    return (weight - GAIN_RATE * direction, new_first, new_second)


def back_kernel(cfg, meta, dq, dk, dv, wq, wk, wv, out):
    out[...] = (mm(dq[...], wq[...], NN) + mm(dk[...], wk[...], NN) + mm(dv[...], wv[...], NN)).astype(BF)


def back_in(meta, dq, dk, dv, wq, wk, wv, n):
    tok, qw = dq.shape
    d = wq.shape[1]
    tile = tok // n
    rows = pl.BlockSpec((tile, qw), lambda i, meta: (i, 0))
    whole = pl.BlockSpec((qw, d), lambda i, meta: (0, 0))
    return pl.pallas_call(
        functools.partial(back_kernel, n),
        grid_spec=pltpu.PrefetchScalarGridSpec(
            num_scalar_prefetch=1,
            grid=(n,),
            in_specs=[rows] * 3 + [whole] * 3,
            out_specs=pl.BlockSpec((tile, d), lambda i, meta: ((meta[0] - i + n) % n, 0)),
        ),
        out_shape=jax.ShapeDtypeStruct((tok, d), BF),
        compiler_params=params(),
        cost_estimate=cost(6 * tok * d * qw, 6 * qw * (tok + d) + 2 * tok * d),
        name="back_in",
    )(meta, dq, dk, dv, wq, wk, wv)


def shards(
    tokens,
    cotangent,
    lengths,
    retrieve,
    owners,
    masters,
    first_moment,
    second_moment,
    averaged,
    statistics,
    bases,
    gains,
    gain_first,
    gain_second,
):
    tok, d = tokens.shape
    n_seq, n_tp = lax.axis_size("seq"), lax.axis_size("tp")
    me, z = lax.axis_index("seq"), lax.axis_index("tp")
    qw, ff = H // n_tp * HD, FF // n_tp
    slots_dev, panel = masters.shape[1:3]
    split = (slots_dev + 1) // 2
    docs, picks = lengths.shape[0], retrieve.shape[1]
    recalled = lax.dynamic_index_in_dim(retrieve, me, 0, keepdims=False)
    meta = jnp.concatenate([me.astype(I32).reshape(1), lengths, recalled])
    place_meta = z.astype(I32).reshape(1)
    forth, back = routes(n_seq)
    block = tok // n_tp

    own = masters[0].astype(BF)
    low = gather_seq(own[:split], n_seq, forth)
    high = gather_seq(own[split:], n_seq, back)
    pieces = list(zip(low, high, strict=True))
    q, k, v, normed_one = project_in(meta, owners, tokens, gains, pieces, qw, slots_dev, split, panel)
    keys = gather_seq(k, n_seq, forth)
    values = gather_seq(v, n_seq, back)
    sizes = tuple(s // panel for s in (qw, qw, qw, qw, ff, ff, ff))
    wq, wk, wv, wo, wg, wu, wd = order_weights(meta, owners, pieces, sizes, slots_dev, split)
    wo_all = gather_tp(wo, n_tp)
    attended, wide, logs = attend(meta, q, keys, values, docs, picks)
    heads = gather_tp(attended, n_tp)
    mixed, normed_two, hidden, d_gate, d_up, back_two, feed = feed_forward(
        place_meta, tokens, cotangent, gains, wg, wu, wd, heads, wo_all
    )

    def turned(rows):
        return [rows[i * block : (i + 1) * block] for i in range(n_tp)]

    def mine(rows):
        return lax.dynamic_slice_in_dim(rows, z * block, block, 0)

    a, b = reduce_tp(turned(back_two), n_tp)
    d_normed_two = a.astype(F32) + b.astype(F32)
    mixed_here = mine(mixed)
    unit_two, inverse_two, _ = norm_rows(mixed_here, gains[1])
    grad_gain_two = jnp.sum(d_normed_two * unit_two, axis=0)
    d_mixed = mine(cotangent).astype(F32) + norm_back(d_normed_two, unit_two, inverse_two, gains[1])
    d_branch = place(place_meta, gather_tp(d_mixed.astype(BF), n_tp))
    d_attended = mm(d_branch, wo, NT).astype(BF)
    dq, dk_parts, dv_parts = attend_back(meta, q, d_attended, wide, logs, keys, values, docs, picks)

    a, b = reduce_tp(turned(feed), n_tp)
    out_here = (mixed_here + a.astype(F32) + b.astype(F32)).astype(BF)
    output = place(place_meta, gather_tp(out_here, n_tp))

    dk = plus(*reduce_seq(dk_parts, n_seq, forth))
    dv = plus(*reduce_seq(dv_parts, n_seq, back))

    low, high = grads_to_slots(
        meta,
        owners,
        [dq, dk, dv, attended, d_gate, d_up, hidden],
        [normed_one, normed_one, normed_one, d_branch, normed_two, normed_two, cotangent],
        n_seq, slots_dev, split, panel,
    )
    low_pair = reduce_seq(low, n_seq, forth)
    high_pair = reduce_seq(high, n_seq, back)

    back_one = back_in(place_meta, dq, dk, dv, wq, wk, wv, n_tp)
    a, b = reduce_tp(turned(back_one), n_tp)
    d_normed_one = a.astype(F32) + b.astype(F32)
    unit_one, inverse_one, _ = norm_rows(mine(tokens).astype(F32), gains[0])
    grad_gain_one = jnp.sum(d_normed_one * unit_one, axis=0)
    grad_here = d_mixed + norm_back(d_normed_one, unit_one, inverse_one, gains[0])
    grad_input = place(place_meta, gather_tp(grad_here.astype(BF), n_tp), F32)

    gain_total = sum_all(jnp.stack([grad_gain_one, grad_gain_two]), n_seq, n_tp)
    new_gains, new_gain_first, new_gain_second = adam_gain(gain_total, gains, gain_first, gain_second)

    g1 = jnp.concatenate([low_pair[0], high_pair[0]], axis=0)
    g2 = jnp.concatenate([low_pair[1], high_pair[1]], axis=0)
    new_weight, new_first, new_second, new_average, new_stat, turned_basis = soap(
        g1, g2, masters[0], first_moment[0], second_moment[0], averaged[0], statistics[0], bases[0]
    )
    new_basis = orthonormal(turned_basis)
    return (
        output,
        grad_input,
        new_weight[None],
        new_first[None],
        new_second[None],
        new_average[None],
        new_stat[None],
        new_basis[None],
        new_gains,
        new_gain_first,
        new_gain_second,
    )


def solution(mesh):
    by_token, by_slot = P("seq", None), P("tp", "seq", None, None)
    in_specs = (by_token, by_token, P(), P(), P()) + (by_slot,) * 6 + (P(),) * 3
    out_specs = (by_token, by_token) + (by_slot,) * 6 + (P(),) * 3
    return jax.shard_map(shards, mesh=mesh, in_specs=in_specs, out_specs=out_specs, check_vma=False)
```

```python
import functools

import jax
import jax.numpy as jnp
from jax import lax
from jax.experimental import pallas as pl
from jax.experimental.pallas import tpu as pltpu
from jax.sharding import PartitionSpec as P

H = 8
HD = 128
FF = 2816
MEMB = 128
STEP = 10

EPSILON = 1e-06
RATE = 0.02
GAIN_RATE = 0.5
BETA_ONE = 0.9
BETA_TWO = 0.95
ADAM_EPSILON = 1e-08
WEIGHT_DECAY = 0.01
AVERAGE_DECAY = 0.8
NEGATIVE = -1e30
START_TOP = -1e29
LOG2E = 1.4426950408889634

BF = jnp.bfloat16
F32 = jnp.float32
I32 = jnp.int32
HIGH = lax.Precision.HIGHEST
ANY = pl.BlockSpec(memory_space=pl.ANY)
SMEM = pl.BlockSpec(memory_space=pltpu.SMEM)
VMEM = pl.BlockSpec(memory_space=pltpu.VMEM)
VMEM_BYTES = 58 * 2**20

NT = (((1,), (1,)), ((), ()))
NN = (((1,), (0,)), ((), ()))
TN = (((0,), (0,)), ((), ()))


def mm(left, right, dims):
    return lax.dot_general(left, right, dims, preferred_element_type=F32)


QUICK = pl.CostEstimate(flops=1000, bytes_accessed=1000, transcendentals=0)


def params(**more):
    return pltpu.CompilerParams(vmem_limit_bytes=VMEM_BYTES, **more)


def pin(*values):
    return lax.optimization_barrier(values)


def routes(count):
    bits = []
    bit = 2
    while bit < count:
        bits.append(bit)
        bit *= 2
    return bits, bits[::-1]


def swap(value, count, bit):
    return lax.ppermute(value, "seq", [(i, i ^ bit) for i in range(count)])


def gather_seq(owns, count, beside=None):
    orders = routes(count)
    held = [{0: own} for own in owns]
    hops = len(orders[0])
    for stage in range(hops + 1):
        for i, pieces in enumerate(held):
            order = orders[i % 2]
            come = {}
            for m, piece in pieces.items():
                if m & 1 or bin(m).count("1") != stage:
                    continue
                for bit in order:
                    if all(other == bit or not m & other for other in order[order.index(bit) :]) and not m & bit:
                        come[m | bit] = swap(piece, count, bit)
                come[m | 1] = swap(piece, count, 1)
            pieces.update(come)
        if stage < hops:
            held, beside = pin(held, beside)
    return [[pieces[m] for m in range(count)] for pieces in held], beside


def plus(left, right):
    return (left.astype(F32) + right.astype(F32)).astype(left.dtype)


def reduce_bits(count, route):
    return [1, *routes(count)[route][::-1]]


def reduce_place(count, route, m):
    bits = reduce_bits(count, route)
    block = 0
    for bit in bits[1:]:
        block = 2 * block + bool(m & bit)
    return int(bool(m & bits[0])), block


def reduce_level(pair, count, route, at):
    keep, send = pair
    bits = reduce_bits(count, route)
    came = swap(send, count, bits[at])
    if at == len(bits) - 1:
        return keep, came
    half = keep.shape[0] // 2
    return plus(keep[:half], came[:half]), plus(keep[half:], came[half:])


def reduce_levels(pairs, count, at):
    return [reduce_level(pair, count, i % 2, at) for i, pair in enumerate(pairs)]


def direct_reduce(rows, count, sizes):
    parts = []
    for m in range(0, count, 2):
        at = reduce_place(count, 0, m)[1]
        part = rows[at * sizes : (at + 1) * sizes]
        parts.append(swap(part, count, m) if m else part)
    return parts


def direct_gather(rows, count):
    return jnp.concatenate([swap(rows, count, m) if m else rows for m in range(0, count, 2)], axis=0)


def core_gather(rows, count):
    return jnp.concatenate([rows, swap(rows, count, 1)], axis=0)


def gather_place(count, distance):
    return distance // 2 + (count // 2) * (distance % 2)


def ring(value, count, step):
    return lax.ppermute(value, "tp", [(i, (i + step) % count) for i in range(count)])


def trade_tp(parts, count):
    return [parts[0]] + [ring(parts[k], count, k) for k in range(1, count)]


def gather_tp(own, count):
    pieces = [own]
    for _ in range(count - 1):
        pieces.append(ring(pieces[-1], count, 1))
    return pieces


def reduce_tp(parts, count):
    total = parts[count - 1]
    for k in range(count - 2, -1, -1):
        came = ring(total, count, -1)
        if k == 0:
            return parts[0], came
        total = plus(parts[k], came)
    return None


def sum_steps(n_seq, n_tp):
    steps = []
    for axis, count in (("seq", n_seq), ("tp", n_tp)):
        bit = 1
        while bit < count:
            pairs = [(i, i ^ bit) for i in range(count)]
            steps.append(lambda v, axis=axis, pairs=pairs: v + lax.ppermute(v, axis, pairs))
            bit *= 2
    return steps


def panel_copies(owners_ref, me, first, amount, slots_dev, split, pieces, view, sem, back):
    def one(i, carry):
        slot = owners_ref[first + i]
        spot = lax.bitwise_xor(slot // slots_dev, me)
        row = slot % slots_dev
        for m, (low, high) in enumerate(pieces):
            for ref, base, size in ((low, 0, split), (high, split, slots_dev - split)):

                @pl.when((spot == m) & (row >= base) & (row < base + size))
                def _(ref=ref, base=base):
                    there = ref.at[row - base]
                    source, target = (view(i), there) if back else (there, view(i))
                    pltpu.make_async_copy(source, target, sem).start()

        return carry

    lax.fori_loop(0, amount, one, 0)


def norm_rows(rows, gain):
    inverse = lax.rsqrt(jnp.mean(rows * rows, axis=-1, keepdims=True) + EPSILON)
    unit = rows * inverse
    return unit, inverse, unit * gain


def project_kernel(cfg, meta, owners, x_ref, gain_ref, *refs):
    n, pq, pf, cap, slots_dev, split = cfg
    pieces = list(zip(refs[:n], refs[n : 2 * n], strict=True))
    outs = refs[2 * n : 2 * n + 3]
    normed_ref, inner, share, sems = refs[2 * n + 3 :]
    me, panel, d = meta[0], inner.shape[1], x_ref.shape[1]
    mine = jnp.clip(pf - me * cap, 0, cap)

    @pl.when(pl.program_id(0) == 0)
    def _():
        copies = functools.partial(panel_copies, owners, me)
        copies(0, 3 * pq, slots_dev, split, pieces, lambda i: inner.at[i], sems.at[0], False)
        copies(3 * pq, pq, slots_dev, split, pieces, lambda i: share.at[3 * cap + i], sems.at[1], False)
        for kind in range(3):
            for j in range(cap):

                @pl.when(j >= mine)
                def _(at=kind * cap + j):
                    share[at] = jnp.zeros(share.shape[1:], BF)

            copies(
                4 * pq + kind * pf + me * cap, mine, slots_dev, split, pieces,
                lambda i, kind=kind: share.at[kind * cap + i], sems.at[1], False,
            )

    _, _, normed = norm_rows(x_ref[...].astype(F32), gain_ref[0:1, :])
    normed = normed.astype(BF)
    normed_ref[...] = normed

    @pl.when(pl.program_id(0) == 0)
    def _():
        pltpu.make_async_copy(inner, inner, sems.at[0]).wait()

    for at in range(3):
        w = inner[at * pq : (at + 1) * pq].reshape(pq * panel, d)
        outs[at][...] = mm(normed, w, NT).astype(BF)

    @pl.when(pl.program_id(0) == pl.num_programs(0) - 1)
    def _():
        def finish(i, c):
            pltpu.make_async_copy(share.at[0], share.at[0], sems.at[1]).wait()
            return c

        lax.fori_loop(0, 3 * mine + pq, finish, 0)


def project_in(meta, owners, x, gains, pieces, pq, pf, cap, slots_dev, split):
    n = len(pieces)
    tok, d = x.shape
    panel = pieces[0][0].shape[1]
    qw = pq * panel
    tile = 256
    out = lambda w: pl.BlockSpec((tile, w), lambda i: (i, 0))
    whole = lambda count: pl.BlockSpec((count, panel, d), lambda i: (0, 0, 0))
    shape = lambda *dims: jax.ShapeDtypeStruct(dims, BF)
    q, k, v, normed, inner, share = pl.pallas_call(
        functools.partial(project_kernel, (n, pq, pf, cap, slots_dev, split)),
        grid=(tok // tile,),
        in_specs=[SMEM, SMEM, out(d), pl.BlockSpec(gains.shape, lambda i: (0, 0))] + [ANY] * (2 * n),
        out_specs=[out(qw)] * 3 + [out(d), whole(3 * pq), whole(3 * cap + pq)],
        out_shape=[shape(tok, qw)] * 3 + [shape(tok, d), shape(3 * pq, panel, d), shape(3 * cap + pq, panel, d)],
        scratch_shapes=[pltpu.SemaphoreType.DMA((2,))],
        compiler_params=params(),
        cost_estimate=QUICK,
        name="project",
    )(meta, owners, x, gains, *[p[0] for p in pieces], *[p[1] for p in pieces])
    return q, k, v, normed, inner.reshape(3, qw, d), share.reshape(-1, d)


def doc_start(meta, positions, docs):
    start = jnp.int32(0)
    found = jnp.zeros_like(positions)
    for at in range(docs):
        found = jnp.where(positions >= start, start, found)
        start = start + meta[2 + at]
    return found


def load_pieces(me, pieces, buffer, sem, tok):
    for m, piece in enumerate(pieces):
        owner = lax.bitwise_xor(me, m)
        at = pl.multiple_of(owner * tok, tok)
        pltpu.make_async_copy(piece, buffer.at[pl.ds(at, tok)], sem).start()


def member_table(meta, table, docs, picks, blocks):
    def clear(i, c):
        table[i] = 0
        return c

    lax.fori_loop(0, blocks, clear, 0)
    for e in range(picks):
        table[meta[2 + docs + e]] = 1


def memory_list(meta, blocks_ref, docs, picks, limit):
    count = jnp.int32(0)
    for e in range(picks):
        block = meta[2 + docs + e]
        fresh = (block + 1) * MEMB <= limit
        for other in range(e):
            fresh = fresh & (meta[2 + docs + other] != block)

        @pl.when(fresh)
        def _(count=count, block=block):
            blocks_ref[count] = block

        count = count + fresh.astype(I32)
    return count


def hide(scores, at, table, starts, queries, fill):
    rows = scores.shape[0]
    row = lax.broadcasted_iota(I32, (MEMB, scores.shape[1]), 0)
    kept = []
    for b in range(rows // MEMB):
        base = at + b * MEMB
        lowest = starts * (1 - table[base // MEMB]) - base
        seen = (row >= lowest) & (row <= queries - base)
        kept.append(jnp.where(seen, scores[b * MEMB : (b + 1) * MEMB], fill))
    return jnp.concatenate(kept, axis=0)


def attend_kernel(cfg, meta, q_ref, *refs):
    n, docs, picks, qt, kt, block = cfg
    keys, values = refs[:n], refs[n : 2 * n]
    out_ref, turn_ref, wide_ref, log_ref, kbuf, vbuf, acc, table, blocks, sems = refs[2 * n :]
    tok, width = q_ref.shape
    me = meta[0]
    factor = HD**-0.5 * LOG2E
    load_pieces(me, keys, kbuf, sems.at[0], tok)
    load_pieces(me, values, vbuf, sems.at[1], tok)
    member_table(meta, table, docs, picks, kbuf.shape[0] // MEMB)
    pltpu.make_async_copy(kbuf, kbuf, sems.at[0]).wait()
    pltpu.make_async_copy(vbuf, vbuf, sems.at[1]).wait()
    for head in range(width // HD):
        cols = slice(head * HD, (head + 1) * HD)

        def query_tile(t, carry, head=head, cols=cols):
            base = pl.multiple_of(t * qt, qt)
            first = me * tok + base
            queries = first + lax.broadcasted_iota(I32, (1, qt), 1)
            starts = doc_start(meta, queries, docs)
            low_tile = doc_start(meta, first, docs) // kt
            high_tile = (first + qt - 1) // kt
            q = q_ref[pl.ds(base, qt), cols]
            acc[...] = jnp.zeros_like(acc)

            def visit(at, rows, state, masked):
                top, total = state
                scores = mm(kbuf[pl.ds(at, rows), cols], q, NT)
                if masked:
                    scores = hide(scores, at, table, starts, queries, NEGATIVE)
                new_top = jnp.maximum(top, jnp.max(scores, axis=0, keepdims=True))
                fade = jnp.exp2((top - new_top) * factor)
                probs = jnp.exp2((scores - new_top) * factor)
                total = total * fade + jnp.sum(probs, axis=0, keepdims=True)
                acc[...] = acc[...] * fade + mm(vbuf[pl.ds(at, rows), cols], probs.astype(BF), TN)
                return new_top, total

            def dense(i, state):
                return visit(pl.multiple_of(i * kt, kt), kt, state, True)

            def memory(i, state):
                return visit(pl.multiple_of(blocks[i] * MEMB, MEMB), MEMB, state, False)

            count = memory_list(meta, blocks, docs, picks, low_tile * kt)
            state = (jnp.full((1, qt), START_TOP, F32), jnp.zeros((1, qt), F32))
            state = lax.fori_loop(low_tile, high_tile + 1, dense, state)
            top, total = lax.fori_loop(0, count, memory, state)
            rows = jnp.transpose(acc[...] * (1.0 / total))
            wide_ref[pl.ds(base, qt), cols] = rows
            rows = rows.astype(BF)
            out_ref[pl.ds(base, qt), cols] = rows
            spans = tok // block
            for part in range(qt // block):
                spot = lax.rem(base // block + part - meta[1] + spans, spans)
                spot = pl.multiple_of(spot * block, block)
                turn_ref[pl.ds(spot, block), cols] = rows[part * block : (part + 1) * block]
            log_ref[head : head + 1, pl.ds(base, qt)] = top * factor + jnp.log2(total)
            return carry

        lax.fori_loop(0, tok // qt, query_tile, 0)


def attend(meta, q, keys, values, docs, picks, block):
    n = len(keys)
    tok, width = q.shape
    qt, kt = 512, 512
    return pl.pallas_call(
        functools.partial(attend_kernel, (n, docs, picks, qt, kt, block)),
        in_specs=[SMEM, VMEM] + [ANY] * (2 * n),
        out_specs=[VMEM] * 4,
        out_shape=[
            jax.ShapeDtypeStruct((tok, width), BF),
            jax.ShapeDtypeStruct((tok, width), BF),
            jax.ShapeDtypeStruct((tok, width), F32),
            jax.ShapeDtypeStruct((width // HD, tok), F32),
        ],
        scratch_shapes=[
            pltpu.VMEM((n * tok, width), BF),
            pltpu.VMEM((n * tok, width), BF),
            pltpu.VMEM((HD, qt), F32),
            pltpu.SMEM((n * tok // MEMB,), I32),
            pltpu.SMEM((picks,), I32),
            pltpu.SemaphoreType.DMA((2,)),
        ],
        compiler_params=params(),
        cost_estimate=QUICK,
        name="attend",
    )(meta, q, *keys, *values)


def attend_back_kernel(cfg, meta, q_ref, wide_ref, log_ref, *refs):
    n, docs, picks, qt, kt, spans = cfg
    parts, refs = refs[:spans], refs[spans:]
    keys, values = refs[:n], refs[n : 2 * n]
    dq_ref = refs[2 * n]
    outs = (refs[2 * n + 1 : 2 * n + 3], refs[2 * n + 3 : 2 * n + 5])
    kbuf, vbuf, dk_acc, dv_acc, g_ref, acc, stage, table, blocks, sems = refs[2 * n + 5 :]
    tok, width = q_ref.shape
    me = meta[0]
    block = tok // spans
    scale = HD**-0.5
    factor = scale * LOG2E
    load_pieces(me, keys, kbuf, sems.at[0], tok)
    load_pieces(me, values, vbuf, sems.at[1], tok)
    member_table(meta, table, docs, picks, kbuf.shape[0] // MEMB)

    def clear(i, c):
        at = pl.ds(pl.multiple_of(i * 256, 256), 256)
        dk_acc[at, :] = jnp.zeros((256, width), F32)
        dv_acc[at, :] = jnp.zeros((256, width), F32)
        return c

    lax.fori_loop(0, kbuf.shape[0] // 256, clear, 0)
    for k, part in enumerate(parts):
        spot = pl.multiple_of(lax.rem(meta[1] - k + spans, spans) * block, block)
        g_ref[pl.ds(spot, block), :] = part[...]
    pltpu.make_async_copy(kbuf, kbuf, sems.at[0]).wait()
    pltpu.make_async_copy(vbuf, vbuf, sems.at[1]).wait()
    for head in range(width // HD):
        cols = slice(head * HD, (head + 1) * HD)

        def query_tile(t, carry, head=head, cols=cols):
            base = pl.multiple_of(t * qt, qt)
            first = me * tok + base
            queries = first + lax.broadcasted_iota(I32, (1, qt), 1)
            starts = doc_start(meta, queries, docs)
            low_tile = doc_start(meta, first, docs) // kt
            high_tile = (first + qt - 1) // kt
            q = q_ref[pl.ds(base, qt), cols]
            grad = g_ref[pl.ds(base, qt), cols]
            logs = log_ref[head : head + 1, pl.ds(base, qt)]
            product = grad.astype(F32) * wide_ref[pl.ds(base, qt), cols]
            delta = jnp.sum(jnp.transpose(product), axis=0, keepdims=True)
            acc[...] = jnp.zeros_like(acc)

            def visit(at, rows, masked):
                here = pl.ds(at, rows)
                k = kbuf[here, cols]
                probs = jnp.exp2(mm(k, q, NT) * factor - logs)
                if masked:
                    probs = hide(probs, at, table, starts, queries, 0.0)
                slopes = probs * (mm(vbuf[here, cols], grad, NT) - delta)
                slopes = slopes.astype(BF)
                dv_acc[here, cols] += mm(probs.astype(BF), grad, NN)
                dk_acc[here, cols] += mm(slopes, q, NN)
                acc[...] += mm(k, slopes, TN)

            def dense(i, c):
                visit(pl.multiple_of(i * kt, kt), kt, True)
                return c

            def memory(i, c):
                visit(pl.multiple_of(blocks[i] * MEMB, MEMB), MEMB, False)
                return c

            count = memory_list(meta, blocks, docs, picks, low_tile * kt)
            lax.fori_loop(low_tile, high_tile + 1, dense, 0)
            lax.fori_loop(0, count, memory, 0)
            dq_ref[pl.ds(base, qt), cols] = (jnp.transpose(acc[...]) * scale).astype(BF)
            return carry

        lax.fori_loop(0, tok // qt, query_tile, 0)

    def put(which, m):
        side, at = reduce_place(n, which, m)
        out = outs[which][side].at[at * tok : (at + 1) * tok]
        return pltpu.make_async_copy(stage.at[which], out, sems.at[2 + which])

    for m in range(n):
        at = pl.ds(pl.multiple_of(lax.bitwise_xor(me, m) * tok, tok), tok)
        for which in range(2):
            if m:
                put(which, m - 1).wait()
            rows = dk_acc[at, :] * scale if which == 0 else dv_acc[at, :]
            stage[which] = rows.astype(BF)
            put(which, m).start()
    for which in range(2):
        put(which, n - 1).wait()


def attend_back(meta, q, grads, wide, logs, keys, values, docs, picks):
    n = len(keys)
    tok, width = q.shape
    qt, kt = 512, 512
    got = pl.pallas_call(
        functools.partial(attend_back_kernel, (n, docs, picks, qt, kt, len(grads))),
        in_specs=[SMEM] + [VMEM] * (3 + len(grads)) + [ANY] * (2 * n),
        out_specs=[VMEM] + [ANY] * 4,
        out_shape=[jax.ShapeDtypeStruct((tok, width), BF)]
        + [jax.ShapeDtypeStruct((n * tok // 2, width), BF)] * 4,
        scratch_shapes=[
            pltpu.VMEM((n * tok, width), BF),
            pltpu.VMEM((n * tok, width), BF),
            pltpu.VMEM((n * tok, width), F32),
            pltpu.VMEM((n * tok, width), F32),
            pltpu.VMEM((tok, width), BF),
            pltpu.VMEM((HD, qt), F32),
            pltpu.VMEM((2, tok, width), BF),
            pltpu.SMEM((n * tok // MEMB,), I32),
            pltpu.SMEM((picks,), I32),
            pltpu.SemaphoreType.DMA((4,)),
        ],
        compiler_params=params(),
        cost_estimate=QUICK,
        name="attend_back",
    )(meta, q, wide, logs, *grads, *keys, *values)
    return got[0], got[1:3], got[3:5]


def mix_kernel(first, meta, x_ref, gain_ref, wo_ref, *refs):
    heads, (mixed_ref, left_ref, right_ref) = refs[:-3], refs[-3:]
    spans, qw = len(heads), heads[0].shape[1]
    mixed = x_ref[...].astype(F32)
    for k, head in enumerate(heads):
        mixed = mixed + mm(head[...], wo_ref[lax.rem(meta[1] - k + spans, spans), first:], NN)
    mixed_ref[...] = mixed
    _, _, normed = norm_rows(mixed, gain_ref[1:2, :])
    normed = normed.astype(BF)
    half = normed.shape[1] // 2
    left_ref[...] = normed[:, :half]
    right_ref[...] = normed[:, half:]


def mix(meta, x, gains, weights, heads):
    block, d = heads[0].shape[0], x.shape[1]
    whole = lambda a: pl.BlockSpec(a.shape, lambda i, meta: (0, 0))
    shape = lambda w, t: jax.ShapeDtypeStruct((block, w), t)
    outs = [shape(d, F32), shape(d // 2, BF), shape(d // 2, BF)]
    return pl.pallas_call(
        functools.partial(mix_kernel, weights.shape[1] - heads[0].shape[1]),
        grid_spec=pltpu.PrefetchScalarGridSpec(
            num_scalar_prefetch=1,
            grid=(1,),
            in_specs=[pl.BlockSpec((block, d), lambda i, meta: (meta[1], 0)), whole(gains), VMEM]
            + [whole(h) for h in heads],
            out_specs=[whole(o) for o in outs],
        ),
        out_shape=outs,
        compiler_params=params(),
        cost_estimate=QUICK,
        name="mix",
    )(meta, x, gains, weights, *heads)


def feed_kernel(cfg, meta, w_ref, g_ref, *refs):
    n, spans, fs = cfg
    pieces = refs[: 2 * n]
    normed_ref, hidden_ref, dgate_ref, dup_ref = refs[2 * n : 2 * n + 4]
    backs = (refs[2 * n + 4 : 2 * n + 6], refs[2 * n + 6 : 2 * n + 8])
    feeds = refs[2 * n + 8 : 2 * n + 10]
    rows, stage, feed, wg, wu, wd, sem, out_sem = refs[2 * n + 10 :]
    at = pl.program_id(0)
    block, half = g_ref.shape[0], g_ref.shape[1] // 2

    @pl.when(at == 0)
    def _():
        for m in range(n):
            pltpu.make_async_copy(pieces[m], rows.at[m, :, :half], sem).start()
            pltpu.make_async_copy(pieces[n + m], rows.at[m, :, half:], sem).start()
        for t in range(spans):
            for kind, w in enumerate((wg, wu, wd)):
                w[t * fs : (t + 1) * fs] = w_ref[t, kind * fs : (kind + 1) * fs]
        pltpu.make_async_copy(rows, rows, sem).wait()

    normed = rows[at]
    normed_ref[...] = normed
    gate = mm(normed, wg[...], NT)
    up = mm(normed, wu[...], NT)
    sigma = jax.nn.sigmoid(gate)
    silu = gate * sigma
    hidden = (silu * up).astype(BF)
    hidden_ref[...] = hidden
    d_hidden = mm(g_ref[...], wd[...], NT).astype(BF).astype(F32)
    d_gate = (d_hidden * up * (sigma * (1.0 + gate * (1.0 - sigma)))).astype(BF)
    d_up = (d_hidden * silu).astype(BF)
    dgate_ref[...] = d_gate
    dup_ref[...] = d_up
    stage[at] = (mm(d_gate, wg[...], NN) + mm(d_up, wu[...], NN)).astype(BF)
    feed[at] = mm(hidden, wd[...], NN).astype(BF)
    for m in range(n):

        @pl.when(at == m)
        def _(m=m):
            for route, cols in enumerate((slice(0, half), slice(half, 2 * half))):
                side, spot = reduce_place(n, route, m)
                there = backs[route][side].at[spot * block : (spot + 1) * block]
                pltpu.make_async_copy(stage.at[m, :, cols], there, out_sem).start()
            side, spot = reduce_place(n, 0, m)
            there = feeds[side].at[spot * block : (spot + 1) * block]
            pltpu.make_async_copy(feed.at[m], there, out_sem).start()

    @pl.when(at == n - 1)
    def _():
        pltpu.make_async_copy(stage, stage, out_sem).wait()
        pltpu.make_async_copy(feed, feed, out_sem).wait()


def feed_forward(meta, weights, grads, pieces, fs):
    n = len(pieces) // 2
    rows, d = grads.shape
    block = rows // n
    spans = weights.shape[0]
    units = spans * fs
    turned = lambda w: pl.BlockSpec((block, w), lambda m, meta: (lax.bitwise_xor(meta[0], m), 0))
    shape = lambda w: jax.ShapeDtypeStruct((rows, w), BF)
    got = pl.pallas_call(
        functools.partial(feed_kernel, (n, spans, fs)),
        grid_spec=pltpu.PrefetchScalarGridSpec(
            num_scalar_prefetch=1,
            grid=(n,),
            in_specs=[VMEM, turned(d)] + [ANY] * (2 * n),
            out_specs=[turned(d), turned(units), turned(units), turned(units)] + [ANY] * 6,
            scratch_shapes=[
                pltpu.VMEM((n, block, d), BF),
                pltpu.VMEM((n, block, d), BF),
                pltpu.VMEM((n, block, d), BF),
                pltpu.VMEM((units, d), BF),
                pltpu.VMEM((units, d), BF),
                pltpu.VMEM((units, d), BF),
                pltpu.SemaphoreType.DMA,
                pltpu.SemaphoreType.DMA,
            ],
        ),
        out_shape=[shape(d), shape(units), shape(units), shape(units)]
        + [jax.ShapeDtypeStruct((rows // 2, d // 2), BF)] * 4
        + [jax.ShapeDtypeStruct((rows // 2, d), BF)] * 2,
        compiler_params=params(),
        cost_estimate=QUICK,
        name="feed_forward",
    )(meta, weights, grads, *pieces)
    return got[:4], (got[4:6], got[6:8]), got[8:]


def branch_kernel(cfg, meta, left_a, left_b, right_a, right_b, mixed_ref, g_ref, gain_ref, wo_ref, *refs):
    first, n, spans = cfg
    heads, (mixed_out, gain_out), parts = refs[:spans], refs[spans : spans + 2], refs[spans + 2 : 2 * spans + 2]
    sides, (outer, sem) = refs[2 * spans + 2 : 2 * spans + 4], refs[2 * spans + 4 :]
    qw, out_rows = parts[0].shape[1], outer.shape[1] // n
    total = lambda a, b: a[...].astype(F32) + b[...].astype(F32)
    grad = jnp.concatenate([total(left_a, left_b), total(right_a, right_b)], axis=1)
    gain = gain_ref[1:2, :]
    unit, inverse, _ = norm_rows(mixed_ref[...], gain)
    gain_out[...] = jnp.sum(grad * unit, axis=0, keepdims=True)
    d_mixed = g_ref[...].astype(F32) + norm_back(grad, unit, inverse, gain)
    mixed_out[...] = d_mixed
    branch = d_mixed.astype(BF)
    for k, part in enumerate(parts):
        part[...] = mm(branch, wo_ref[lax.rem(meta[1] + k, spans), first:], NT).astype(BF)
    for k in range(spans):
        if outer.shape[1] > qw:
            outer[k, qw:] = jnp.zeros((outer.shape[1] - qw, outer.shape[2]), BF)
        outer[k, :qw] = mm(heads[(spans - k) % spans][...], branch, TN).astype(BF)
        spread(meta, outer.at[k], sides, n, 0, out_rows, sem, k * out_rows, spans * out_rows)
    pltpu.make_async_copy(outer, outer, sem).wait()


def branch_back(meta, pairs, mixed, grads, gains, weights, heads, n, first):
    block, d = mixed.shape
    spans, qw = weights.shape[0], weights.shape[1] - first
    out_rows = share_rows(qw, n)
    whole = lambda a: pl.BlockSpec(a.shape, lambda i, meta: (0, 0))
    terms = [*pairs[0], *pairs[1]]
    shape = jax.ShapeDtypeStruct
    outs = [shape((block, d), F32), shape((1, d), F32)] + [shape((block, qw), BF)] * spans
    got = pl.pallas_call(
        functools.partial(branch_kernel, (first, n, spans)),
        grid_spec=pltpu.PrefetchScalarGridSpec(
            num_scalar_prefetch=1,
            grid=(1,),
            in_specs=[whole(t) for t in terms]
            + [whole(mixed), pl.BlockSpec((block, d), lambda i, meta: (meta[1], 0)), whole(gains), VMEM]
            + [whole(h) for h in heads],
            out_specs=[whole(o) for o in outs] + [ANY] * 2,
            scratch_shapes=[pltpu.VMEM((spans, n * out_rows, d), BF), pltpu.SemaphoreType.DMA],
        ),
        out_shape=outs + [shape((n // 2 * spans * out_rows, d), BF)] * 2,
        compiler_params=params(),
        cost_estimate=QUICK,
        name="branch_back",
    )(meta, *terms, mixed, grads, gains, weights, *heads)
    return got[0], got[1], got[2 : 2 + spans], got[2 + spans :]


def place_kernel(n, meta, *refs):
    pieces, out = refs[:n], refs[n]
    rows = out.shape[0] // n
    for k, piece in enumerate(pieces):
        block = lax.rem(meta[1] - k + n, n)
        out[pl.ds(pl.multiple_of(block * rows, rows), rows), :] = piece[:rows, :].astype(out.dtype)


def place(meta, pieces, rows, kind=BF):
    n, d = len(pieces), pieces[0].shape[1]
    return pl.pallas_call(
        functools.partial(place_kernel, n),
        in_specs=[SMEM] + [VMEM] * n,
        out_specs=VMEM,
        out_shape=jax.ShapeDtypeStruct((n * rows, d), kind),
        compiler_params=params(),
        cost_estimate=QUICK,
        name="place",
    )(meta, *pieces)


def norm_back(grad_normed, unit_rows, inverse, gain_row):
    scaled = grad_normed * gain_row
    return inverse * (scaled - unit_rows * jnp.mean(scaled * unit_rows, axis=-1, keepdims=True))


def feed_grads_kernel(cfg, meta, d_gate, d_up, hidden, normed, grads, out):
    spans, fs = cfg
    for kind, (left, right) in enumerate(((d_gate, normed), (d_up, normed), (hidden, grads))):
        product = mm(left[...], right[...], TN).astype(BF)
        for t in range(spans):
            out[t, kind * fs : (kind + 1) * fs] = product[t * fs : (t + 1) * fs]


def feed_grads(meta, d_gate, d_up, hidden, normed, grads, fs):
    (rows, units), d = d_gate.shape, normed.shape[1]
    return pl.pallas_call(
        functools.partial(feed_grads_kernel, (units // fs, fs)),
        in_specs=[SMEM] + [VMEM] * 5,
        out_specs=VMEM,
        out_shape=jax.ShapeDtypeStruct((units // fs, 3 * fs, d), BF),
        compiler_params=params(),
        cost_estimate=QUICK,
        name="feed_grads",
    )(meta, d_gate, d_up, hidden, normed, grads)


def share_rows(rows, n):
    return -(-rows // (16 * n)) * 16


def spread(meta, stage, sides, n, route, rows, sem, base=0, total=None):
    for m in range(n):
        at = pl.ds(pl.multiple_of(lax.bitwise_xor(meta[0], m) * rows, rows), rows)
        side, spot = reduce_place(n, route, m)
        first = spot * (total or rows) + base
        pltpu.make_async_copy(stage.at[at], sides[side].at[first : first + rows], sem).start()


def late_kernel(cfg, meta, dq, dk, dv, normed, *refs):
    n, qw = cfg
    sides, (stage, sem) = refs[:2], refs[2:]
    used = 3 * qw
    if stage.shape[0] > used:
        stage[used:] = jnp.zeros((stage.shape[0] - used, stage.shape[1]), BF)
    for at, left in enumerate((dq, dk, dv)):
        stage[at * qw : (at + 1) * qw] = mm(left[...], normed[...], TN).astype(BF)
    spread(meta, stage, sides, n, 0, stage.shape[0] // n, sem)
    pltpu.make_async_copy(stage, stage, sem).wait()


def late_grads(meta, dq, dk, dv, normed, n):
    (tok, qw), d = dq.shape, normed.shape[1]
    rows = share_rows(3 * qw, n)
    return pl.pallas_call(
        functools.partial(late_kernel, (n, qw)),
        in_specs=[SMEM] + [VMEM] * 4,
        out_specs=[ANY] * 2,
        out_shape=[jax.ShapeDtypeStruct((n * rows // 2, d), BF)] * 2,
        scratch_shapes=[pltpu.VMEM((n * rows, d), BF), pltpu.SemaphoreType.DMA],
        compiler_params=params(),
        cost_estimate=QUICK,
        name="late_grads",
    )(meta, dq, dk, dv, normed)


def soap_kernel(cfg, meta, held, early, late, weight_ref, first_ref, second_ref, average_ref, stat_ref, basis_ref,
                weight_out, first_out, second_out, average_out, stat_out, turned_out, grads, wide, sem):
    n, late_panels, out_panels, pf, cap, rows, out_rows, group = cfg
    slots, panel, width = weight_ref.shape
    me, step = meta[0], pl.program_id(0)
    inner_panels = late_panels - out_panels

    def fetch(slot, source, share, base):
        grain = min(share, panel)
        for part in range(panel // grain):
            row = source * panel + part * grain
            at = gather_place(n, lax.bitwise_xor(me, row // share)) * (rows + out_rows) + base + row % share
            there = grads.at[slot, part * grain : (part + 1) * grain]
            pltpu.make_async_copy(late.at[pl.ds(pl.multiple_of(at, grain), grain)], there, sem).start()

    @pl.when(step == 0)
    def _():
        for slot in range(slots):
            source = held[slot]

            @pl.when(source < 0)
            def _(slot=slot):
                grads[slot] = jnp.zeros((panel, grads.shape[2]), BF)

            @pl.when((source >= 0) & (source < inner_panels))
            def _(slot=slot, source=source):
                fetch(slot, source, rows, 0)

            @pl.when((source >= inner_panels) & (source < late_panels))
            def _(slot=slot, source=source):
                fetch(slot, source - inner_panels, out_rows, rows)

            @pl.when(source >= late_panels)
            def _(slot=slot, source=source):
                kind, unit = (source - late_panels) // pf, (source - late_panels) % pf
                spot = (unit // cap) * 3 * cap + kind * cap + unit % cap
                pltpu.make_async_copy(early.at[spot], grads.at[slot], sem).start()

        for slot in range(slots):

            @pl.when(held[slot] >= 0)
            def _(slot=slot):
                pltpu.make_async_copy(grads.at[slot], grads.at[slot], sem).wait()

    high = functools.partial(lax.dot_general, precision=HIGH, preferred_element_type=F32)
    cols = pl.ds(pl.multiple_of(step * width, width), width)

    def parts(value):
        top = value.astype(BF)
        return top, (value - top.astype(F32)).astype(BF)

    for low in range(0, slots, group):
        count = min(group, slots - low)
        size = count * panel
        slot_range = slice(low, low + count)
        diagonal = wide.at[low // group]

        @pl.when(step == 0)
        def _(low=low, count=count, diagonal=diagonal):
            diagonal[...] = jnp.zeros_like(diagonal)
            for j in range(count):
                at = slice(j * panel, (j + 1) * panel)
                diagonal[at, at] = basis_ref[low + j]
                stat_out[low + j] = BETA_TWO * stat_ref[low + j]

        grad = grads[slot_range, :, cols].reshape(size, width)
        square = mm(grad, grad, NT)
        for j in range(count):
            at = slice(j * panel, (j + 1) * panel)
            stat_out[low + j] += (1.0 - BETA_TWO) * square[at, at]
        top, rest = parts(diagonal[:size, :size])
        flat = lambda ref, slot_range=slot_range, size=size: ref[slot_range].reshape(size, width)
        rotated = mm(top, grad, TN) + mm(rest, grad, TN)
        first = BETA_ONE * flat(first_ref) + (1.0 - BETA_ONE) * rotated
        second = BETA_TWO * flat(second_ref) + (1.0 - BETA_TWO) * rotated * rotated
        direction = (first / (1.0 - BETA_ONE**STEP)) / (
            jnp.sqrt(second / (1.0 - BETA_TWO**STEP)) + ADAM_EPSILON
        )
        high_part, low_part = parts(direction)
        update = mm(top, high_part, NN) + (mm(top, low_part, NN) + mm(rest, high_part, NN))
        weight = flat(weight_ref)
        new_weight = weight - RATE * (update + WEIGHT_DECAY * weight)
        average = AVERAGE_DECAY * flat(average_ref) + (1.0 - AVERAGE_DECAY) * new_weight
        shape = (count, panel, width)
        first_out[slot_range] = first.reshape(shape)
        second_out[slot_range] = second.reshape(shape)
        weight_out[slot_range] = new_weight.reshape(shape)
        average_out[slot_range] = average.reshape(shape)

        @pl.when(step == pl.num_programs(0) - 1)
        def _(low=low, count=count):
            for j in range(count):
                turned_out[low + j] = high(stat_out[low + j], basis_ref[low + j], NN)


def soap(meta, held, early, late, n, weight, first, second, average, stat, basis, late_panels, out_panels, pf, cap, rows):
    slots, panel, d = weight.shape
    width, group = 256, 8
    out_rows = late.shape[0] // n - rows
    big = pl.BlockSpec((slots, panel, width), lambda i, meta, held: (0, 0, i))
    small = pl.BlockSpec((slots, panel, panel), lambda i, meta, held: (0, 0, 0))
    shape = jax.ShapeDtypeStruct
    return pl.pallas_call(
        functools.partial(soap_kernel, (n, late_panels, out_panels, pf, cap, rows, out_rows, group)),
        grid_spec=pltpu.PrefetchScalarGridSpec(
            num_scalar_prefetch=2,
            grid=(d // width,),
            in_specs=[ANY] * 2 + [big] * 4 + [small] * 2,
            out_specs=[big] * 4 + [small] * 2,
            scratch_shapes=[
                pltpu.VMEM((slots, panel, d), BF),
                pltpu.VMEM((-(-slots // group), group * panel, group * panel), F32),
                pltpu.SemaphoreType.DMA,
            ],
        ),
        out_shape=[shape((slots, panel, d), F32)] * 4 + [shape((slots, panel, panel), F32)] * 2,
        compiler_params=params(),
        cost_estimate=QUICK,
        name="soap",
    )(meta, held, early, late, weight, first, second, average, stat, basis)


def orthonormal_kernel(columns_ref, out_ref):
    size = columns_ref.shape[0]
    out_ref[...] = columns_ref[...]
    for i in range(size):
        vector = out_ref[i]
        vector = vector * lax.rsqrt(jnp.sum(vector * vector, axis=0, keepdims=True))
        out_ref[i] = vector
        if i < size - 1:
            rest = out_ref[i + 1 :]
            out_ref[i + 1 :] = rest - jnp.sum(rest * vector[None], axis=1, keepdims=True) * vector[None]


def orthonormal(matrix):
    columns = jnp.transpose(matrix, (2, 1, 0))
    found = pl.pallas_call(
        orthonormal_kernel,
        in_specs=[VMEM],
        out_specs=VMEM,
        out_shape=jax.ShapeDtypeStruct(columns.shape, F32),
        compiler_params=params(),
        name="orthonormal",
    )(columns)
    return jnp.transpose(found, (2, 1, 0))


def adam_gain(gradient, weight, first_state, second):
    new_first = BETA_ONE * first_state + (1.0 - BETA_ONE) * gradient
    new_second = BETA_TWO * second + (1.0 - BETA_TWO) * gradient * gradient
    direction = (
        new_first
        / (1.0 - BETA_ONE**STEP)
        / (jnp.sqrt(new_second / (1.0 - BETA_TWO**STEP)) + ADAM_EPSILON)
    )
    return (weight - GAIN_RATE * direction, new_first, new_second)


def back_kernel(meta, dq, dk, dv, wq, wk, wv, out):
    out[...] = (mm(dq[...], wq[...], NN) + mm(dk[...], wk[...], NN) + mm(dv[...], wv[...], NN)).astype(BF)


def back_in(meta, dq, dk, dv, wq, wk, wv, n, low, high):
    tok, (qw, d) = dq.shape[0], wq.shape
    tile = tok // n
    rows = pl.BlockSpec((tile, qw), lambda i, meta: ((meta[1] - i - low + n) % n, 0))
    whole = pl.BlockSpec((qw, d), lambda i, meta: (0, 0))
    return pl.pallas_call(
        back_kernel,
        grid_spec=pltpu.PrefetchScalarGridSpec(
            num_scalar_prefetch=1,
            grid=(high - low,),
            in_specs=[rows] * 3 + [whole] * 3,
            out_specs=pl.BlockSpec((tile, d), lambda i, meta: (i, 0)),
        ),
        out_shape=jax.ShapeDtypeStruct(((high - low) * tile, d), BF),
        compiler_params=params(),
        cost_estimate=QUICK,
        name="back_in",
    )(meta, dq, dk, dv, wq, wk, wv)


def shards(
    tokens,
    cotangent,
    lengths,
    retrieve,
    owners,
    masters,
    first_moment,
    second_moment,
    averaged,
    statistics,
    bases,
    gains,
    gain_first,
    gain_second,
):
    tok, d = tokens.shape
    n_seq, n_tp = lax.axis_size("seq"), lax.axis_size("tp")
    me, z = lax.axis_index("seq"), lax.axis_index("tp")
    qw, ff = H // n_tp * HD, FF // n_tp
    slots_dev, panel = masters.shape[1:3]
    split = (slots_dev + 1) // 2
    docs, picks = lengths.shape[0], retrieve.shape[1]
    recalled = lax.dynamic_index_in_dim(retrieve, me, 0, keepdims=False)
    meta = jnp.concatenate([jnp.stack([me, z]).astype(I32), lengths, recalled])
    block = tok // n_tp
    pq, pf = qw // panel, ff // panel
    cap = -(-pf // n_seq)
    fs = cap * panel
    slot_ids = me * slots_dev + jnp.arange(slots_dev, dtype=I32)
    panel_ids = jnp.arange(1, owners.shape[0] + 1, dtype=I32)
    held = jnp.sum(jnp.where(slot_ids[:, None] == owners[None, :], panel_ids[None, :], 0), axis=1) - 1

    def mine(rows):
        return lax.dynamic_slice_in_dim(rows, z * block, block, 0)

    def whole_tp(rows):
        return lax.all_gather(rows, "tp", axis=0, tiled=True)

    def whole_seq(rows):
        return lax.all_gather(rows, "seq", axis=0, tiled=True)

    own = masters[0].astype(BF)
    pieces, _ = gather_seq([own[:split], own[split:]], n_seq)
    pieces = list(zip(*pieces, strict=True))
    q, k, v, normed_one, inner, share = project_in(
        meta, owners, tokens, gains, pieces, pq, pf, cap, slots_dev, split
    )
    (keys, values), _ = gather_seq([k, v], n_seq)
    weights = whole_tp(share).reshape(n_tp, -1, d)
    own_grads, keys[n_seq - 2], values[n_seq - 2] = pin(mine(cotangent), keys[n_seq - 2], values[n_seq - 2])
    grads_all = whole_seq(own_grads)
    attended, turned_heads, wide, logs = attend(meta, q, keys, values, docs, picks, block)
    heads = trade_tp([turned_heads[i * block : (i + 1) * block] for i in range(n_tp)], n_tp)
    mixed, left, right = mix(meta, tokens, gains, weights, heads)
    (left, right), _ = gather_seq([left, right], n_seq)
    (normed_two, hidden, d_gate, d_up), pairs, feed = feed_forward(meta, weights, grads_all, left + right, fs)

    last = len(routes(n_seq)[0])
    inner_rows, out_rows = share_rows(3 * qw, n_seq), share_rows(qw, n_seq)
    feed_sums_in = (d_gate, d_up, hidden, normed_two, grads_all)
    for at in range(last + 1):
        pairs = reduce_levels(pairs, n_seq, at)
        if at == last - 1:
            pairs, feed, feed_sums = pin(pairs, (feed[0], swap(feed[1], n_seq, 1)), feed_sums)
            feed = plus(*feed)
        elif at == 0:
            pairs, feed, feed_sums_in = pin(pairs, feed, feed_sums_in)
            feed_sums = feed_grads(meta, *feed_sums_in, fs)
    d_mixed, grad_gain_two, d_heads, outer = branch_back(
        meta, pairs, mixed, cotangent, gains, weights, heads, n_seq, 3 * fs
    )
    d_heads = trade_tp(d_heads, n_tp)
    outer = plus(outer[0], swap(outer[1], n_seq, 1))

    size = n_tp * out_rows
    parts = {}
    for m in range(0, n_seq, 2):
        at = reduce_place(n_seq, 0, m)[1]
        parts[m] = jnp.concatenate([feed[at * block : (at + 1) * block], outer[at * size : (at + 1) * size]], axis=0)
    d_heads, parts, feed_sums = pin(d_heads, parts, feed_sums)
    parts = [swap(part, n_seq, m) if m else part for m, part in parts.items()]
    feed_sums = lax.psum_scatter(feed_sums.reshape(-1, d), "tp", scatter_dimension=0, tiled=True)
    dq, *pairs = attend_back(meta, q, d_heads, wide, logs, keys, values, docs, picks)
    parts, feed_sums, dq, pairs = pin(parts, feed_sums, dq, pairs)
    pairs = reduce_levels(pairs, n_seq, 0)
    total = sum(part.astype(F32) for part in parts)
    output = (mixed + total[:block]).astype(BF)
    outer = [total[block + k * out_rows : block + (k + 1) * out_rows].astype(BF) for k in range(n_tp)]
    outputs = [output]
    for at in range(last + 1):
        if at:
            pairs = reduce_levels(pairs, n_seq, at)
            while len(outputs) < n_tp and (at == last or len(outputs) < 1 + 2 * at):
                outputs.append(ring(outputs[-1], n_tp, 1))
        pairs, outputs, feed_sums, dq = pin(pairs, outputs, feed_sums, dq)
    dk, dv = [plus(*pair) for pair in pairs]
    early = whole_seq(feed_sums).reshape(-1, panel, d)

    inputs = (meta, dq, dk, dv, inner[0], inner[1], inner[2], n_tp)
    total = back_in(*inputs, n_tp - 1, n_tp)
    total, lefts = pin(total, (dq, dk, dv))
    back_rest = back_in(meta, *lefts, *inputs[4:], 0, n_tp - 1)
    late = late_grads(meta, *lefts, normed_one, n_seq)

    def advance(late, step):
        if step == 1:
            late = plus(late[0], swap(late[1], n_seq, 1))
        elif step == 2:
            parts = direct_reduce(late, n_seq, inner_rows)
            late = sum(part.astype(F32) for part in parts).astype(BF)
            late = jnp.concatenate([late, outer], axis=0)
        elif step == 3:
            late = direct_gather(late, n_seq)
        elif step == 4:
            late = core_gather(late, n_seq)
        return late

    steps = max(2 * (n_tp - 1), 6)
    gain_steps = sum_steps(n_seq, n_tp)
    gather = []
    for step in range(steps):
        if step < n_tp - 1:
            k = n_tp - 2 - step
            came = ring(total, n_tp, -1)
            late = advance(late, step)
            if step == 0:
                outer = trade_tp(outer, n_tp)
            came, late, back_rest, outer = pin(came, late, back_rest, outer)
            if step == 0:
                outer = sum(part.astype(F32) for part in outer).astype(BF)
            part = back_rest[k * block : (k + 1) * block]
            if k:
                total = plus(part, came)
                continue
            d_normed_one = part.astype(F32) + came.astype(F32)
            unit_one, inverse_one, _ = norm_rows(mine(tokens).astype(F32), gains[0])
            grad_gain_one = jnp.sum(d_normed_one * unit_one, axis=0)
            grad_here = d_mixed + norm_back(d_normed_one, unit_one, inverse_one, gains[0])
            gain_total = jnp.stack([grad_gain_one, grad_gain_two[0]])
            gather.append(grad_here.astype(BF))
            continue
        if len(gather) < n_tp:
            gather.append(ring(gather[-1], n_tp, 1))
        if gain_steps:
            gain_total = gain_steps.pop(0)(gain_total)
        late = advance(late, step)
        if step == steps - 2:
            new_weight, new_first, new_second, new_average, new_stat, turned_basis = soap(
                meta, held, early, late, n_seq, masters[0], first_moment[0], second_moment[0], averaged[0],
                statistics[0], bases[0], 4 * pq, pq, pf, cap, inner_rows,
            )
            gather[-1], turned_basis, gain_total = pin(gather[-1], turned_basis, gain_total)
        elif step == steps - 1:
            new_basis = orthonormal(turned_basis)
            gather, new_basis, gain_total = pin(gather, new_basis, gain_total)
        else:
            gather[-1], late, gain_total = pin(gather[-1], late, gain_total)
    for step in gain_steps:
        gain_total = step(gain_total)
    output = place(meta, outputs, block)
    grad_input = place(meta, gather, block, F32)
    new_gains, new_gain_first, new_gain_second = adam_gain(gain_total, gains, gain_first, gain_second)
    return (
        output,
        grad_input,
        new_weight[None],
        new_first[None],
        new_second[None],
        new_average[None],
        new_stat[None],
        new_basis[None],
        new_gains,
        new_gain_first,
        new_gain_second,
    )


def solution(mesh):
    by_token, by_slot = P("seq", None), P("tp", "seq", None, None)
    in_specs = (by_token, by_token, P(), P(), P()) + (by_slot,) * 6 + (P(),) * 3
    out_specs = (by_token, by_token) + (by_slot,) * 6 + (P(),) * 3
    return jax.shard_map(shards, mesh=mesh, in_specs=in_specs, out_specs=out_specs, check_vma=False)
```

```python
import functools

import jax
import jax.numpy as jnp
from jax import lax
from jax.experimental import pallas as pl
from jax.experimental.pallas import tpu as pltpu
from jax.sharding import PartitionSpec as P

H = 8
HD = 128
FF = 2816
MEMB = 128
STEP = 10

EPSILON = 1e-06
RATE = 0.02
GAIN_RATE = 0.5
BETA_ONE = 0.9
BETA_TWO = 0.95
ADAM_EPSILON = 1e-08
WEIGHT_DECAY = 0.01
AVERAGE_DECAY = 0.8
NEGATIVE = -1e30
START_TOP = -1e29
LOG2E = 1.4426950408889634

BF = jnp.bfloat16
F32 = jnp.float32
I32 = jnp.int32
HIGH = lax.Precision.HIGHEST
ANY = pl.BlockSpec(memory_space=pl.ANY)
SMEM = pl.BlockSpec(memory_space=pltpu.SMEM)
VMEM = pl.BlockSpec(memory_space=pltpu.VMEM)
VMEM_BYTES = 58 * 2**20

NT = (((1,), (1,)), ((), ()))
NN = (((1,), (0,)), ((), ()))
TN = (((0,), (0,)), ((), ()))


def mm(left, right, dims):
    return lax.dot_general(left, right, dims, preferred_element_type=F32)


QUICK = pl.CostEstimate(flops=1000, bytes_accessed=1000, transcendentals=0)


def params(**more):
    return pltpu.CompilerParams(vmem_limit_bytes=VMEM_BYTES, **more)


def pin(*values):
    return lax.optimization_barrier(values)


def routes(count):
    bits = []
    bit = 2
    while bit < count:
        bits.append(bit)
        bit *= 2
    return bits, bits[::-1]


def swap(value, count, bit):
    return lax.ppermute(value, "seq", [(i, i ^ bit) for i in range(count)])


def gather_seq(owns, count, beside=None):
    orders = routes(count)
    held = [{0: own} for own in owns]
    hops = len(orders[0])
    for stage in range(hops + 1):
        for i, pieces in enumerate(held):
            order = orders[i % 2]
            come = {}
            for m, piece in pieces.items():
                if m & 1 or bin(m).count("1") != stage:
                    continue
                for bit in order:
                    if all(other == bit or not m & other for other in order[order.index(bit) :]) and not m & bit:
                        come[m | bit] = swap(piece, count, bit)
                come[m | 1] = swap(piece, count, 1)
            pieces.update(come)
        if stage < hops:
            held, beside = pin(held, beside)
    return [[pieces[m] for m in range(count)] for pieces in held], beside


def plus(left, right):
    return (left.astype(F32) + right.astype(F32)).astype(left.dtype)


def reduce_bits(count, route):
    return [1, *routes(count)[route][::-1]]


def reduce_place(count, route, m):
    bits = reduce_bits(count, route)
    block = 0
    for bit in bits[1:]:
        block = 2 * block + bool(m & bit)
    return int(bool(m & bits[0])), block


def reduce_level(pair, count, route, at):
    keep, send = pair
    bits = reduce_bits(count, route)
    came = swap(send, count, bits[at])
    if at == len(bits) - 1:
        return keep, came
    half = keep.shape[0] // 2
    return plus(keep[:half], came[:half]), plus(keep[half:], came[half:])


def reduce_levels(pairs, count, at):
    return [reduce_level(pair, count, i % 2, at) for i, pair in enumerate(pairs)]


def direct_reduce(rows, count, sizes):
    parts = []
    for m in range(0, count, 2):
        at = reduce_place(count, 0, m)[1]
        part = rows[at * sizes : (at + 1) * sizes]
        parts.append(swap(part, count, m) if m else part)
    return parts


def direct_pieces(rows, count):
    return [swap(rows, count, m) if m else rows for m in range(0, count, 2)]


def direct_gather(rows, count):
    return jnp.concatenate(direct_pieces(rows, count), axis=0)


def core_gather(rows, count):
    return jnp.concatenate([rows, swap(rows, count, 1)], axis=0)


def gather_place(count, distance):
    return distance // 2 + (count // 2) * (distance % 2)


def ring(value, count, step):
    return lax.ppermute(value, "tp", [(i, (i + step) % count) for i in range(count)])


def trade_tp(parts, count):
    return [parts[0]] + [ring(parts[k], count, k) for k in range(1, count)]


def gather_tp(own, count):
    pieces = [own]
    for _ in range(count - 1):
        pieces.append(ring(pieces[-1], count, 1))
    return pieces


def reduce_tp(parts, count):
    total = parts[count - 1]
    for k in range(count - 2, -1, -1):
        came = ring(total, count, -1)
        if k == 0:
            return parts[0], came
        total = plus(parts[k], came)
    return None


def sum_steps(n_seq, n_tp):
    steps = []
    for axis, count in (("seq", n_seq), ("tp", n_tp)):
        bit = 1
        while bit < count:
            pairs = [(i, i ^ bit) for i in range(count)]
            steps.append(lambda v, axis=axis, pairs=pairs: v + lax.ppermute(v, axis, pairs))
            bit *= 2
    return steps


def panel_copies(owners_ref, me, first, amount, slots_dev, split, pieces, view, sem, back):
    def one(i, carry):
        slot = owners_ref[first + i]
        spot = lax.bitwise_xor(slot // slots_dev, me)
        row = slot % slots_dev
        for m, (low, high) in enumerate(pieces):
            for ref, base, size in ((low, 0, split), (high, split, slots_dev - split)):

                @pl.when((spot == m) & (row >= base) & (row < base + size))
                def _(ref=ref, base=base):
                    there = ref.at[row - base]
                    source, target = (view(i), there) if back else (there, view(i))
                    pltpu.make_async_copy(source, target, sem).start()

        return carry

    lax.fori_loop(0, amount, one, 0)


def norm_rows(rows, gain):
    inverse = lax.rsqrt(jnp.mean(rows * rows, axis=-1, keepdims=True) + EPSILON)
    unit = rows * inverse
    return unit, inverse, unit * gain


def project_kernel(cfg, meta, owners, x_ref, gain_ref, *refs):
    n, pq, pf, cap, slots_dev, split = cfg
    pieces = list(zip(refs[:n], refs[n : 2 * n], strict=True))
    outs = refs[2 * n : 2 * n + 3]
    normed_ref, inner, share, sems = refs[2 * n + 3 :]
    me, panel, d = meta[0], inner.shape[1], x_ref.shape[1]
    mine = jnp.clip(pf - me * cap, 0, cap)

    @pl.when(pl.program_id(0) == 0)
    def _():
        copies = functools.partial(panel_copies, owners, me)
        copies(0, 3 * pq, slots_dev, split, pieces, lambda i: inner.at[i], sems.at[0], False)
        copies(3 * pq, pq, slots_dev, split, pieces, lambda i: share.at[3 * cap + i], sems.at[1], False)
        for kind in range(3):
            for j in range(cap):

                @pl.when(j >= mine)
                def _(at=kind * cap + j):
                    share[at] = jnp.zeros(share.shape[1:], BF)

            copies(
                4 * pq + kind * pf + me * cap, mine, slots_dev, split, pieces,
                lambda i, kind=kind: share.at[kind * cap + i], sems.at[1], False,
            )

    _, _, normed = norm_rows(x_ref[...].astype(F32), gain_ref[0:1, :])
    normed = normed.astype(BF)
    normed_ref[...] = normed

    @pl.when(pl.program_id(0) == 0)
    def _():
        pltpu.make_async_copy(inner, inner, sems.at[0]).wait()

    for at in range(3):
        w = inner[at * pq : (at + 1) * pq].reshape(pq * panel, d)
        outs[at][...] = mm(normed, w, NT).astype(BF)

    @pl.when(pl.program_id(0) == pl.num_programs(0) - 1)
    def _():
        def finish(i, c):
            pltpu.make_async_copy(share.at[0], share.at[0], sems.at[1]).wait()
            return c

        lax.fori_loop(0, 3 * mine + pq, finish, 0)


def project_in(meta, owners, x, gains, pieces, pq, pf, cap, slots_dev, split):
    n = len(pieces)
    tok, d = x.shape
    panel = pieces[0][0].shape[1]
    qw = pq * panel
    tile = 256
    out = lambda w: pl.BlockSpec((tile, w), lambda i: (i, 0))
    whole = lambda count: pl.BlockSpec((count, panel, d), lambda i: (0, 0, 0))
    shape = lambda *dims: jax.ShapeDtypeStruct(dims, BF)
    q, k, v, normed, inner, share = pl.pallas_call(
        functools.partial(project_kernel, (n, pq, pf, cap, slots_dev, split)),
        grid=(tok // tile,),
        in_specs=[SMEM, SMEM, out(d), pl.BlockSpec(gains.shape, lambda i: (0, 0))] + [ANY] * (2 * n),
        out_specs=[out(qw)] * 3 + [out(d), whole(3 * pq), whole(3 * cap + pq)],
        out_shape=[shape(tok, qw)] * 3 + [shape(tok, d), shape(3 * pq, panel, d), shape(3 * cap + pq, panel, d)],
        scratch_shapes=[pltpu.SemaphoreType.DMA((2,))],
        compiler_params=params(),
        cost_estimate=QUICK,
        name="project",
    )(meta, owners, x, gains, *[p[0] for p in pieces], *[p[1] for p in pieces])
    return q, k, v, normed, inner.reshape(3, qw, d), share.reshape(-1, d)


def doc_start(meta, positions, docs):
    start = jnp.int32(0)
    found = jnp.zeros_like(positions)
    for at in range(docs):
        found = jnp.where(positions >= start, start, found)
        start = start + meta[2 + at]
    return found


def load_pieces(me, pieces, buffer, sem, tok):
    for m, piece in enumerate(pieces):
        owner = lax.bitwise_xor(me, m)
        at = pl.multiple_of(owner * tok, tok)
        pltpu.make_async_copy(piece, buffer.at[pl.ds(at, tok)], sem).start()


def member_table(meta, table, docs, picks, blocks):
    def clear(i, c):
        table[i] = 0
        return c

    lax.fori_loop(0, blocks, clear, 0)
    for e in range(picks):
        table[meta[2 + docs + e]] = 1


def memory_list(meta, blocks_ref, docs, picks, limit):
    count = jnp.int32(0)
    for e in range(picks):
        block = meta[2 + docs + e]
        fresh = (block + 1) * MEMB <= limit
        for other in range(e):
            fresh = fresh & (meta[2 + docs + other] != block)

        @pl.when(fresh)
        def _(count=count, block=block):
            blocks_ref[count] = block

        count = count + fresh.astype(I32)
    return count


def seen_rows(at, rows, table, starts, queries):
    row = lax.broadcasted_iota(I32, (MEMB, queries.shape[1]), 0)
    seen = []
    for b in range(rows // MEMB):
        base = at + b * MEMB
        lowest = starts * (1 - table[base // MEMB]) - base
        seen.append((row >= lowest) & (row <= queries - base))
    return seen


def hide(scores, seen, fill):
    kept = [jnp.where(mask, scores[b * MEMB : (b + 1) * MEMB], fill) for b, mask in enumerate(seen)]
    return jnp.concatenate(kept, axis=0)


def rows_of(buffer, spots, rows, cols):
    parts = [buffer[pl.ds(at, rows), cols] for at in spots]
    return parts[0] if len(parts) == 1 else jnp.concatenate(parts, axis=0)


def visit_keys(visit, state, meta, first, qt, kt, docs, picks, blocks):
    low = doc_start(meta, first, docs) // kt
    high = (first + qt - 1) // kt + 1
    clear = jnp.clip((doc_start(meta, first + qt - 1, docs) + kt - 1) // kt, low, high)
    full = jnp.clip(first // kt, clear, high)
    count = memory_list(meta, blocks, docs, picks, low * kt)

    def dense(masked):
        return lambda i, state: visit([pl.multiple_of(i * kt, kt)], kt, state, masked)

    def memory(together, base):
        def go(i, state):
            spots = [pl.multiple_of(blocks[base + i * together + j] * MEMB, MEMB) for j in range(together)]
            return visit(spots, MEMB, state, False)

        return go

    state = lax.fori_loop(low, clear, dense(True), state)
    state = lax.fori_loop(clear, full, dense(False), state)
    state = lax.fori_loop(full, high, dense(True), state)
    state = lax.fori_loop(0, count // 4, memory(4, 0), state)
    return lax.fori_loop(0, count % 4, memory(1, count // 4 * 4), state)


def attend_kernel(cfg, meta, q_ref, *refs):
    n, docs, picks, qt, kt, block = cfg
    keys, values = refs[:n], refs[n : 2 * n]
    turn_ref, wide_ref, log_ref, kbuf, vbuf, acc, table, blocks, sems = refs[2 * n :]
    tok, width = q_ref.shape
    me = meta[0]
    factor = HD**-0.5 * LOG2E
    load_pieces(me, keys, kbuf, sems.at[0], tok)
    load_pieces(me, values, vbuf, sems.at[1], tok)
    member_table(meta, table, docs, picks, kbuf.shape[0] // MEMB)
    pltpu.make_async_copy(kbuf, kbuf, sems.at[0]).wait()
    pltpu.make_async_copy(vbuf, vbuf, sems.at[1]).wait()
    heads = [slice(head * HD, (head + 1) * HD) for head in range(width // HD)]
    spans = tok // block

    def query_tile(t, carry):
        base = pl.multiple_of(t * qt, qt)
        first = me * tok + base
        queries = first + lax.broadcasted_iota(I32, (1, qt), 1)
        starts = doc_start(meta, queries, docs)
        acc[...] = jnp.zeros_like(acc)

        def visit(spots, rows, state, masked):
            seen = seen_rows(spots[0], rows, table, starts, queries) if masked else None
            result = []
            for head, cols in enumerate(heads):
                top, total = state[head]
                scores = mm(rows_of(kbuf, spots, rows, cols), q_ref[pl.ds(base, qt), cols], NT)
                if masked:
                    scores = hide(scores, seen, NEGATIVE)
                new_top = jnp.maximum(top, jnp.max(scores, axis=0, keepdims=True))
                fade = jnp.exp2((top - new_top) * factor)
                probs = jnp.exp2((scores - new_top) * factor)
                total = total * fade + jnp.sum(probs, axis=0, keepdims=True)
                product = mm(rows_of(vbuf, spots, rows, cols), probs.astype(BF), TN)
                acc[head] = acc[head] * fade + product
                result.append((new_top, total))
            return tuple(result)

        state = tuple((jnp.full((1, qt), START_TOP, F32), jnp.zeros((1, qt), F32)) for _ in heads)
        state = visit_keys(visit, state, meta, first, qt, kt, docs, picks, blocks)
        for head, cols in enumerate(heads):
            top, total = state[head]
            rows = jnp.transpose(acc[head] * (1.0 / total))
            wide_ref[pl.ds(base, qt), cols] = rows
            rows = rows.astype(BF)
            for part in range(max(qt // block, 1)):
                size = min(block, qt)
                spot = lax.rem(base // block + part - meta[1] + spans, spans) * block + lax.rem(base, block)
                spot = pl.multiple_of(spot, size)
                turn_ref[pl.ds(spot, size), cols] = rows[part * size : (part + 1) * size]
            log_ref[head : head + 1, pl.ds(base, qt)] = top * factor + jnp.log2(total)
        return carry

    lax.fori_loop(0, tok // qt, query_tile, 0)


def attend(meta, q, keys, values, docs, picks, block):
    n = len(keys)
    tok, width = q.shape
    qt, kt = 512, 1024
    return pl.pallas_call(
        functools.partial(attend_kernel, (n, docs, picks, qt, kt, block)),
        in_specs=[SMEM, VMEM] + [ANY] * (2 * n),
        out_specs=[VMEM] * 3,
        out_shape=[
            jax.ShapeDtypeStruct((tok, width), BF),
            jax.ShapeDtypeStruct((tok, width), F32),
            jax.ShapeDtypeStruct((width // HD, tok), F32),
        ],
        scratch_shapes=[
            pltpu.VMEM((n * tok, width), BF),
            pltpu.VMEM((n * tok, width), BF),
            pltpu.VMEM((width // HD, HD, qt), F32),
            pltpu.SMEM((n * tok // MEMB,), I32),
            pltpu.SMEM((picks,), I32),
            pltpu.SemaphoreType.DMA((2,)),
        ],
        compiler_params=params(),
        cost_estimate=QUICK,
        name="attend",
    )(meta, q, *keys, *values)


def attend_back_kernel(cfg, meta, q_ref, wide_ref, log_ref, *refs):
    n, docs, picks, qt, kt, spans = cfg
    parts, refs = refs[:spans], refs[spans:]
    keys, values = refs[:n], refs[n : 2 * n]
    dq_ref = refs[2 * n]
    outs = (refs[2 * n + 1 : 2 * n + 3], refs[2 * n + 3 : 2 * n + 5])
    kbuf, vbuf, dk_acc, dv_acc, g_ref, acc, stage, table, blocks, sems = refs[2 * n + 5 :]
    tok, width = q_ref.shape
    me = meta[0]
    block = tok // spans
    scale = HD**-0.5
    factor = scale * LOG2E
    load_pieces(me, keys, kbuf, sems.at[0], tok)
    load_pieces(me, values, vbuf, sems.at[1], tok)
    member_table(meta, table, docs, picks, kbuf.shape[0] // MEMB)

    def clear(i, c):
        at = pl.ds(pl.multiple_of(i * 256, 256), 256)
        dk_acc[at, :] = jnp.zeros((256, width), F32)
        dv_acc[at, :] = jnp.zeros((256, width), F32)
        return c

    lax.fori_loop(0, kbuf.shape[0] // 256, clear, 0)
    for k, part in enumerate(parts):
        spot = pl.multiple_of(lax.rem(meta[1] - k + spans, spans) * block, block)
        g_ref[pl.ds(spot, block), :] = part[...]
    pltpu.make_async_copy(kbuf, kbuf, sems.at[0]).wait()
    pltpu.make_async_copy(vbuf, vbuf, sems.at[1]).wait()
    heads = [slice(head * HD, (head + 1) * HD) for head in range(width // HD)]

    def query_tile(t, carry):
        base = pl.multiple_of(t * qt, qt)
        first = me * tok + base
        queries = first + lax.broadcasted_iota(I32, (1, qt), 1)
        starts = doc_start(meta, queries, docs)
        here = pl.ds(base, qt)
        deltas = []
        for cols in heads:
            product = g_ref[here, cols].astype(F32) * wide_ref[here, cols]
            deltas.append(jnp.sum(jnp.transpose(product), axis=0, keepdims=True))
        acc[...] = jnp.zeros_like(acc)

        def visit(spots, rows, state, masked):
            seen = seen_rows(spots[0], rows, table, starts, queries) if masked else None
            for head, cols in enumerate(heads):
                q, grad = q_ref[here, cols], g_ref[here, cols]
                k = rows_of(kbuf, spots, rows, cols)
                probs = jnp.exp2(mm(k, q, NT) * factor - log_ref[head : head + 1, here])
                if masked:
                    probs = hide(probs, seen, 0.0)
                slopes = probs * (mm(rows_of(vbuf, spots, rows, cols), grad, NT) - deltas[head])
                slopes = slopes.astype(BF)
                d_values = mm(probs.astype(BF), grad, NN)
                d_keys = mm(slopes, q, NN)
                for j, at in enumerate(spots):
                    part = slice(j * rows, (j + 1) * rows)
                    dv_acc[pl.ds(at, rows), cols] += d_values[part]
                    dk_acc[pl.ds(at, rows), cols] += d_keys[part]
                acc[head] += mm(k, slopes, TN)
            return state

        visit_keys(visit, jnp.int32(0), meta, first, qt, kt, docs, picks, blocks)
        for head, cols in enumerate(heads):
            dq_ref[here, cols] = (jnp.transpose(acc[head]) * scale).astype(BF)
        return carry

    lax.fori_loop(0, tok // qt, query_tile, 0)

    def put(which, m):
        side, at = reduce_place(n, which, m)
        out = outs[which][side].at[at * tok : (at + 1) * tok]
        return pltpu.make_async_copy(stage.at[which], out, sems.at[2 + which])

    for m in range(n):
        at = pl.ds(pl.multiple_of(lax.bitwise_xor(me, m) * tok, tok), tok)
        for which in range(2):
            if m:
                put(which, m - 1).wait()
            rows = dk_acc[at, :] * scale if which == 0 else dv_acc[at, :]
            stage[which] = rows.astype(BF)
            put(which, m).start()
    for which in range(2):
        put(which, n - 1).wait()


def attend_back(meta, q, grads, wide, logs, keys, values, docs, picks):
    n = len(keys)
    tok, width = q.shape
    qt, kt = 512, 512
    got = pl.pallas_call(
        functools.partial(attend_back_kernel, (n, docs, picks, qt, kt, len(grads))),
        in_specs=[SMEM] + [VMEM] * (3 + len(grads)) + [ANY] * (2 * n),
        out_specs=[VMEM] + [ANY] * 4,
        out_shape=[jax.ShapeDtypeStruct((tok, width), BF)]
        + [jax.ShapeDtypeStruct((n * tok // 2, width), BF)] * 4,
        scratch_shapes=[
            pltpu.VMEM((n * tok, width), BF),
            pltpu.VMEM((n * tok, width), BF),
            pltpu.VMEM((n * tok, width), F32),
            pltpu.VMEM((n * tok, width), F32),
            pltpu.VMEM((tok, width), BF),
            pltpu.VMEM((width // HD, HD, qt), F32),
            pltpu.VMEM((2, tok, width), BF),
            pltpu.SMEM((n * tok // MEMB,), I32),
            pltpu.SMEM((picks,), I32),
            pltpu.SemaphoreType.DMA((4,)),
        ],
        compiler_params=params(),
        cost_estimate=QUICK,
        name="attend_back",
    )(meta, q, wide, logs, *grads, *keys, *values)
    return got[0], got[1:3], got[3:5]


def mix_kernel(first, meta, x_ref, gain_ref, wo_ref, *refs):
    heads, (mixed_ref, left_ref, right_ref) = refs[:-3], refs[-3:]
    spans, qw = len(heads), heads[0].shape[1]
    mixed = x_ref[...].astype(F32)
    for k, head in enumerate(heads):
        mixed = mixed + mm(head[...], wo_ref[lax.rem(meta[1] - k + spans, spans), first:], NN)
    mixed_ref[...] = mixed
    _, _, normed = norm_rows(mixed, gain_ref[1:2, :])
    normed = normed.astype(BF)
    half = normed.shape[1] // 2
    left_ref[...] = normed[:, :half]
    right_ref[...] = normed[:, half:]


def mix(meta, x, gains, weights, heads):
    block, d = heads[0].shape[0], x.shape[1]
    whole = lambda a: pl.BlockSpec(a.shape, lambda i, meta: (0, 0))
    shape = lambda w, t: jax.ShapeDtypeStruct((block, w), t)
    outs = [shape(d, F32), shape(d // 2, BF), shape(d // 2, BF)]
    return pl.pallas_call(
        functools.partial(mix_kernel, weights.shape[1] - heads[0].shape[1]),
        grid_spec=pltpu.PrefetchScalarGridSpec(
            num_scalar_prefetch=1,
            grid=(1,),
            in_specs=[pl.BlockSpec((block, d), lambda i, meta: (meta[1], 0)), whole(gains), VMEM]
            + [whole(h) for h in heads],
            out_specs=[whole(o) for o in outs],
        ),
        out_shape=outs,
        compiler_params=params(),
        cost_estimate=QUICK,
        name="mix",
    )(meta, x, gains, weights, *heads)


def feed_kernel(cfg, meta, w_ref, g_ref, *refs):
    n, spans, fs = cfg
    pieces = refs[: 2 * n]
    normed_ref, hidden_ref, inner_ref = refs[2 * n : 2 * n + 3]
    backs = (refs[2 * n + 3 : 2 * n + 5], refs[2 * n + 5 : 2 * n + 7])
    feeds = refs[2 * n + 7 : 2 * n + 9]
    rows, stage, feed, w, sem, out_sem = refs[2 * n + 9 :]
    step, units = pl.program_id(0), spans * fs
    block, d = rows.shape[1:]
    tile, half = g_ref.shape[0], d // 2
    per = tile // block

    @pl.when(step == 0)
    def _():
        for m in range(n):
            spot = gather_place(n, m)
            pltpu.make_async_copy(pieces[m], rows.at[spot, :, :half], sem).start()
            pltpu.make_async_copy(pieces[n + m], rows.at[spot, :, half:], sem).start()
        for t in range(spans):
            for kind, first in enumerate((0, units, 2 * units)):
                w[first + t * fs : first + (t + 1) * fs] = w_ref[t, kind * fs : (kind + 1) * fs]
        pltpu.make_async_copy(rows, rows, sem).wait()

    these = pl.ds(step * per, per)
    normed = rows[these].reshape(tile, d)
    normed_ref[...] = normed
    inner = mm(normed, w[: 2 * units], NT)
    gate, up = inner[:, :units], inner[:, units:]
    sigma = jax.nn.sigmoid(gate)
    silu = gate * sigma
    hidden = (silu * up).astype(BF)
    hidden_ref[...] = hidden
    d_hidden = mm(g_ref[...], w[2 * units :], NT).astype(BF).astype(F32)
    d_gate = (d_hidden * up * (sigma * (1.0 + gate * (1.0 - sigma)))).astype(BF)
    d_inner = jnp.concatenate([d_gate, (d_hidden * silu).astype(BF)], axis=1)
    inner_ref[...] = d_inner
    stage[these] = mm(d_inner, w[: 2 * units], NN).astype(BF).reshape(per, block, d)
    feed[these] = mm(hidden, w[2 * units :], NN).astype(BF).reshape(per, block, d)
    for part in range(per):
        at = step * per + part
        for m in range(n):

            @pl.when(at == gather_place(n, m))
            def _(at=at, m=m):
                for route, cols in enumerate((slice(0, half), slice(half, d))):
                    side, spot = reduce_place(n, route, m)
                    there = backs[route][side].at[spot * block : (spot + 1) * block]
                    pltpu.make_async_copy(stage.at[at, :, cols], there, out_sem).start()
                side, spot = reduce_place(n, 0, m)
                there = feeds[side].at[spot * block : (spot + 1) * block]
                pltpu.make_async_copy(feed.at[at], there, out_sem).start()

    @pl.when(step == pl.num_programs(0) - 1)
    def _():
        pltpu.make_async_copy(stage, stage, out_sem).wait()
        pltpu.make_async_copy(feed, feed, out_sem).wait()


def feed_forward(meta, weights, grads, pieces, fs):
    n = len(pieces) // 2
    rows, d = grads.shape
    block = rows // n
    spans = weights.shape[0]
    units = spans * fs
    tile = min(512, rows)
    turned = lambda w: pl.BlockSpec((tile, w), lambda i, meta: (i, 0))
    shape = lambda w: jax.ShapeDtypeStruct((rows, w), BF)
    got = pl.pallas_call(
        functools.partial(feed_kernel, (n, spans, fs)),
        grid_spec=pltpu.PrefetchScalarGridSpec(
            num_scalar_prefetch=1,
            grid=(rows // tile,),
            in_specs=[VMEM, turned(d)] + [ANY] * (2 * n),
            out_specs=[turned(d), turned(units), turned(2 * units)] + [ANY] * 6,
            scratch_shapes=[
                pltpu.VMEM((n, block, d), BF),
                pltpu.VMEM((n, block, d), BF),
                pltpu.VMEM((n, block, d), BF),
                pltpu.VMEM((3 * units, d), BF),
                pltpu.SemaphoreType.DMA,
                pltpu.SemaphoreType.DMA,
            ],
        ),
        out_shape=[shape(d), shape(units), shape(2 * units)]
        + [jax.ShapeDtypeStruct((rows // 2, d // 2), BF)] * 4
        + [jax.ShapeDtypeStruct((rows // 2, d), BF)] * 2,
        compiler_params=params(),
        cost_estimate=QUICK,
        name="feed_forward",
    )(meta, weights, grads, *pieces)
    return got[:3], (got[3:5], got[5:7]), got[7:]


def branch_kernel(cfg, meta, left_a, left_b, right_a, right_b, mixed_ref, g_ref, gain_ref, wo_ref, *refs):
    first, n, spans = cfg
    heads, (mixed_out, gain_out), parts = refs[:spans], refs[spans : spans + 2], refs[spans + 2 : 2 * spans + 2]
    sides, (outer, sem) = refs[2 * spans + 2 : 2 * spans + 4], refs[2 * spans + 4 :]
    qw, out_rows = parts[0].shape[1], outer.shape[1] // n
    total = lambda a, b: a[...].astype(F32) + b[...].astype(F32)
    grad = jnp.concatenate([total(left_a, left_b), total(right_a, right_b)], axis=1)
    gain = gain_ref[1:2, :]
    unit, inverse, _ = norm_rows(mixed_ref[...], gain)
    gain_out[...] = jnp.sum(grad * unit, axis=0, keepdims=True)
    d_mixed = g_ref[...].astype(F32) + norm_back(grad, unit, inverse, gain)
    mixed_out[...] = d_mixed
    branch = d_mixed.astype(BF)
    for k, part in enumerate(parts):
        part[...] = mm(branch, wo_ref[lax.rem(meta[1] + k, spans), first:], NT).astype(BF)
    for k in range(spans):
        if outer.shape[1] > qw:
            outer[k, qw:] = jnp.zeros((outer.shape[1] - qw, outer.shape[2]), BF)
        outer[k, :qw] = mm(heads[(spans - k) % spans][...], branch, TN).astype(BF)
        spread(meta, outer.at[k], sides, n, 0, out_rows, sem, k * out_rows, spans * out_rows)
    pltpu.make_async_copy(outer, outer, sem).wait()


def branch_back(meta, pairs, mixed, grads, gains, weights, heads, n, first):
    block, d = mixed.shape
    spans, qw = weights.shape[0], weights.shape[1] - first
    out_rows = share_rows(qw, n)
    whole = lambda a: pl.BlockSpec(a.shape, lambda i, meta: (0, 0))
    terms = [*pairs[0], *pairs[1]]
    shape = jax.ShapeDtypeStruct
    outs = [shape((block, d), F32), shape((1, d), F32)] + [shape((block, qw), BF)] * spans
    got = pl.pallas_call(
        functools.partial(branch_kernel, (first, n, spans)),
        grid_spec=pltpu.PrefetchScalarGridSpec(
            num_scalar_prefetch=1,
            grid=(1,),
            in_specs=[whole(t) for t in terms]
            + [whole(mixed), pl.BlockSpec((block, d), lambda i, meta: (meta[1], 0)), whole(gains), VMEM]
            + [whole(h) for h in heads],
            out_specs=[whole(o) for o in outs] + [ANY] * 2,
            scratch_shapes=[pltpu.VMEM((spans, n * out_rows, d), BF), pltpu.SemaphoreType.DMA],
        ),
        out_shape=outs + [shape((n // 2 * spans * out_rows, d), BF)] * 2,
        compiler_params=params(),
        cost_estimate=QUICK,
        name="branch_back",
    )(meta, *terms, mixed, grads, gains, weights, *heads)
    return got[0], got[1], got[2 : 2 + spans], got[2 + spans :]


def place_kernel(n, meta, *refs):
    pieces, out = refs[:n], refs[n]
    rows = out.shape[0] // n
    for k, piece in enumerate(pieces):
        block = lax.rem(meta[1] - k + n, n)
        out[pl.ds(pl.multiple_of(block * rows, rows), rows), :] = piece[:rows, :].astype(out.dtype)


def place(meta, pieces, rows, kind=BF):
    n, d = len(pieces), pieces[0].shape[1]
    return pl.pallas_call(
        functools.partial(place_kernel, n),
        in_specs=[SMEM] + [VMEM] * n,
        out_specs=VMEM,
        out_shape=jax.ShapeDtypeStruct((n * rows, d), kind),
        compiler_params=params(),
        cost_estimate=QUICK,
        name="place",
    )(meta, *pieces)


def norm_back(grad_normed, unit_rows, inverse, gain_row):
    scaled = grad_normed * gain_row
    return inverse * (scaled - unit_rows * jnp.mean(scaled * unit_rows, axis=-1, keepdims=True))


def feed_grads_kernel(cfg, hidden, d_inner, normed, grads, out):
    spans, fs = cfg
    units = spans * fs
    pairs = [(d_inner.at[:, :units], normed), (d_inner.at[:, units:], normed), (hidden, grads)]
    for kind, (left, right) in enumerate(pairs):
        product = mm(left[...], right[...], TN).astype(BF)
        for t in range(spans):
            out[t, kind * fs : (kind + 1) * fs] = product[t * fs : (t + 1) * fs]


def feed_grads(hidden, d_inner, normed, grads, fs):
    (rows, units), d = hidden.shape, normed.shape[1]
    return pl.pallas_call(
        functools.partial(feed_grads_kernel, (units // fs, fs)),
        in_specs=[VMEM] * 4,
        out_specs=VMEM,
        out_shape=jax.ShapeDtypeStruct((units // fs, 3 * fs, d), BF),
        compiler_params=params(),
        cost_estimate=QUICK,
        name="feed_grads",
    )(hidden, d_inner, normed, grads)


def share_rows(rows, n):
    return -(-rows // (16 * n)) * 16


def spread(meta, stage, sides, n, route, rows, sem, base=0, total=None):
    for m in range(n):
        at = pl.ds(pl.multiple_of(lax.bitwise_xor(meta[0], m) * rows, rows), rows)
        side, spot = reduce_place(n, route, m)
        first = spot * (total or rows) + base
        pltpu.make_async_copy(stage.at[at], sides[side].at[first : first + rows], sem).start()


def both(pair):
    return (pair[0][...].astype(F32) + pair[1][...].astype(F32)).astype(BF)


def late_kernel(cfg, meta, dq, dk_a, dk_b, dv_a, dv_b, normed, *refs):
    n, qw = cfg
    sides, (stage, sem) = refs[:2], refs[2:]
    used = 3 * qw
    if stage.shape[0] > used:
        stage[used:] = jnp.zeros((stage.shape[0] - used, stage.shape[1]), BF)
    for at, left in enumerate((dq[...], both((dk_a, dk_b)), both((dv_a, dv_b)))):
        stage[at * qw : (at + 1) * qw] = mm(left, normed[...], TN).astype(BF)
    spread(meta, stage, sides, n, 0, stage.shape[0] // n, sem)
    pltpu.make_async_copy(stage, stage, sem).wait()


def late_grads(meta, dq, dk, dv, normed, n):
    (tok, qw), d = dq.shape, normed.shape[1]
    rows = share_rows(3 * qw, n)
    return pl.pallas_call(
        functools.partial(late_kernel, (n, qw)),
        in_specs=[SMEM] + [VMEM] * 6,
        out_specs=[ANY] * 2,
        out_shape=[jax.ShapeDtypeStruct((n * rows // 2, d), BF)] * 2,
        scratch_shapes=[pltpu.VMEM((n * rows, d), BF), pltpu.SemaphoreType.DMA],
        compiler_params=params(),
        cost_estimate=QUICK,
        name="late_grads",
    )(meta, dq, *dk, *dv, normed)


def soap_kernel(cfg, meta, held, early, late, weight_ref, first_ref, second_ref, average_ref, stat_ref, basis_ref,
                weight_out, first_out, second_out, average_out, stat_out, turned_out, grads, wide, sem):
    n, late_panels, out_panels, pf, cap, rows, out_rows, group = cfg
    slots, panel, width = weight_ref.shape
    me, step = meta[0], pl.program_id(0)
    inner_panels = late_panels - out_panels

    def fetch(slot, source, share, base):
        grain = min(share, panel)
        for part in range(panel // grain):
            row = source * panel + part * grain
            at = gather_place(n, lax.bitwise_xor(me, row // share)) * (rows + out_rows) + base + row % share
            there = grads.at[slot, part * grain : (part + 1) * grain]
            pltpu.make_async_copy(late.at[pl.ds(pl.multiple_of(at, grain), grain)], there, sem).start()

    @pl.when(step == 0)
    def _():
        for slot in range(slots):
            source = held[slot]

            @pl.when(source < 0)
            def _(slot=slot):
                grads[slot] = jnp.zeros((panel, grads.shape[2]), BF)

            @pl.when((source >= 0) & (source < inner_panels))
            def _(slot=slot, source=source):
                fetch(slot, source, rows, 0)

            @pl.when((source >= inner_panels) & (source < late_panels))
            def _(slot=slot, source=source):
                fetch(slot, source - inner_panels, out_rows, rows)

            @pl.when(source >= late_panels)
            def _(slot=slot, source=source):
                kind, unit = (source - late_panels) // pf, (source - late_panels) % pf
                spot = (unit // cap) * 3 * cap + kind * cap + unit % cap
                pltpu.make_async_copy(early.at[spot], grads.at[slot], sem).start()

        for slot in range(slots):

            @pl.when(held[slot] >= 0)
            def _(slot=slot):
                pltpu.make_async_copy(grads.at[slot], grads.at[slot], sem).wait()

    high = functools.partial(lax.dot_general, precision=HIGH, preferred_element_type=F32)
    cols = pl.ds(pl.multiple_of(step * width, width), width)

    def parts(value):
        top = value.astype(BF)
        return top, (value - top.astype(F32)).astype(BF)

    for low in range(0, slots, group):
        count = min(group, slots - low)
        size = count * panel
        slot_range = slice(low, low + count)
        diagonal = wide.at[low // group]

        @pl.when(step == 0)
        def _(low=low, count=count, diagonal=diagonal):
            diagonal[...] = jnp.zeros_like(diagonal)
            for j in range(count):
                at = slice(j * panel, (j + 1) * panel)
                diagonal[at, at] = basis_ref[low + j]
                stat_out[low + j] = BETA_TWO * stat_ref[low + j]

        grad = grads[slot_range, :, cols].reshape(size, width)
        square = mm(grad, grad, NT)
        for j in range(count):
            at = slice(j * panel, (j + 1) * panel)
            stat_out[low + j] += (1.0 - BETA_TWO) * square[at, at]
        top, rest = parts(diagonal[:size, :size])
        flat = lambda ref, slot_range=slot_range, size=size: ref[slot_range].reshape(size, width)
        rotated = mm(top, grad, TN) + mm(rest, grad, TN)
        first = BETA_ONE * flat(first_ref) + (1.0 - BETA_ONE) * rotated
        second = BETA_TWO * flat(second_ref) + (1.0 - BETA_TWO) * rotated * rotated
        direction = (first / (1.0 - BETA_ONE**STEP)) / (
            jnp.sqrt(second / (1.0 - BETA_TWO**STEP)) + ADAM_EPSILON
        )
        high_part, low_part = parts(direction)
        update = mm(top, high_part, NN) + (mm(top, low_part, NN) + mm(rest, high_part, NN))
        weight = flat(weight_ref)
        new_weight = weight - RATE * (update + WEIGHT_DECAY * weight)
        average = AVERAGE_DECAY * flat(average_ref) + (1.0 - AVERAGE_DECAY) * new_weight
        shape = (count, panel, width)
        first_out[slot_range] = first.reshape(shape)
        second_out[slot_range] = second.reshape(shape)
        weight_out[slot_range] = new_weight.reshape(shape)
        average_out[slot_range] = average.reshape(shape)

        @pl.when(step == pl.num_programs(0) - 1)
        def _(low=low, count=count):
            for j in range(count):
                turned_out[low + j] = high(stat_out[low + j], basis_ref[low + j], NN)


def soap(meta, held, early, late, n, weight, first, second, average, stat, basis, late_panels, out_panels, pf, cap, rows):
    slots, panel, d = weight.shape
    width, group = 256, 8
    out_rows = late.shape[0] // n - rows
    big = pl.BlockSpec((slots, panel, width), lambda i, meta, held: (0, 0, i))
    small = pl.BlockSpec((slots, panel, panel), lambda i, meta, held: (0, 0, 0))
    shape = jax.ShapeDtypeStruct
    return pl.pallas_call(
        functools.partial(soap_kernel, (n, late_panels, out_panels, pf, cap, rows, out_rows, group)),
        grid_spec=pltpu.PrefetchScalarGridSpec(
            num_scalar_prefetch=2,
            grid=(d // width,),
            in_specs=[ANY] * 2 + [big] * 4 + [small] * 2,
            out_specs=[big] * 4 + [small] * 2,
            scratch_shapes=[
                pltpu.VMEM((slots, panel, d), BF),
                pltpu.VMEM((-(-slots // group), group * panel, group * panel), F32),
                pltpu.SemaphoreType.DMA,
            ],
        ),
        out_shape=[shape((slots, panel, d), F32)] * 4 + [shape((slots, panel, panel), F32)] * 2,
        compiler_params=params(),
        cost_estimate=QUICK,
        name="soap",
    )(meta, held, early, late, weight, first, second, average, stat, basis)


def orthonormal_kernel(columns_ref, out_ref):
    size = columns_ref.shape[0]
    out_ref[...] = columns_ref[...]
    for i in range(size):
        vector = out_ref[i]
        vector = vector * lax.rsqrt(jnp.sum(vector * vector, axis=0, keepdims=True))
        out_ref[i] = vector
        if i < size - 1:
            rest = out_ref[i + 1 :]
            out_ref[i + 1 :] = rest - jnp.sum(rest * vector[None], axis=1, keepdims=True) * vector[None]


def orthonormal(matrix):
    columns = jnp.transpose(matrix, (2, 1, 0))
    found = pl.pallas_call(
        orthonormal_kernel,
        in_specs=[VMEM],
        out_specs=VMEM,
        out_shape=jax.ShapeDtypeStruct(columns.shape, F32),
        compiler_params=params(),
        name="orthonormal",
    )(columns)
    return jnp.transpose(found, (2, 1, 0))


def adam_gain(gradient, weight, first_state, second):
    new_first = BETA_ONE * first_state + (1.0 - BETA_ONE) * gradient
    new_second = BETA_TWO * second + (1.0 - BETA_TWO) * gradient * gradient
    direction = (
        new_first
        / (1.0 - BETA_ONE**STEP)
        / (jnp.sqrt(new_second / (1.0 - BETA_TWO**STEP)) + ADAM_EPSILON)
    )
    return (weight - GAIN_RATE * direction, new_first, new_second)


def back_kernel(meta, x_ref, dq, dk_a, dk_b, dv_a, dv_b, wq, wk, wv, out, gain_out):
    total = mm(dq[...], wq[...], NN) + mm(both((dk_a, dk_b)), wk[...], NN)
    total = total + mm(both((dv_a, dv_b)), wv[...], NN)
    out[...] = total.astype(BF)
    unit, _, _ = norm_rows(x_ref[...].astype(F32), 1.0)
    share = jnp.sum(total * unit, axis=0, keepdims=True)

    @pl.when(pl.program_id(0) == 0)
    def _():
        gain_out[...] = share

    @pl.when(pl.program_id(0) > 0)
    def _():
        gain_out[...] += share


def back_in(meta, x, dq, dk, dv, wq, wk, wv, n, low, high):
    tok, (qw, d) = dq.shape[0], wq.shape
    tile = tok // n
    rows = lambda w: pl.BlockSpec((tile, w), lambda i, meta: ((meta[1] - i - low + n) % n, 0))
    whole = pl.BlockSpec((qw, d), lambda i, meta: (0, 0))
    return pl.pallas_call(
        back_kernel,
        grid_spec=pltpu.PrefetchScalarGridSpec(
            num_scalar_prefetch=1,
            grid=(high - low,),
            in_specs=[rows(d)] + [rows(qw)] * 5 + [whole] * 3,
            out_specs=[pl.BlockSpec((tile, d), lambda i, meta: (i, 0)), pl.BlockSpec((1, d), lambda i, meta: (0, 0))],
        ),
        out_shape=[jax.ShapeDtypeStruct(((high - low) * tile, d), BF), jax.ShapeDtypeStruct((1, d), F32)],
        compiler_params=params(),
        cost_estimate=QUICK,
        name="back_in",
    )(meta, x, dq, *dk, *dv, wq, wk, wv)


def shards(
    tokens,
    cotangent,
    lengths,
    retrieve,
    owners,
    masters,
    first_moment,
    second_moment,
    averaged,
    statistics,
    bases,
    gains,
    gain_first,
    gain_second,
):
    tok, d = tokens.shape
    n_seq, n_tp = lax.axis_size("seq"), lax.axis_size("tp")
    me, z = lax.axis_index("seq"), lax.axis_index("tp")
    qw, ff = H // n_tp * HD, FF // n_tp
    slots_dev, panel = masters.shape[1:3]
    split = (slots_dev + 1) // 2
    docs, picks = lengths.shape[0], retrieve.shape[1]
    recalled = lax.dynamic_index_in_dim(retrieve, me, 0, keepdims=False)
    meta = jnp.concatenate([jnp.stack([me, z]).astype(I32), lengths, recalled])
    block = tok // n_tp
    pq, pf = qw // panel, ff // panel
    cap = -(-pf // n_seq)
    fs = cap * panel
    slot_ids = me * slots_dev + jnp.arange(slots_dev, dtype=I32)
    panel_ids = jnp.arange(1, owners.shape[0] + 1, dtype=I32)
    held = jnp.sum(jnp.where(slot_ids[:, None] == owners[None, :], panel_ids[None, :], 0), axis=1) - 1

    def mine(rows):
        return lax.dynamic_slice_in_dim(rows, z * block, block, 0)

    def whole_tp(rows):
        return lax.all_gather(rows, "tp", axis=0, tiled=True)

    def whole_seq(rows):
        return lax.all_gather(rows, "seq", axis=0, tiled=True)

    own = masters[0].astype(BF)
    pieces, _ = gather_seq([own[:split], own[split:]], n_seq)
    pieces = list(zip(*pieces, strict=True))
    q, k, v, normed_one, inner, share = project_in(
        meta, owners, tokens, gains, pieces, pq, pf, cap, slots_dev, split
    )
    (keys, values), _ = gather_seq([k, v], n_seq)
    weights = whole_tp(share).reshape(n_tp, -1, d)
    own_grads, keys[n_seq - 2], values[n_seq - 2] = pin(mine(cotangent), keys[n_seq - 2], values[n_seq - 2])
    grads_all = direct_pieces(own_grads, n_seq)
    turned_heads, wide, logs = attend(meta, q, keys, values, docs, picks, block)
    turned_heads, grads_all = pin(turned_heads, grads_all)
    heads = trade_tp([turned_heads[i * block : (i + 1) * block] for i in range(n_tp)], n_tp)
    mixed, left, right = mix(meta, tokens, gains, weights, heads)
    left, grads_all = pin(left, grads_all)
    grads_all = core_gather(jnp.concatenate(grads_all, axis=0), n_seq)
    (left, right), _ = gather_seq([left, right], n_seq)
    (normed_two, hidden, d_inner), pairs, feed = feed_forward(meta, weights, grads_all, left + right, fs)

    last = len(routes(n_seq)[0])
    inner_rows, out_rows = share_rows(3 * qw, n_seq), share_rows(qw, n_seq)
    feed_sums_in = (hidden, d_inner, normed_two, grads_all)
    for at in range(last + 1):
        pairs = reduce_levels(pairs, n_seq, at)
        if at == last - 1:
            pairs, feed, feed_sums = pin(pairs, (feed[0], swap(feed[1], n_seq, 1)), feed_sums)
            feed = plus(*feed)
        elif at == 0:
            pairs, feed, feed_sums_in = pin(pairs, feed, feed_sums_in)
            feed_sums = feed_grads(*feed_sums_in, fs)
    d_mixed, grad_gain_two, d_heads, outer = branch_back(
        meta, pairs, mixed, cotangent, gains, weights, heads, n_seq, 3 * fs
    )
    d_heads = trade_tp(d_heads, n_tp)
    outer = plus(outer[0], swap(outer[1], n_seq, 1))

    size = n_tp * out_rows
    parts = {}
    for m in range(0, n_seq, 2):
        at = reduce_place(n_seq, 0, m)[1]
        parts[m] = jnp.concatenate([feed[at * block : (at + 1) * block], outer[at * size : (at + 1) * size]], axis=0)
    d_heads, parts, feed_sums = pin(d_heads, parts, feed_sums)
    parts = [swap(part, n_seq, m) if m else part for m, part in parts.items()]
    feed_sums = lax.psum_scatter(feed_sums.reshape(-1, d), "tp", scatter_dimension=0, tiled=True)
    dq, *pairs = attend_back(meta, q, d_heads, wide, logs, keys, values, docs, picks)
    parts, feed_sums, dq, pairs = pin(parts, feed_sums, dq, pairs)
    pairs = reduce_levels(pairs, n_seq, 0)
    total = sum(part.astype(F32) for part in parts)
    output = (mixed + total[:block]).astype(BF)
    outer = [total[block + k * out_rows : block + (k + 1) * out_rows].astype(BF) for k in range(n_tp)]
    outputs = [output]
    for at in range(last + 1):
        if at:
            pairs = reduce_levels(pairs, n_seq, at)
            while len(outputs) < n_tp and (at == last or len(outputs) < 1 + 2 * at):
                outputs.append(ring(outputs[-1], n_tp, 1))
        pairs, outputs, feed_sums, dq = pin(pairs, outputs, feed_sums, dq)
    dk, dv = pairs
    output = place(meta, outputs, block)
    early = whole_seq(feed_sums).reshape(-1, panel, d)

    inputs = (meta, tokens, dq, dk, dv, inner[0], inner[1], inner[2], n_tp)
    total, gain_a = back_in(*inputs, n_tp - 1, n_tp)
    total, lefts = pin(total, (dq, dk, dv))
    back_rest, gain_b = back_in(meta, tokens, *lefts, *inputs[5:], 0, n_tp - 1)
    gain_total = jnp.concatenate([gain_a + gain_b, grad_gain_two], axis=0)
    late = late_grads(meta, *lefts, normed_one, n_seq)

    def advance(late, step):
        if step == 1:
            late = plus(late[0], swap(late[1], n_seq, 1))
        elif step == 2:
            parts = direct_reduce(late, n_seq, inner_rows)
            late = sum(part.astype(F32) for part in parts).astype(BF)
            late = jnp.concatenate([late, outer], axis=0)
        elif step == 3:
            late = direct_gather(late, n_seq)
        elif step == 4:
            late = core_gather(late, n_seq)
        return late

    steps = max(2 * (n_tp - 1), 6)
    gain_steps = sum_steps(n_seq, n_tp)
    gather = []
    for step in range(steps):
        if step < n_tp - 1:
            k = n_tp - 2 - step
            came = ring(total, n_tp, -1)
            late = advance(late, step)
            if step == 0:
                outer = trade_tp(outer, n_tp)
            if step == 1:
                came, output = pin(came, output)
            for _ in range(min(len(gain_steps), 2 if 0 < step else 0)):
                gain_total = gain_steps.pop(0)(gain_total)
            came, late, back_rest, outer, held, gain_total = pin(came, late, back_rest, outer, held, gain_total)
            if step == 0:
                outer = sum(part.astype(F32) for part in outer).astype(BF)
            part = back_rest[k * block : (k + 1) * block]
            if k:
                total = plus(part, came)
                continue
            d_normed_one = part.astype(F32) + came.astype(F32)
            unit_one, inverse_one, _ = norm_rows(mine(tokens).astype(F32), gains[0])
            grad_here = d_mixed + norm_back(d_normed_one, unit_one, inverse_one, gains[0])
            gather.append(grad_here.astype(BF))
            continue
        if len(gather) < n_tp:
            gather.append(ring(gather[-1], n_tp, 1))
        for _ in range(min(len(gain_steps), 1)):
            gain_total = gain_steps.pop(0)(gain_total)
        late = advance(late, step)
        if step == steps - 2:
            new_weight, new_first, new_second, new_average, new_stat, turned_basis = soap(
                meta, held, early, late, n_seq, masters[0], first_moment[0], second_moment[0], averaged[0],
                statistics[0], bases[0], 4 * pq, pq, pf, cap, inner_rows,
            )
            gather[-1], turned_basis, gain_total = pin(gather[-1], turned_basis, gain_total)
        elif step == steps - 1:
            new_basis = orthonormal(turned_basis)
            gather, new_basis, gain_total = pin(gather, new_basis, gain_total)
        else:
            gather[-1], late, gain_total = pin(gather[-1], late, gain_total)
    for step in gain_steps:
        gain_total = step(gain_total)
    grad_input = place(meta, gather, block, F32)
    new_gains, new_gain_first, new_gain_second = adam_gain(gain_total, gains, gain_first, gain_second)
    return (
        output,
        grad_input,
        new_weight[None],
        new_first[None],
        new_second[None],
        new_average[None],
        new_stat[None],
        new_basis[None],
        new_gains,
        new_gain_first,
        new_gain_second,
    )


def solution(mesh):
    by_token, by_slot = P("seq", None), P("tp", "seq", None, None)
    in_specs = (by_token, by_token, P(), P(), P()) + (by_slot,) * 6 + (P(),) * 3
    out_specs = (by_token, by_token) + (by_slot,) * 6 + (P(),) * 3
    return jax.shard_map(shards, mesh=mesh, in_specs=in_specs, out_specs=out_specs, check_vma=False)
```

```python
import functools

import jax
import jax.numpy as jnp
from jax import lax
from jax.experimental import pallas as pl
from jax.experimental.pallas import tpu as pltpu
from jax.sharding import PartitionSpec as P

H = 8
HD = 128
FF = 2816
MEMB = 128
STEP = 10

EPSILON = 1e-06
RATE = 0.02
GAIN_RATE = 0.5
BETA_ONE = 0.9
BETA_TWO = 0.95
ADAM_EPSILON = 1e-08
WEIGHT_DECAY = 0.01
AVERAGE_DECAY = 0.8
NEGATIVE = -1e30
START_TOP = -1e29
LOG2E = 1.4426950408889634

BF = jnp.bfloat16
F32 = jnp.float32
I32 = jnp.int32
HIGH = lax.Precision.HIGHEST
ANY = pl.BlockSpec(memory_space=pl.ANY)
SMEM = pl.BlockSpec(memory_space=pltpu.SMEM)
VMEM = pl.BlockSpec(memory_space=pltpu.VMEM)
VMEM_BYTES = 58 * 2**20

NT = (((1,), (1,)), ((), ()))
NN = (((1,), (0,)), ((), ()))
TN = (((0,), (0,)), ((), ()))


def mm(left, right, dims):
    return lax.dot_general(left, right, dims, preferred_element_type=F32)


QUICK = pl.CostEstimate(flops=1000, bytes_accessed=1000, transcendentals=0)


def params(**more):
    return pltpu.CompilerParams(vmem_limit_bytes=VMEM_BYTES, **more)


def pin(*values):
    return lax.optimization_barrier(values)


def routes(count):
    bits = []
    bit = 2
    while bit < count:
        bits.append(bit)
        bit *= 2
    return bits, bits[::-1]


def swap(value, count, bit):
    return lax.ppermute(value, "seq", [(i, i ^ bit) for i in range(count)])


def gather_seq(owns, count, beside=None):
    orders = routes(count)
    held = [{0: own} for own in owns]
    hops = len(orders[0])
    for stage in range(hops + 1):
        for i, pieces in enumerate(held):
            order = orders[i % 2]
            come = {}
            for m, piece in pieces.items():
                if m & 1 or bin(m).count("1") != stage:
                    continue
                for bit in order:
                    if all(other == bit or not m & other for other in order[order.index(bit) :]) and not m & bit:
                        come[m | bit] = swap(piece, count, bit)
                come[m | 1] = swap(piece, count, 1)
            pieces.update(come)
        if stage < hops:
            held, beside = pin(held, beside)
    return [[pieces[m] for m in range(count)] for pieces in held], beside


def plus(left, right):
    return (left.astype(F32) + right.astype(F32)).astype(left.dtype)


def reduce_bits(count, route):
    return [1, *routes(count)[route][::-1]]


def reduce_place(count, route, m):
    bits = reduce_bits(count, route)
    block = 0
    for bit in bits[1:]:
        block = 2 * block + bool(m & bit)
    return int(bool(m & bits[0])), block


def reduce_level(pair, count, route, at):
    keep, send = pair
    bits = reduce_bits(count, route)
    came = swap(send, count, bits[at])
    if at == len(bits) - 1:
        return keep, came
    half = keep.shape[0] // 2
    return plus(keep[:half], came[:half]), plus(keep[half:], came[half:])


def reduce_levels(pairs, count, at):
    return [reduce_level(pair, count, i % 2, at) for i, pair in enumerate(pairs)]


def direct_reduce(rows, count, sizes):
    parts = []
    for m in range(0, count, 2):
        at = reduce_place(count, 0, m)[1]
        part = rows[at * sizes : (at + 1) * sizes]
        parts.append(swap(part, count, m) if m else part)
    return parts


def direct_pieces(rows, count):
    return [swap(rows, count, m) if m else rows for m in range(0, count, 2)]


def direct_gather(rows, count):
    return jnp.concatenate(direct_pieces(rows, count), axis=0)


def core_gather(rows, count):
    return jnp.concatenate([rows, swap(rows, count, 1)], axis=0)


def gather_place(count, distance):
    return distance // 2 + (count // 2) * (distance % 2)


def ring(value, count, step):
    return lax.ppermute(value, "tp", [(i, (i + step) % count) for i in range(count)])


def trade_tp(parts, count):
    return [parts[0]] + [ring(parts[k], count, k) for k in range(1, count)]


def gather_tp(own, count):
    pieces = [own]
    for _ in range(count - 1):
        pieces.append(ring(pieces[-1], count, 1))
    return pieces


def reduce_tp(parts, count):
    total = parts[count - 1]
    for k in range(count - 2, -1, -1):
        came = ring(total, count, -1)
        if k == 0:
            return parts[0], came
        total = plus(parts[k], came)
    return None


def sum_steps(n_seq, n_tp):
    steps = []
    for axis, count in (("seq", n_seq), ("tp", n_tp)):
        bit = 1
        while bit < count:
            pairs = [(i, i ^ bit) for i in range(count)]
            steps.append(lambda v, axis=axis, pairs=pairs: v + lax.ppermute(v, axis, pairs))
            bit *= 2
    return steps


def panel_copies(owners_ref, me, first, amount, slots_dev, split, pieces, view, sem, back):
    def one(i, carry):
        slot = owners_ref[first + i]
        spot = lax.bitwise_xor(slot // slots_dev, me)
        row = slot % slots_dev
        for m, (low, high) in enumerate(pieces):
            for ref, base, size in ((low, 0, split), (high, split, slots_dev - split)):

                @pl.when((spot == m) & (row >= base) & (row < base + size))
                def _(ref=ref, base=base):
                    there = ref.at[row - base]
                    source, target = (view(i), there) if back else (there, view(i))
                    pltpu.make_async_copy(source, target, sem).start()

        return carry

    lax.fori_loop(0, amount, one, 0)


def norm_rows(rows, gain):
    inverse = lax.rsqrt(jnp.mean(rows * rows, axis=-1, keepdims=True) + EPSILON)
    unit = rows * inverse
    return unit, inverse, unit * gain


def project_kernel(cfg, meta, owners, x_ref, gain_ref, *refs):
    n, pq, pf, cap, slots_dev, split = cfg
    pieces = list(zip(refs[:n], refs[n : 2 * n], strict=True))
    outs = refs[2 * n : 2 * n + 3]
    normed_ref, inner, share, sems = refs[2 * n + 3 :]
    me, panel, d = meta[0], inner.shape[1], x_ref.shape[1]
    mine = jnp.clip(pf - me * cap, 0, cap)

    @pl.when(pl.program_id(0) == 0)
    def _():
        copies = functools.partial(panel_copies, owners, me)
        copies(0, 3 * pq, slots_dev, split, pieces, lambda i: inner.at[i], sems.at[0], False)
        copies(3 * pq, pq, slots_dev, split, pieces, lambda i: share.at[3 * cap + i], sems.at[1], False)
        for kind in range(3):
            for j in range(cap):

                @pl.when(j >= mine)
                def _(at=kind * cap + j):
                    share[at] = jnp.zeros(share.shape[1:], BF)

            copies(
                4 * pq + kind * pf + me * cap, mine, slots_dev, split, pieces,
                lambda i, kind=kind: share.at[kind * cap + i], sems.at[1], False,
            )

    _, _, normed = norm_rows(x_ref[...].astype(F32), gain_ref[0:1, :])
    normed = normed.astype(BF)
    normed_ref[...] = normed

    @pl.when(pl.program_id(0) == 0)
    def _():
        pltpu.make_async_copy(inner, inner, sems.at[0]).wait()

    for at in range(3):
        w = inner[at * pq : (at + 1) * pq].reshape(pq * panel, d)
        outs[at][...] = mm(normed, w, NT).astype(BF)

    @pl.when(pl.program_id(0) == pl.num_programs(0) - 1)
    def _():
        def finish(i, c):
            pltpu.make_async_copy(share.at[0], share.at[0], sems.at[1]).wait()
            return c

        lax.fori_loop(0, 3 * mine + pq, finish, 0)


def project_in(meta, owners, x, gains, pieces, pq, pf, cap, slots_dev, split):
    n = len(pieces)
    tok, d = x.shape
    panel = pieces[0][0].shape[1]
    qw = pq * panel
    tile = 256
    out = lambda w: pl.BlockSpec((tile, w), lambda i: (i, 0))
    whole = lambda count: pl.BlockSpec((count, panel, d), lambda i: (0, 0, 0))
    shape = lambda *dims: jax.ShapeDtypeStruct(dims, BF)
    q, k, v, normed, inner, share = pl.pallas_call(
        functools.partial(project_kernel, (n, pq, pf, cap, slots_dev, split)),
        grid=(tok // tile,),
        in_specs=[SMEM, SMEM, out(d), pl.BlockSpec(gains.shape, lambda i: (0, 0))] + [ANY] * (2 * n),
        out_specs=[out(qw)] * 3 + [out(d), whole(3 * pq), whole(3 * cap + pq)],
        out_shape=[shape(tok, qw)] * 3 + [shape(tok, d), shape(3 * pq, panel, d), shape(3 * cap + pq, panel, d)],
        scratch_shapes=[pltpu.SemaphoreType.DMA((2,))],
        compiler_params=params(),
        cost_estimate=QUICK,
        name="project",
    )(meta, owners, x, gains, *[p[0] for p in pieces], *[p[1] for p in pieces])
    return q, k, v, normed, inner.reshape(3, qw, d), share.reshape(-1, d)


def doc_start(meta, positions, docs):
    start = jnp.int32(0)
    found = jnp.zeros_like(positions)
    for at in range(docs):
        found = jnp.where(positions >= start, start, found)
        start = start + meta[2 + at]
    return found


def load_pieces(me, pieces, buffer, sem, tok):
    for m, piece in enumerate(pieces):
        owner = lax.bitwise_xor(me, m)
        at = pl.multiple_of(owner * tok, tok)
        pltpu.make_async_copy(piece, buffer.at[pl.ds(at, tok)], sem).start()


def member_table(meta, table, docs, picks, blocks):
    def clear(i, c):
        table[i] = 0
        return c

    lax.fori_loop(0, blocks, clear, 0)
    for e in range(picks):
        table[meta[2 + docs + e]] = 1


def memory_list(meta, blocks_ref, docs, picks, limit):
    count = jnp.int32(0)
    for e in range(picks):
        block = meta[2 + docs + e]
        fresh = (block + 1) * MEMB <= limit
        for other in range(e):
            fresh = fresh & (meta[2 + docs + other] != block)

        @pl.when(fresh)
        def _(count=count, block=block):
            blocks_ref[count] = block

        count = count + fresh.astype(I32)
    return count


def seen_rows(at, rows, table, starts, queries):
    row = lax.broadcasted_iota(I32, (MEMB, queries.shape[1]), 0)
    seen = []
    for b in range(rows // MEMB):
        base = at + b * MEMB
        lowest = starts * (1 - table[base // MEMB]) - base
        seen.append((row >= lowest) & (row <= queries - base))
    return seen


def hide(scores, seen, fill):
    kept = [jnp.where(mask, scores[b * MEMB : (b + 1) * MEMB], fill) for b, mask in enumerate(seen)]
    return jnp.concatenate(kept, axis=0)


def rows_of(buffer, spots, rows, cols):
    parts = [buffer[pl.ds(at, rows), cols] for at in spots]
    return parts[0] if len(parts) == 1 else jnp.concatenate(parts, axis=0)


def visit_keys(visit, state, meta, first, qt, kt, docs, picks, blocks):
    low = doc_start(meta, first, docs) // kt
    high = (first + qt - 1) // kt + 1
    clear = jnp.clip((doc_start(meta, first + qt - 1, docs) + kt - 1) // kt, low, high)
    full = jnp.clip(first // kt, clear, high)
    count = memory_list(meta, blocks, docs, picks, low * kt)

    def dense(masked):
        return lambda i, state: visit([pl.multiple_of(i * kt, kt)], kt, state, masked)

    def memory(together, base):
        def go(i, state):
            spots = [pl.multiple_of(blocks[base + i * together + j] * MEMB, MEMB) for j in range(together)]
            return visit(spots, MEMB, state, False)

        return go

    state = lax.fori_loop(low, clear, dense(True), state)
    state = lax.fori_loop(clear, full, dense(False), state)
    state = lax.fori_loop(full, high, dense(True), state)
    state = lax.fori_loop(0, count // 4, memory(4, 0), state)
    return lax.fori_loop(0, count % 4, memory(1, count // 4 * 4), state)


def attend_kernel(cfg, meta, q_ref, *refs):
    n, docs, picks, qt, kt, block = cfg
    keys, values = refs[:n], refs[n : 2 * n]
    turn_ref, wide_ref, log_ref, kbuf, vbuf, acc, table, blocks, sems = refs[2 * n :]
    tok, width = q_ref.shape
    me = meta[0]
    factor = HD**-0.5 * LOG2E
    load_pieces(me, keys, kbuf, sems.at[0], tok)
    load_pieces(me, values, vbuf, sems.at[1], tok)
    member_table(meta, table, docs, picks, kbuf.shape[0] // MEMB)
    pltpu.make_async_copy(kbuf, kbuf, sems.at[0]).wait()
    pltpu.make_async_copy(vbuf, vbuf, sems.at[1]).wait()
    heads = [slice(head * HD, (head + 1) * HD) for head in range(width // HD)]
    spans = tok // block

    def query_tile(t, carry):
        base = pl.multiple_of(t * qt, qt)
        first = me * tok + base
        queries = first + lax.broadcasted_iota(I32, (1, qt), 1)
        starts = doc_start(meta, queries, docs)
        acc[...] = jnp.zeros_like(acc)

        def visit(spots, rows, state, masked):
            seen = seen_rows(spots[0], rows, table, starts, queries) if masked else None
            result = []
            for head, cols in enumerate(heads):
                top, total = state[head]
                scores = mm(rows_of(kbuf, spots, rows, cols), q_ref[pl.ds(base, qt), cols], NT)
                if masked:
                    scores = hide(scores, seen, NEGATIVE)
                new_top = jnp.maximum(top, jnp.max(scores, axis=0, keepdims=True))
                fade = jnp.exp2((top - new_top) * factor)
                probs = jnp.exp2((scores - new_top) * factor)
                total = total * fade + jnp.sum(probs, axis=0, keepdims=True)
                product = mm(rows_of(vbuf, spots, rows, cols), probs.astype(BF), TN)
                acc[head] = acc[head] * fade + product
                result.append((new_top, total))
            return tuple(result)

        state = tuple((jnp.full((1, qt), START_TOP, F32), jnp.zeros((1, qt), F32)) for _ in heads)
        state = visit_keys(visit, state, meta, first, qt, kt, docs, picks, blocks)
        for head, cols in enumerate(heads):
            top, total = state[head]
            rows = jnp.transpose(acc[head] * (1.0 / total))
            wide_ref[pl.ds(base, qt), cols] = rows
            rows = rows.astype(BF)
            for part in range(max(qt // block, 1)):
                size = min(block, qt)
                spot = lax.rem(base // block + part - meta[1] + spans, spans) * block + lax.rem(base, block)
                spot = pl.multiple_of(spot, size)
                turn_ref[pl.ds(spot, size), cols] = rows[part * size : (part + 1) * size]
            log_ref[head : head + 1, pl.ds(base, qt)] = top * factor + jnp.log2(total)
        return carry

    lax.fori_loop(0, tok // qt, query_tile, 0)


def attend(meta, q, keys, values, docs, picks, block):
    n = len(keys)
    tok, width = q.shape
    qt, kt = 512, 1024
    return pl.pallas_call(
        functools.partial(attend_kernel, (n, docs, picks, qt, kt, block)),
        in_specs=[SMEM, VMEM] + [ANY] * (2 * n),
        out_specs=[VMEM] * 3,
        out_shape=[
            jax.ShapeDtypeStruct((tok, width), BF),
            jax.ShapeDtypeStruct((tok, width), F32),
            jax.ShapeDtypeStruct((width // HD, tok), F32),
        ],
        scratch_shapes=[
            pltpu.VMEM((n * tok, width), BF),
            pltpu.VMEM((n * tok, width), BF),
            pltpu.VMEM((width // HD, HD, qt), F32),
            pltpu.SMEM((n * tok // MEMB,), I32),
            pltpu.SMEM((picks,), I32),
            pltpu.SemaphoreType.DMA((2,)),
        ],
        compiler_params=params(),
        cost_estimate=QUICK,
        name="attend",
    )(meta, q, *keys, *values)


def attend_back_kernel(cfg, meta, q_ref, wide_ref, log_ref, *refs):
    n, docs, picks, qt, kt, spans = cfg
    parts, refs = refs[:spans], refs[spans:]
    keys, values = refs[:n], refs[n : 2 * n]
    dq_ref = refs[2 * n]
    outs = (refs[2 * n + 1 : 2 * n + 3], refs[2 * n + 3 : 2 * n + 5])
    kbuf, vbuf, dk_acc, dv_acc, g_ref, acc, stage, table, blocks, sems, out_sems = refs[2 * n + 5 :]
    tok, width = q_ref.shape
    me = meta[0]
    block = tok // spans
    scale = HD**-0.5
    factor = scale * LOG2E
    load_pieces(me, keys, kbuf, sems.at[0], tok)
    load_pieces(me, values, vbuf, sems.at[1], tok)
    member_table(meta, table, docs, picks, kbuf.shape[0] // MEMB)

    def clear(i, c):
        at = pl.ds(pl.multiple_of(i * 256, 256), 256)
        dk_acc[at, :] = jnp.zeros((256, width), F32)
        dv_acc[at, :] = jnp.zeros((256, width), F32)
        return c

    lax.fori_loop(0, kbuf.shape[0] // 256, clear, 0)
    for k, part in enumerate(parts):
        spot = pl.multiple_of(lax.rem(meta[1] - k + spans, spans) * block, block)
        g_ref[pl.ds(spot, block), :] = part[...]
    pltpu.make_async_copy(kbuf, kbuf, sems.at[0]).wait()
    pltpu.make_async_copy(vbuf, vbuf, sems.at[1]).wait()
    heads = [slice(head * HD, (head + 1) * HD) for head in range(width // HD)]

    def query_tile(t, carry):
        base = pl.multiple_of(t * qt, qt)
        first = me * tok + base
        queries = first + lax.broadcasted_iota(I32, (1, qt), 1)
        starts = doc_start(meta, queries, docs)
        here = pl.ds(base, qt)
        deltas = []
        for cols in heads:
            product = g_ref[here, cols].astype(F32) * wide_ref[here, cols]
            deltas.append(jnp.sum(jnp.transpose(product), axis=0, keepdims=True))
        acc[...] = jnp.zeros_like(acc)

        def visit(spots, rows, state, masked):
            seen = seen_rows(spots[0], rows, table, starts, queries) if masked else None
            for head, cols in enumerate(heads):
                q, grad = q_ref[here, cols], g_ref[here, cols]
                k = rows_of(kbuf, spots, rows, cols)
                probs = jnp.exp2(mm(k, q, NT) * factor - log_ref[head : head + 1, here])
                if masked:
                    probs = hide(probs, seen, 0.0)
                slopes = probs * (mm(rows_of(vbuf, spots, rows, cols), grad, NT) - deltas[head])
                slopes = slopes.astype(BF)
                d_values = mm(probs.astype(BF), grad, NN)
                d_keys = mm(slopes, q, NN)
                for j, at in enumerate(spots):
                    part = slice(j * rows, (j + 1) * rows)
                    dv_acc[pl.ds(at, rows), cols] += d_values[part]
                    dk_acc[pl.ds(at, rows), cols] += d_keys[part]
                acc[head] += mm(k, slopes, TN)
            return state

        visit_keys(visit, jnp.int32(0), meta, first, qt, kt, docs, picks, blocks)
        for head, cols in enumerate(heads):
            dq_ref[here, cols] = (jnp.transpose(acc[head]) * scale).astype(BF)
        return carry

    lax.fori_loop(0, tok // qt, query_tile, 0)

    depth = stage.shape[1]

    def put(which, m):
        side, at = reduce_place(n, which, m)
        out = outs[which][side].at[at * tok : (at + 1) * tok]
        return pltpu.make_async_copy(stage.at[which, m % depth], out, out_sems.at[which, m % depth])

    for m in range(n):
        at = pl.ds(pl.multiple_of(lax.bitwise_xor(me, m) * tok, tok), tok)
        for which in range(2):
            if m >= depth:
                put(which, m - depth).wait()
            rows = dk_acc[at, :] * scale if which == 0 else dv_acc[at, :]
            stage[which, m % depth] = rows.astype(BF)
            put(which, m).start()
    for m in range(max(n - depth, 0), n):
        for which in range(2):
            put(which, m).wait()


def attend_back(meta, q, grads, wide, logs, keys, values, docs, picks):
    n = len(keys)
    tok, width = q.shape
    qt, kt = 512, 512
    got = pl.pallas_call(
        functools.partial(attend_back_kernel, (n, docs, picks, qt, kt, len(grads))),
        in_specs=[SMEM] + [VMEM] * (3 + len(grads)) + [ANY] * (2 * n),
        out_specs=[VMEM] + [ANY] * 4,
        out_shape=[jax.ShapeDtypeStruct((tok, width), BF)]
        + [jax.ShapeDtypeStruct((n * tok // 2, width), BF)] * 4,
        scratch_shapes=[
            pltpu.VMEM((n * tok, width), BF),
            pltpu.VMEM((n * tok, width), BF),
            pltpu.VMEM((n * tok, width), F32),
            pltpu.VMEM((n * tok, width), F32),
            pltpu.VMEM((tok, width), BF),
            pltpu.VMEM((width // HD, HD, qt), F32),
            pltpu.VMEM((2, 4, tok, width), BF),
            pltpu.SMEM((n * tok // MEMB,), I32),
            pltpu.SMEM((picks,), I32),
            pltpu.SemaphoreType.DMA((2,)),
            pltpu.SemaphoreType.DMA((2, 4)),
        ],
        compiler_params=params(),
        cost_estimate=QUICK,
        name="attend_back",
    )(meta, q, wide, logs, *grads, *keys, *values)
    return got[0], got[1:3], got[3:5]


def mix_kernel(first, meta, x_ref, gain_ref, wo_ref, *refs):
    heads, (mixed_ref, left_ref, right_ref) = refs[:-3], refs[-3:]
    spans, qw = len(heads), heads[0].shape[1]
    mixed = x_ref[...].astype(F32)
    for k, head in enumerate(heads):
        mixed = mixed + mm(head[...], wo_ref[lax.rem(meta[1] - k + spans, spans), first:], NN)
    mixed_ref[...] = mixed
    _, _, normed = norm_rows(mixed, gain_ref[1:2, :])
    normed = normed.astype(BF)
    half = normed.shape[1] // 2
    left_ref[...] = normed[:, :half]
    right_ref[...] = normed[:, half:]


def mix(meta, x, gains, weights, heads):
    block, d = heads[0].shape[0], x.shape[1]
    whole = lambda a: pl.BlockSpec(a.shape, lambda i, meta: (0, 0))
    shape = lambda w, t: jax.ShapeDtypeStruct((block, w), t)
    outs = [shape(d, F32), shape(d // 2, BF), shape(d // 2, BF)]
    return pl.pallas_call(
        functools.partial(mix_kernel, weights.shape[1] - heads[0].shape[1]),
        grid_spec=pltpu.PrefetchScalarGridSpec(
            num_scalar_prefetch=1,
            grid=(1,),
            in_specs=[pl.BlockSpec((block, d), lambda i, meta: (meta[1], 0)), whole(gains), VMEM]
            + [whole(h) for h in heads],
            out_specs=[whole(o) for o in outs],
        ),
        out_shape=outs,
        compiler_params=params(),
        cost_estimate=QUICK,
        name="mix",
    )(meta, x, gains, weights, *heads)


def feed_kernel(cfg, meta, w_ref, g_ref, *refs):
    n, spans, fs = cfg
    pieces = refs[: 2 * n]
    normed_ref, hidden_ref, inner_ref = refs[2 * n : 2 * n + 3]
    backs = (refs[2 * n + 3 : 2 * n + 5], refs[2 * n + 5 : 2 * n + 7])
    feeds = refs[2 * n + 7 : 2 * n + 9]
    rows, stage, feed, w, sem, out_sem = refs[2 * n + 9 :]
    step, units = pl.program_id(0), spans * fs
    block, d = rows.shape[1:]
    tile, half = g_ref.shape[0], d // 2
    per = tile // block

    @pl.when(step == 0)
    def _():
        for m in range(n):
            spot = gather_place(n, m)
            pltpu.make_async_copy(pieces[m], rows.at[spot, :, :half], sem.at[spot // per]).start()
            pltpu.make_async_copy(pieces[n + m], rows.at[spot, :, half:], sem.at[spot // per]).start()
        for t in range(spans):
            for kind, first in enumerate((0, units, 2 * units)):
                w[first + t * fs : first + (t + 1) * fs] = w_ref[t, kind * fs : (kind + 1) * fs]

    these = pl.ds(step * per, per)
    pltpu.make_async_copy(rows.at[these], rows.at[these], sem.at[step]).wait()
    normed = rows[these].reshape(tile, d)
    normed_ref[...] = normed
    inner = mm(normed, w[: 2 * units], NT)
    gate, up = inner[:, :units], inner[:, units:]
    sigma = jax.nn.sigmoid(gate)
    silu = gate * sigma
    hidden = (silu * up).astype(BF)
    hidden_ref[...] = hidden
    d_hidden = mm(g_ref[...], w[2 * units :], NT).astype(BF).astype(F32)
    d_gate = (d_hidden * up * (sigma * (1.0 + gate * (1.0 - sigma)))).astype(BF)
    d_inner = jnp.concatenate([d_gate, (d_hidden * silu).astype(BF)], axis=1)
    inner_ref[...] = d_inner
    stage[these] = mm(d_inner, w[: 2 * units], NN).astype(BF).reshape(per, block, d)
    feed[these] = mm(hidden, w[2 * units :], NN).astype(BF).reshape(per, block, d)
    for part in range(per):
        at = step * per + part
        for m in range(n):

            @pl.when(at == gather_place(n, m))
            def _(at=at, m=m):
                for route, cols in enumerate((slice(0, half), slice(half, d))):
                    side, spot = reduce_place(n, route, m)
                    there = backs[route][side].at[spot * block : (spot + 1) * block]
                    pltpu.make_async_copy(stage.at[at, :, cols], there, out_sem).start()
                side, spot = reduce_place(n, 0, m)
                there = feeds[side].at[spot * block : (spot + 1) * block]
                pltpu.make_async_copy(feed.at[at], there, out_sem).start()

    @pl.when(step == pl.num_programs(0) - 1)
    def _():
        pltpu.make_async_copy(stage, stage, out_sem).wait()
        pltpu.make_async_copy(feed, feed, out_sem).wait()


def feed_forward(meta, weights, grads, pieces, fs):
    n = len(pieces) // 2
    rows, d = grads.shape
    block = rows // n
    spans = weights.shape[0]
    units = spans * fs
    tile = min(512, rows)
    turned = lambda w: pl.BlockSpec((tile, w), lambda i, meta: (i, 0))
    shape = lambda w: jax.ShapeDtypeStruct((rows, w), BF)
    got = pl.pallas_call(
        functools.partial(feed_kernel, (n, spans, fs)),
        grid_spec=pltpu.PrefetchScalarGridSpec(
            num_scalar_prefetch=1,
            grid=(rows // tile,),
            in_specs=[VMEM, turned(d)] + [ANY] * (2 * n),
            out_specs=[turned(d), turned(units), turned(2 * units)] + [ANY] * 6,
            scratch_shapes=[
                pltpu.VMEM((n, block, d), BF),
                pltpu.VMEM((n, block, d), BF),
                pltpu.VMEM((n, block, d), BF),
                pltpu.VMEM((3 * units, d), BF),
                pltpu.SemaphoreType.DMA((rows // tile,)),
                pltpu.SemaphoreType.DMA,
            ],
        ),
        out_shape=[shape(d), shape(units), shape(2 * units)]
        + [jax.ShapeDtypeStruct((rows // 2, d // 2), BF)] * 4
        + [jax.ShapeDtypeStruct((rows // 2, d), BF)] * 2,
        compiler_params=params(),
        cost_estimate=QUICK,
        name="feed_forward",
    )(meta, weights, grads, *pieces)
    return got[:3], (got[3:5], got[5:7]), got[7:]


def branch_kernel(cfg, meta, left_a, left_b, right_a, right_b, mixed_ref, g_ref, gain_ref, wo_ref, *refs):
    first, n, spans = cfg
    heads, (mixed_out, gain_out), parts = refs[:spans], refs[spans : spans + 2], refs[spans + 2 : 2 * spans + 2]
    sides, (outer, sem) = refs[2 * spans + 2 : 2 * spans + 4], refs[2 * spans + 4 :]
    qw, out_rows = parts[0].shape[1], outer.shape[1] // n
    total = lambda a, b: a[...].astype(F32) + b[...].astype(F32)
    grad = jnp.concatenate([total(left_a, left_b), total(right_a, right_b)], axis=1)
    gain = gain_ref[1:2, :]
    unit, inverse, _ = norm_rows(mixed_ref[...], gain)
    gain_out[...] = jnp.sum(grad * unit, axis=0, keepdims=True)
    d_mixed = g_ref[...].astype(F32) + norm_back(grad, unit, inverse, gain)
    mixed_out[...] = d_mixed
    branch = d_mixed.astype(BF)
    for k, part in enumerate(parts):
        part[...] = mm(branch, wo_ref[lax.rem(meta[1] + k, spans), first:], NT).astype(BF)
    for k in range(spans):
        if outer.shape[1] > qw:
            outer[k, qw:] = jnp.zeros((outer.shape[1] - qw, outer.shape[2]), BF)
        outer[k, :qw] = mm(heads[(spans - k) % spans][...], branch, TN).astype(BF)
        spread(meta, outer.at[k], sides, n, 0, out_rows, sem, k * out_rows, spans * out_rows)
    pltpu.make_async_copy(outer, outer, sem).wait()


def branch_back(meta, pairs, mixed, grads, gains, weights, heads, n, first):
    block, d = mixed.shape
    spans, qw = weights.shape[0], weights.shape[1] - first
    out_rows = share_rows(qw, n)
    whole = lambda a: pl.BlockSpec(a.shape, lambda i, meta: (0, 0))
    terms = [*pairs[0], *pairs[1]]
    shape = jax.ShapeDtypeStruct
    outs = [shape((block, d), F32), shape((1, d), F32)] + [shape((block, qw), BF)] * spans
    got = pl.pallas_call(
        functools.partial(branch_kernel, (first, n, spans)),
        grid_spec=pltpu.PrefetchScalarGridSpec(
            num_scalar_prefetch=1,
            grid=(1,),
            in_specs=[whole(t) for t in terms]
            + [whole(mixed), pl.BlockSpec((block, d), lambda i, meta: (meta[1], 0)), whole(gains), VMEM]
            + [whole(h) for h in heads],
            out_specs=[whole(o) for o in outs] + [ANY] * 2,
            scratch_shapes=[pltpu.VMEM((spans, n * out_rows, d), BF), pltpu.SemaphoreType.DMA],
        ),
        out_shape=outs + [shape((n // 2 * spans * out_rows, d), BF)] * 2,
        compiler_params=params(),
        cost_estimate=QUICK,
        name="branch_back",
    )(meta, *terms, mixed, grads, gains, weights, *heads)
    return got[0], got[1], got[2 : 2 + spans], got[2 + spans :]


def place_kernel(n, meta, *refs):
    pieces, out = refs[:n], refs[n]
    rows = out.shape[0] // n
    for k, piece in enumerate(pieces):
        block = lax.rem(meta[1] - k + n, n)
        out[pl.ds(pl.multiple_of(block * rows, rows), rows), :] = piece[:rows, :].astype(out.dtype)


def place(meta, pieces, rows, kind=BF):
    n, d = len(pieces), pieces[0].shape[1]
    return pl.pallas_call(
        functools.partial(place_kernel, n),
        in_specs=[SMEM] + [VMEM] * n,
        out_specs=VMEM,
        out_shape=jax.ShapeDtypeStruct((n * rows, d), kind),
        compiler_params=params(),
        cost_estimate=QUICK,
        name="place",
    )(meta, *pieces)


def norm_back(grad_normed, unit_rows, inverse, gain_row):
    scaled = grad_normed * gain_row
    return inverse * (scaled - unit_rows * jnp.mean(scaled * unit_rows, axis=-1, keepdims=True))


def feed_grads_kernel(cfg, hidden, d_inner, normed, grads, out):
    spans, fs = cfg
    units = spans * fs
    pairs = [(d_inner.at[:, :units], normed), (d_inner.at[:, units:], normed), (hidden, grads)]
    for kind, (left, right) in enumerate(pairs):
        product = mm(left[...], right[...], TN).astype(BF)
        for t in range(spans):
            out[t, kind * fs : (kind + 1) * fs] = product[t * fs : (t + 1) * fs]


def feed_grads(hidden, d_inner, normed, grads, fs):
    (rows, units), d = hidden.shape, normed.shape[1]
    return pl.pallas_call(
        functools.partial(feed_grads_kernel, (units // fs, fs)),
        in_specs=[VMEM] * 4,
        out_specs=VMEM,
        out_shape=jax.ShapeDtypeStruct((units // fs, 3 * fs, d), BF),
        compiler_params=params(),
        cost_estimate=QUICK,
        name="feed_grads",
    )(hidden, d_inner, normed, grads)


def share_rows(rows, n):
    return -(-rows // (16 * n)) * 16


def spread(meta, stage, sides, n, route, rows, sem, base=0, total=None):
    for m in range(n):
        at = pl.ds(pl.multiple_of(lax.bitwise_xor(meta[0], m) * rows, rows), rows)
        side, spot = reduce_place(n, route, m)
        first = spot * (total or rows) + base
        pltpu.make_async_copy(stage.at[at], sides[side].at[first : first + rows], sem).start()


def both(pair):
    return (pair[0][...].astype(F32) + pair[1][...].astype(F32)).astype(BF)


def late_kernel(cfg, meta, dq, dk_a, dk_b, dv_a, dv_b, normed, *refs):
    n, qw = cfg
    sides, (stage, sem) = refs[:2], refs[2:]
    used = 3 * qw
    if stage.shape[0] > used:
        stage[used:] = jnp.zeros((stage.shape[0] - used, stage.shape[1]), BF)
    for at, left in enumerate((dq[...], both((dk_a, dk_b)), both((dv_a, dv_b)))):
        stage[at * qw : (at + 1) * qw] = mm(left, normed[...], TN).astype(BF)
    spread(meta, stage, sides, n, 0, stage.shape[0] // n, sem)
    pltpu.make_async_copy(stage, stage, sem).wait()


def late_grads(meta, dq, dk, dv, normed, n):
    (tok, qw), d = dq.shape, normed.shape[1]
    rows = share_rows(3 * qw, n)
    return pl.pallas_call(
        functools.partial(late_kernel, (n, qw)),
        in_specs=[SMEM] + [VMEM] * 6,
        out_specs=[ANY] * 2,
        out_shape=[jax.ShapeDtypeStruct((n * rows // 2, d), BF)] * 2,
        scratch_shapes=[pltpu.VMEM((n * rows, d), BF), pltpu.SemaphoreType.DMA],
        compiler_params=params(),
        cost_estimate=QUICK,
        name="late_grads",
    )(meta, dq, *dk, *dv, normed)


def soap_kernel(cfg, meta, held, early, late, weight_ref, first_ref, second_ref, average_ref, stat_ref, basis_ref,
                weight_out, first_out, second_out, average_out, stat_out, turned_out, grads, wide, sem):
    n, late_panels, out_panels, pf, cap, rows, out_rows, group = cfg
    slots, panel, width = weight_ref.shape
    me, step = meta[0], pl.program_id(0)
    inner_panels = late_panels - out_panels

    def fetch(slot, source, share, base):
        grain = min(share, panel)
        for part in range(panel // grain):
            row = source * panel + part * grain
            at = gather_place(n, lax.bitwise_xor(me, row // share)) * (rows + out_rows) + base + row % share
            there = grads.at[slot, part * grain : (part + 1) * grain]
            pltpu.make_async_copy(late.at[pl.ds(pl.multiple_of(at, grain), grain)], there, sem).start()

    @pl.when(step == 0)
    def _():
        for slot in range(slots):
            source = held[slot]

            @pl.when(source < 0)
            def _(slot=slot):
                grads[slot] = jnp.zeros((panel, grads.shape[2]), BF)

            @pl.when((source >= 0) & (source < inner_panels))
            def _(slot=slot, source=source):
                fetch(slot, source, rows, 0)

            @pl.when((source >= inner_panels) & (source < late_panels))
            def _(slot=slot, source=source):
                fetch(slot, source - inner_panels, out_rows, rows)

            @pl.when(source >= late_panels)
            def _(slot=slot, source=source):
                kind, unit = (source - late_panels) // pf, (source - late_panels) % pf
                spot = (unit // cap) * 3 * cap + kind * cap + unit % cap
                pltpu.make_async_copy(early.at[spot], grads.at[slot], sem).start()

        for slot in range(slots):

            @pl.when(held[slot] >= 0)
            def _(slot=slot):
                pltpu.make_async_copy(grads.at[slot], grads.at[slot], sem).wait()

    high = functools.partial(lax.dot_general, precision=HIGH, preferred_element_type=F32)
    cols = pl.ds(pl.multiple_of(step * width, width), width)

    def parts(value):
        top = value.astype(BF)
        return top, (value - top.astype(F32)).astype(BF)

    for low in range(0, slots, group):
        count = min(group, slots - low)
        size = count * panel
        slot_range = slice(low, low + count)
        diagonal = wide.at[low // group]

        @pl.when(step == 0)
        def _(low=low, count=count, diagonal=diagonal):
            diagonal[...] = jnp.zeros_like(diagonal)
            for j in range(count):
                at = slice(j * panel, (j + 1) * panel)
                diagonal[at, at] = basis_ref[low + j]
                stat_out[low + j] = BETA_TWO * stat_ref[low + j]

        grad = grads[slot_range, :, cols].reshape(size, width)
        square = mm(grad, grad, NT)
        for j in range(count):
            at = slice(j * panel, (j + 1) * panel)
            stat_out[low + j] += (1.0 - BETA_TWO) * square[at, at]
        top, rest = parts(diagonal[:size, :size])
        flat = lambda ref, slot_range=slot_range, size=size: ref[slot_range].reshape(size, width)
        rotated = mm(top, grad, TN) + mm(rest, grad, TN)
        first = BETA_ONE * flat(first_ref) + (1.0 - BETA_ONE) * rotated
        second = BETA_TWO * flat(second_ref) + (1.0 - BETA_TWO) * rotated * rotated
        direction = (first / (1.0 - BETA_ONE**STEP)) / (
            jnp.sqrt(second / (1.0 - BETA_TWO**STEP)) + ADAM_EPSILON
        )
        high_part, low_part = parts(direction)
        update = mm(top, high_part, NN) + (mm(top, low_part, NN) + mm(rest, high_part, NN))
        weight = flat(weight_ref)
        new_weight = weight - RATE * (update + WEIGHT_DECAY * weight)
        average = AVERAGE_DECAY * flat(average_ref) + (1.0 - AVERAGE_DECAY) * new_weight
        shape = (count, panel, width)
        first_out[slot_range] = first.reshape(shape)
        second_out[slot_range] = second.reshape(shape)
        weight_out[slot_range] = new_weight.reshape(shape)
        average_out[slot_range] = average.reshape(shape)

        @pl.when(step == pl.num_programs(0) - 1)
        def _(low=low, count=count):
            for j in range(count):
                turned_out[low + j] = high(stat_out[low + j], basis_ref[low + j], NN)


def soap(meta, held, early, late, n, weight, first, second, average, stat, basis, late_panels, out_panels, pf, cap, rows):
    slots, panel, d = weight.shape
    width, group = 256, 8
    out_rows = late.shape[0] // n - rows
    big = pl.BlockSpec((slots, panel, width), lambda i, meta, held: (0, 0, i))
    small = pl.BlockSpec((slots, panel, panel), lambda i, meta, held: (0, 0, 0))
    shape = jax.ShapeDtypeStruct
    return pl.pallas_call(
        functools.partial(soap_kernel, (n, late_panels, out_panels, pf, cap, rows, out_rows, group)),
        grid_spec=pltpu.PrefetchScalarGridSpec(
            num_scalar_prefetch=2,
            grid=(d // width,),
            in_specs=[ANY] * 2 + [big] * 4 + [small] * 2,
            out_specs=[big] * 4 + [small] * 2,
            scratch_shapes=[
                pltpu.VMEM((slots, panel, d), BF),
                pltpu.VMEM((-(-slots // group), group * panel, group * panel), F32),
                pltpu.SemaphoreType.DMA,
            ],
        ),
        out_shape=[shape((slots, panel, d), F32)] * 4 + [shape((slots, panel, panel), F32)] * 2,
        compiler_params=params(),
        cost_estimate=QUICK,
        name="soap",
    )(meta, held, early, late, weight, first, second, average, stat, basis)


def orthonormal_kernel(columns_ref, out_ref):
    size = columns_ref.shape[0]
    out_ref[...] = columns_ref[...]
    for i in range(size):
        vector = out_ref[i]
        vector = vector * lax.rsqrt(jnp.sum(vector * vector, axis=0, keepdims=True))
        out_ref[i] = vector
        if i < size - 1:
            rest = out_ref[i + 1 :]
            out_ref[i + 1 :] = rest - jnp.sum(rest * vector[None], axis=1, keepdims=True) * vector[None]


def orthonormal(matrix):
    columns = jnp.transpose(matrix, (2, 1, 0))
    found = pl.pallas_call(
        orthonormal_kernel,
        in_specs=[VMEM],
        out_specs=VMEM,
        out_shape=jax.ShapeDtypeStruct(columns.shape, F32),
        compiler_params=params(),
        name="orthonormal",
    )(columns)
    return jnp.transpose(found, (2, 1, 0))


def adam_gain(gradient, weight, first_state, second):
    new_first = BETA_ONE * first_state + (1.0 - BETA_ONE) * gradient
    new_second = BETA_TWO * second + (1.0 - BETA_TWO) * gradient * gradient
    direction = (
        new_first
        / (1.0 - BETA_ONE**STEP)
        / (jnp.sqrt(new_second / (1.0 - BETA_TWO**STEP)) + ADAM_EPSILON)
    )
    return (weight - GAIN_RATE * direction, new_first, new_second)


def back_kernel(meta, x_ref, dq, dk_a, dk_b, dv_a, dv_b, wq, wk, wv, out, gain_out):
    total = mm(dq[...], wq[...], NN) + mm(both((dk_a, dk_b)), wk[...], NN)
    total = total + mm(both((dv_a, dv_b)), wv[...], NN)
    out[...] = total.astype(BF)
    unit, _, _ = norm_rows(x_ref[...].astype(F32), 1.0)
    share = jnp.sum(total * unit, axis=0, keepdims=True)

    @pl.when(pl.program_id(0) == 0)
    def _():
        gain_out[...] = share

    @pl.when(pl.program_id(0) > 0)
    def _():
        gain_out[...] += share


def back_in(meta, x, dq, dk, dv, wq, wk, wv, n, low, high):
    tok, (qw, d) = dq.shape[0], wq.shape
    tile = tok // n
    rows = lambda w: pl.BlockSpec((tile, w), lambda i, meta: ((meta[1] - i - low + n) % n, 0))
    whole = pl.BlockSpec((qw, d), lambda i, meta: (0, 0))
    return pl.pallas_call(
        back_kernel,
        grid_spec=pltpu.PrefetchScalarGridSpec(
            num_scalar_prefetch=1,
            grid=(high - low,),
            in_specs=[rows(d)] + [rows(qw)] * 5 + [whole] * 3,
            out_specs=[pl.BlockSpec((tile, d), lambda i, meta: (i, 0)), pl.BlockSpec((1, d), lambda i, meta: (0, 0))],
        ),
        out_shape=[jax.ShapeDtypeStruct(((high - low) * tile, d), BF), jax.ShapeDtypeStruct((1, d), F32)],
        compiler_params=params(),
        cost_estimate=QUICK,
        name="back_in",
    )(meta, x, dq, *dk, *dv, wq, wk, wv)


def shards(
    tokens,
    cotangent,
    lengths,
    retrieve,
    owners,
    masters,
    first_moment,
    second_moment,
    averaged,
    statistics,
    bases,
    gains,
    gain_first,
    gain_second,
):
    tok, d = tokens.shape
    n_seq, n_tp = lax.axis_size("seq"), lax.axis_size("tp")
    me, z = lax.axis_index("seq"), lax.axis_index("tp")
    qw, ff = H // n_tp * HD, FF // n_tp
    slots_dev, panel = masters.shape[1:3]
    split = (slots_dev + 1) // 2
    docs, picks = lengths.shape[0], retrieve.shape[1]
    recalled = lax.dynamic_index_in_dim(retrieve, me, 0, keepdims=False)
    meta = jnp.concatenate([jnp.stack([me, z]).astype(I32), lengths, recalled])
    block = tok // n_tp
    pq, pf = qw // panel, ff // panel
    cap = -(-pf // n_seq)
    fs = cap * panel
    slot_ids = me * slots_dev + jnp.arange(slots_dev, dtype=I32)
    panel_ids = jnp.arange(1, owners.shape[0] + 1, dtype=I32)
    held = jnp.sum(jnp.where(slot_ids[:, None] == owners[None, :], panel_ids[None, :], 0), axis=1) - 1

    def mine(rows):
        return lax.dynamic_slice_in_dim(rows, z * block, block, 0)

    def whole_tp(rows):
        return lax.all_gather(rows, "tp", axis=0, tiled=True)

    def whole_seq(rows):
        return lax.all_gather(rows, "seq", axis=0, tiled=True)

    own = masters[0].astype(BF)
    pieces, _ = gather_seq([own[:split], own[split:]], n_seq)
    pieces = list(zip(*pieces, strict=True))
    q, k, v, normed_one, inner, share = project_in(
        meta, owners, tokens, gains, pieces, pq, pf, cap, slots_dev, split
    )
    (keys, values), _ = gather_seq([k, v], n_seq)
    weights = whole_tp(share).reshape(n_tp, -1, d)
    own_grads, keys[n_seq - 2], values[n_seq - 2] = pin(mine(cotangent), keys[n_seq - 2], values[n_seq - 2])
    grads_all = direct_pieces(own_grads, n_seq)
    turned_heads, wide, logs = attend(meta, q, keys, values, docs, picks, block)
    turned_heads, grads_all = pin(turned_heads, grads_all)
    heads = trade_tp([turned_heads[i * block : (i + 1) * block] for i in range(n_tp)], n_tp)
    mixed, left, right = mix(meta, tokens, gains, weights, heads)
    left, grads_all = pin(left, grads_all)
    grads_all = core_gather(jnp.concatenate(grads_all, axis=0), n_seq)
    (left, right), _ = gather_seq([left, right], n_seq)
    (normed_two, hidden, d_inner), pairs, feed = feed_forward(meta, weights, grads_all, left + right, fs)

    last = len(routes(n_seq)[0])
    inner_rows, out_rows = share_rows(3 * qw, n_seq), share_rows(qw, n_seq)
    feed_sums_in = (hidden, d_inner, normed_two, grads_all)
    for at in range(last + 1):
        pairs = reduce_levels(pairs, n_seq, at)
        if at == last - 1:
            pairs, feed, feed_sums = pin(pairs, (feed[0], swap(feed[1], n_seq, 1)), feed_sums)
            feed = plus(*feed)
        elif at == 0:
            pairs, feed, feed_sums_in = pin(pairs, feed, feed_sums_in)
            feed_sums = feed_grads(*feed_sums_in, fs)
    d_mixed, grad_gain_two, d_heads, outer = branch_back(
        meta, pairs, mixed, cotangent, gains, weights, heads, n_seq, 3 * fs
    )
    d_heads = trade_tp(d_heads, n_tp)
    outer = plus(outer[0], swap(outer[1], n_seq, 1))

    size = n_tp * out_rows
    parts = {}
    for m in range(0, n_seq, 2):
        at = reduce_place(n_seq, 0, m)[1]
        parts[m] = jnp.concatenate([feed[at * block : (at + 1) * block], outer[at * size : (at + 1) * size]], axis=0)
    d_heads, parts, feed_sums = pin(d_heads, parts, feed_sums)
    parts = [swap(part, n_seq, m) if m else part for m, part in parts.items()]
    feed_sums = lax.psum_scatter(feed_sums.reshape(-1, d), "tp", scatter_dimension=0, tiled=True)
    dq, *pairs = attend_back(meta, q, d_heads, wide, logs, keys, values, docs, picks)
    parts, dq, pairs = pin(parts, dq, pairs)
    pairs = reduce_levels(pairs, n_seq, 0)
    total = sum(part.astype(F32) for part in parts)
    output = (mixed + total[:block]).astype(BF)
    outer = [total[block + k * out_rows : block + (k + 1) * out_rows].astype(BF) for k in range(n_tp)]
    outputs = [output]
    for at in range(last + 1):
        if at:
            pairs = reduce_levels(pairs, n_seq, at)
            while len(outputs) < n_tp and (at == last or len(outputs) < 1 + 2 * at):
                outputs.append(ring(outputs[-1], n_tp, 1))
        pairs, outputs, feed_sums, dq = pin(pairs, outputs, feed_sums, dq)
    dk, dv = pairs
    output = place(meta, outputs, block)
    early = whole_seq(feed_sums).reshape(-1, panel, d)

    inputs = (meta, tokens, dq, dk, dv, inner[0], inner[1], inner[2], n_tp)
    total, gain_a = back_in(*inputs, n_tp - 1, n_tp)
    total, lefts = pin(total, (dq, dk, dv))
    back_rest, gain_b = back_in(meta, tokens, *lefts, *inputs[5:], 0, n_tp - 1)
    gain_total = jnp.concatenate([gain_a + gain_b, grad_gain_two], axis=0)
    late = late_grads(meta, *lefts, normed_one, n_seq)

    def advance(late, step):
        if step == 1:
            late = plus(late[0], swap(late[1], n_seq, 1))
        elif step == 2:
            parts = direct_reduce(late, n_seq, inner_rows)
            late = sum(part.astype(F32) for part in parts).astype(BF)
            late = jnp.concatenate([late, outer], axis=0)
        elif step == 3:
            late = direct_gather(late, n_seq)
        elif step == 4:
            late = core_gather(late, n_seq)
        return late

    steps = max(2 * (n_tp - 1), 6)
    gain_steps = sum_steps(n_seq, n_tp)
    gather = []
    for step in range(steps):
        if step < n_tp - 1:
            k = n_tp - 2 - step
            came = ring(total, n_tp, -1)
            late = advance(late, step)
            if step == 0:
                outer = trade_tp(outer, n_tp)
            if step == 1:
                came, output = pin(came, output)
            for _ in range(min(len(gain_steps), 2 if 0 < step else 0)):
                gain_total = gain_steps.pop(0)(gain_total)
            came, late, back_rest, outer, held, gain_total = pin(came, late, back_rest, outer, held, gain_total)
            if step == 0:
                outer = sum(part.astype(F32) for part in outer).astype(BF)
            part = back_rest[k * block : (k + 1) * block]
            if k:
                total = plus(part, came)
                total, late, gain_total = pin(total, late, gain_total)
                continue
            d_normed_one = part.astype(F32) + came.astype(F32)
            unit_one, inverse_one, _ = norm_rows(mine(tokens).astype(F32), gains[0])
            grad_here = d_mixed + norm_back(d_normed_one, unit_one, inverse_one, gains[0])
            gather.append(grad_here.astype(BF))
            continue
        if len(gather) < n_tp:
            gather.append(ring(gather[-1], n_tp, 1))
        for _ in range(min(len(gain_steps), 1)):
            gain_total = gain_steps.pop(0)(gain_total)
        late = advance(late, step)
        if step == steps - 2:
            new_weight, new_first, new_second, new_average, new_stat, turned_basis = soap(
                meta, held, early, late, n_seq, masters[0], first_moment[0], second_moment[0], averaged[0],
                statistics[0], bases[0], 4 * pq, pq, pf, cap, inner_rows,
            )
            gather[-1], turned_basis, gain_total = pin(gather[-1], turned_basis, gain_total)
        elif step == steps - 1:
            new_basis = orthonormal(turned_basis)
            gather, new_basis, gain_total = pin(gather, new_basis, gain_total)
        else:
            gather[-1], late, gain_total = pin(gather[-1], late, gain_total)
    for step in gain_steps:
        gain_total = step(gain_total)
    grad_input = place(meta, gather, block, F32)
    new_gains, new_gain_first, new_gain_second = adam_gain(gain_total, gains, gain_first, gain_second)
    return (
        output,
        grad_input,
        new_weight[None],
        new_first[None],
        new_second[None],
        new_average[None],
        new_stat[None],
        new_basis[None],
        new_gains,
        new_gain_first,
        new_gain_second,
    )


def solution(mesh):
    by_token, by_slot = P("seq", None), P("tp", "seq", None, None)
    in_specs = (by_token, by_token, P(), P(), P()) + (by_slot,) * 6 + (P(),) * 3
    out_specs = (by_token, by_token) + (by_slot,) * 6 + (P(),) * 3
    return jax.shard_map(shards, mesh=mesh, in_specs=in_specs, out_specs=out_specs, check_vma=False)
```

```python
import functools

import jax
import jax.numpy as jnp
from jax import lax
from jax.experimental import pallas as pl
from jax.experimental.pallas import tpu as pltpu
from jax.sharding import PartitionSpec as P

H = 8
HD = 128
FF = 2816
MEMB = 128
STEP = 10

EPSILON = 1e-06
RATE = 0.02
GAIN_RATE = 0.5
BETA_ONE = 0.9
BETA_TWO = 0.95
ADAM_EPSILON = 1e-08
WEIGHT_DECAY = 0.01
AVERAGE_DECAY = 0.8
NEGATIVE = -1e30
START_TOP = -1e29
LOG2E = 1.4426950408889634

BF = jnp.bfloat16
F32 = jnp.float32
I32 = jnp.int32
HIGH = lax.Precision.HIGHEST
ANY = pl.BlockSpec(memory_space=pl.ANY)
SMEM = pl.BlockSpec(memory_space=pltpu.SMEM)
VMEM = pl.BlockSpec(memory_space=pltpu.VMEM)
VMEM_BYTES = 58 * 2**20

NT = (((1,), (1,)), ((), ()))
NN = (((1,), (0,)), ((), ()))
TN = (((0,), (0,)), ((), ()))


def mm(left, right, dims):
    return lax.dot_general(left, right, dims, preferred_element_type=F32)


QUICK = pl.CostEstimate(flops=1000, bytes_accessed=1000, transcendentals=0)


def params(**more):
    return pltpu.CompilerParams(vmem_limit_bytes=VMEM_BYTES, **more)


def pin(*values):
    return lax.optimization_barrier(values)


def routes(count):
    bits = []
    bit = 2
    while bit < count:
        bits.append(bit)
        bit *= 2
    return bits, bits[::-1]


def swap(value, count, bit):
    return lax.ppermute(value, "seq", [(i, i ^ bit) for i in range(count)])


def gather_seq(owns, count, beside=None):
    orders = routes(count)
    held = [{0: own} for own in owns]
    hops = len(orders[0])
    for stage in range(hops + 1):
        for i, pieces in enumerate(held):
            order = orders[i % 2]
            come = {}
            for m, piece in pieces.items():
                if m & 1 or bin(m).count("1") != stage:
                    continue
                for bit in order:
                    if all(other == bit or not m & other for other in order[order.index(bit) :]) and not m & bit:
                        come[m | bit] = swap(piece, count, bit)
                come[m | 1] = swap(piece, count, 1)
            pieces.update(come)
        if stage < hops:
            held, beside = pin(held, beside)
    return [[pieces[m] for m in range(count)] for pieces in held], beside


def plus(left, right):
    return (left.astype(F32) + right.astype(F32)).astype(left.dtype)


def reduce_bits(count, route):
    return [1, *routes(count)[route][::-1]]


def reduce_place(count, route, m):
    bits = reduce_bits(count, route)
    block = 0
    for bit in bits[1:]:
        block = 2 * block + bool(m & bit)
    return int(bool(m & bits[0])), block


def reduce_level(pair, count, route, at):
    keep, send = pair
    bits = reduce_bits(count, route)
    came = swap(send, count, bits[at])
    if at == len(bits) - 1:
        return keep, came
    half = keep.shape[0] // 2
    return plus(keep[:half], came[:half]), plus(keep[half:], came[half:])


def reduce_levels(pairs, count, at):
    return [reduce_level(pair, count, i % 2, at) for i, pair in enumerate(pairs)]


def direct_reduce(rows, count, sizes):
    parts = []
    for m in range(0, count, 2):
        at = reduce_place(count, 0, m)[1]
        part = rows[at * sizes : (at + 1) * sizes]
        parts.append(swap(part, count, m) if m else part)
    return parts


def direct_pieces(rows, count):
    return [swap(rows, count, m) if m else rows for m in range(0, count, 2)]


def direct_gather(rows, count):
    return jnp.concatenate(direct_pieces(rows, count), axis=0)


def core_gather(rows, count):
    return jnp.concatenate([rows, swap(rows, count, 1)], axis=0)


def gather_place(count, distance):
    return distance // 2 + (count // 2) * (distance % 2)


def ring(value, count, step):
    return lax.ppermute(value, "tp", [(i, (i + step) % count) for i in range(count)])


def trade_tp(parts, count):
    return [parts[0]] + [ring(parts[k], count, k) for k in range(1, count)]


def gather_tp(own, count):
    pieces = [own]
    for _ in range(count - 1):
        pieces.append(ring(pieces[-1], count, 1))
    return pieces


def reduce_tp(parts, count):
    total = parts[count - 1]
    for k in range(count - 2, -1, -1):
        came = ring(total, count, -1)
        if k == 0:
            return parts[0], came
        total = plus(parts[k], came)
    return None


def sum_steps(n_seq, n_tp):
    steps = []
    for axis, count in (("seq", n_seq), ("tp", n_tp)):
        bit = 1
        while bit < count:
            pairs = [(i, i ^ bit) for i in range(count)]
            steps.append(lambda v, axis=axis, pairs=pairs: v + lax.ppermute(v, axis, pairs))
            bit *= 2
    return steps


def panel_copies(owners_ref, me, first, amount, slots_dev, split, pieces, view, sem, back):
    def one(i, carry):
        slot = owners_ref[first + i]
        spot = lax.bitwise_xor(slot // slots_dev, me)
        row = slot % slots_dev
        for m, (low, high) in enumerate(pieces):
            for ref, base, size in ((low, 0, split), (high, split, slots_dev - split)):

                @pl.when((spot == m) & (row >= base) & (row < base + size))
                def _(ref=ref, base=base):
                    there = ref.at[row - base]
                    source, target = (view(i), there) if back else (there, view(i))
                    pltpu.make_async_copy(source, target, sem).start()

        return carry

    lax.fori_loop(0, amount, one, 0)


def norm_rows(rows, gain):
    inverse = lax.rsqrt(jnp.mean(rows * rows, axis=-1, keepdims=True) + EPSILON)
    unit = rows * inverse
    return unit, inverse, unit * gain


def project_kernel(cfg, meta, owners, x_ref, gain_ref, *refs):
    n, pq, pf, cap, slots_dev, split = cfg
    pieces = list(zip(refs[:n], refs[n : 2 * n], strict=True))
    outs = refs[2 * n : 2 * n + 3]
    normed_ref, inner, share, sems = refs[2 * n + 3 :]
    me, panel, d = meta[0], inner.shape[1], x_ref.shape[1]
    mine = jnp.clip(pf - me * cap, 0, cap)

    @pl.when(pl.program_id(0) == 0)
    def _():
        copies = functools.partial(panel_copies, owners, me)
        copies(0, 3 * pq, slots_dev, split, pieces, lambda i: inner.at[i], sems.at[0], False)
        copies(3 * pq, pq, slots_dev, split, pieces, lambda i: share.at[3 * cap + i], sems.at[1], False)
        for kind in range(3):
            for j in range(cap):

                @pl.when(j >= mine)
                def _(at=kind * cap + j):
                    share[at] = jnp.zeros(share.shape[1:], BF)

            copies(
                4 * pq + kind * pf + me * cap, mine, slots_dev, split, pieces,
                lambda i, kind=kind: share.at[kind * cap + i], sems.at[1], False,
            )

    _, _, normed = norm_rows(x_ref[...].astype(F32), gain_ref[0:1, :])
    normed = normed.astype(BF)
    normed_ref[...] = normed

    @pl.when(pl.program_id(0) == 0)
    def _():
        pltpu.make_async_copy(inner, inner, sems.at[0]).wait()

    for at in range(3):
        w = inner[at * pq : (at + 1) * pq].reshape(pq * panel, d)
        outs[at][...] = mm(normed, w, NT).astype(BF)

    @pl.when(pl.program_id(0) == pl.num_programs(0) - 1)
    def _():
        def finish(i, c):
            pltpu.make_async_copy(share.at[0], share.at[0], sems.at[1]).wait()
            return c

        lax.fori_loop(0, 3 * mine + pq, finish, 0)


def project_in(meta, owners, x, gains, pieces, pq, pf, cap, slots_dev, split):
    n = len(pieces)
    tok, d = x.shape
    panel = pieces[0][0].shape[1]
    qw = pq * panel
    tile = 256
    out = lambda w: pl.BlockSpec((tile, w), lambda i: (i, 0))
    whole = lambda count: pl.BlockSpec((count, panel, d), lambda i: (0, 0, 0))
    shape = lambda *dims: jax.ShapeDtypeStruct(dims, BF)
    q, k, v, normed, inner, share = pl.pallas_call(
        functools.partial(project_kernel, (n, pq, pf, cap, slots_dev, split)),
        grid=(tok // tile,),
        in_specs=[SMEM, SMEM, out(d), pl.BlockSpec(gains.shape, lambda i: (0, 0))] + [ANY] * (2 * n),
        out_specs=[out(qw)] * 3 + [out(d), whole(3 * pq), whole(3 * cap + pq)],
        out_shape=[shape(tok, qw)] * 3 + [shape(tok, d), shape(3 * pq, panel, d), shape(3 * cap + pq, panel, d)],
        scratch_shapes=[pltpu.SemaphoreType.DMA((2,))],
        compiler_params=params(),
        cost_estimate=QUICK,
        name="project",
    )(meta, owners, x, gains, *[p[0] for p in pieces], *[p[1] for p in pieces])
    return q, k, v, normed, inner.reshape(3, qw, d), share.reshape(-1, d)


def doc_start(meta, positions, docs):
    start = jnp.int32(0)
    found = jnp.zeros_like(positions)
    for at in range(docs):
        found = jnp.where(positions >= start, start, found)
        start = start + meta[2 + at]
    return found


def load_pieces(me, pieces, buffer, sem, tok):
    for m, piece in enumerate(pieces):
        owner = lax.bitwise_xor(me, m)
        at = pl.multiple_of(owner * tok, tok)
        pltpu.make_async_copy(piece, buffer.at[pl.ds(at, tok)], sem).start()


def member_table(meta, table, docs, picks, blocks):
    def clear(i, c):
        table[i] = 0
        return c

    lax.fori_loop(0, blocks, clear, 0)
    for e in range(picks):
        table[meta[2 + docs + e]] = 1


def memory_list(meta, blocks_ref, docs, picks, limit):
    count = jnp.int32(0)
    for e in range(picks):
        block = meta[2 + docs + e]
        fresh = (block + 1) * MEMB <= limit
        for other in range(e):
            fresh = fresh & (meta[2 + docs + other] != block)

        @pl.when(fresh)
        def _(count=count, block=block):
            blocks_ref[count] = block

        count = count + fresh.astype(I32)
    return count


def seen_rows(at, rows, table, starts, queries):
    row = lax.broadcasted_iota(I32, (MEMB, queries.shape[1]), 0)
    seen = []
    for b in range(rows // MEMB):
        base = at + b * MEMB
        lowest = starts * (1 - table[base // MEMB]) - base
        seen.append((row >= lowest) & (row <= queries - base))
    return seen


def hide(scores, seen, fill):
    kept = [jnp.where(mask, scores[b * MEMB : (b + 1) * MEMB], fill) for b, mask in enumerate(seen)]
    return jnp.concatenate(kept, axis=0)


def rows_of(buffer, spots, rows, cols):
    parts = [buffer[pl.ds(at, rows), cols] for at in spots]
    return parts[0] if len(parts) == 1 else jnp.concatenate(parts, axis=0)


def visit_keys(visit, state, meta, first, qt, kt, docs, picks, blocks):
    low = doc_start(meta, first, docs) // kt
    high = (first + qt - 1) // kt + 1
    clear = jnp.clip((doc_start(meta, first + qt - 1, docs) + kt - 1) // kt, low, high)
    full = jnp.clip(first // kt, clear, high)
    count = memory_list(meta, blocks, docs, picks, low * kt)

    def dense(masked):
        return lambda i, state: visit([pl.multiple_of(i * kt, kt)], kt, state, masked)

    def memory(together, base):
        def go(i, state):
            spots = [pl.multiple_of(blocks[base + i * together + j] * MEMB, MEMB) for j in range(together)]
            return visit(spots, MEMB, state, False)

        return go

    state = lax.fori_loop(low, clear, dense(True), state)
    state = lax.fori_loop(clear, full, dense(False), state)
    state = lax.fori_loop(full, high, dense(True), state)
    state = lax.fori_loop(0, count // 4, memory(4, 0), state)
    return lax.fori_loop(0, count % 4, memory(1, count // 4 * 4), state)


def attend_kernel(cfg, meta, q_ref, *refs):
    n, docs, picks, qt, kt, block = cfg
    keys, values = refs[:n], refs[n : 2 * n]
    turns, refs = refs[2 * n : 2 * n + q_ref.shape[0] // block], refs[2 * n + q_ref.shape[0] // block :]
    wide_ref, log_ref, kbuf, vbuf, acc, table, blocks, sems = refs
    tok, width = q_ref.shape
    me = meta[0]
    factor = HD**-0.5 * LOG2E
    load_pieces(me, keys, kbuf, sems.at[0], tok)
    load_pieces(me, values, vbuf, sems.at[1], tok)
    member_table(meta, table, docs, picks, kbuf.shape[0] // MEMB)
    pltpu.make_async_copy(kbuf, kbuf, sems.at[0]).wait()
    pltpu.make_async_copy(vbuf, vbuf, sems.at[1]).wait()
    heads = [slice(head * HD, (head + 1) * HD) for head in range(width // HD)]
    spans = tok // block

    def query_tile(t, carry):
        base = pl.multiple_of(t * qt, qt)
        first = me * tok + base
        queries = first + lax.broadcasted_iota(I32, (1, qt), 1)
        starts = doc_start(meta, queries, docs)
        acc[...] = jnp.zeros_like(acc)

        def visit(spots, rows, state, masked):
            seen = seen_rows(spots[0], rows, table, starts, queries) if masked else None
            result = []
            for head, cols in enumerate(heads):
                top, total = state[head]
                scores = mm(rows_of(kbuf, spots, rows, cols), q_ref[pl.ds(base, qt), cols], NT)
                if masked:
                    scores = hide(scores, seen, NEGATIVE)
                new_top = jnp.maximum(top, jnp.max(scores, axis=0, keepdims=True))
                fade = jnp.exp2((top - new_top) * factor)
                probs = jnp.exp2((scores - new_top) * factor)
                total = total * fade + jnp.sum(probs, axis=0, keepdims=True)
                product = mm(rows_of(vbuf, spots, rows, cols), probs.astype(BF), TN)
                acc[head] = acc[head] * fade + product
                result.append((new_top, total))
            return tuple(result)

        state = tuple((jnp.full((1, qt), START_TOP, F32), jnp.zeros((1, qt), F32)) for _ in heads)
        state = visit_keys(visit, state, meta, first, qt, kt, docs, picks, blocks)
        for head, cols in enumerate(heads):
            top, total = state[head]
            rows = jnp.transpose(acc[head] * (1.0 / total))
            wide_ref[pl.ds(base, qt), cols] = rows
            rows = rows.astype(BF)
            size = min(block, qt)
            inside = pl.ds(pl.multiple_of(lax.rem(base, block), size), size)
            for part in range(max(qt // block, 1)):
                spot = lax.rem(base // block + part - meta[1] + spans, spans)
                for k, turn in enumerate(turns):

                    @pl.when(spot == k)
                    def _(turn=turn, part=part, rows=rows, cols=cols):
                        turn[inside, cols] = rows[part * size : (part + 1) * size]

            log_ref[head : head + 1, pl.ds(base, qt)] = top * factor + jnp.log2(total)
        return carry

    lax.fori_loop(0, tok // qt, query_tile, 0)


def attend(meta, q, keys, values, docs, picks, block):
    n = len(keys)
    tok, width = q.shape
    qt, kt = 512, 1024
    *turns, wide, logs = pl.pallas_call(
        functools.partial(attend_kernel, (n, docs, picks, qt, kt, block)),
        in_specs=[SMEM, VMEM] + [ANY] * (2 * n),
        out_specs=[VMEM] * (2 + tok // block),
        out_shape=[jax.ShapeDtypeStruct((block, width), BF)] * (tok // block)
        + [
            jax.ShapeDtypeStruct((tok, width), F32),
            jax.ShapeDtypeStruct((width // HD, tok), F32),
        ],
        scratch_shapes=[
            pltpu.VMEM((n * tok, width), BF),
            pltpu.VMEM((n * tok, width), BF),
            pltpu.VMEM((width // HD, HD, qt), F32),
            pltpu.SMEM((n * tok // MEMB,), I32),
            pltpu.SMEM((picks,), I32),
            pltpu.SemaphoreType.DMA((2,)),
        ],
        compiler_params=params(),
        cost_estimate=QUICK,
        name="attend",
    )(meta, q, *keys, *values)
    return turns, wide, logs


def attend_back_kernel(cfg, meta, q_ref, wide_ref, log_ref, *refs):
    n, docs, picks, qt, kt, spans = cfg
    parts, refs = refs[:spans], refs[spans:]
    keys, values = refs[:n], refs[n : 2 * n]
    dq_ref = refs[2 * n]
    outs = (refs[2 * n + 1 : 2 * n + 3], refs[2 * n + 3 : 2 * n + 5])
    kbuf, vbuf, dk_acc, dv_acc, g_ref, acc, stage, table, blocks, sems, out_sems = refs[2 * n + 5 :]
    tok, width = q_ref.shape
    me = meta[0]
    block = tok // spans
    scale = HD**-0.5
    factor = scale * LOG2E
    load_pieces(me, keys, kbuf, sems.at[0], tok)
    load_pieces(me, values, vbuf, sems.at[1], tok)
    member_table(meta, table, docs, picks, kbuf.shape[0] // MEMB)

    def clear(i, c):
        at = pl.ds(pl.multiple_of(i * 256, 256), 256)
        dk_acc[at, :] = jnp.zeros((256, width), F32)
        dv_acc[at, :] = jnp.zeros((256, width), F32)
        return c

    lax.fori_loop(0, kbuf.shape[0] // 256, clear, 0)
    for k, part in enumerate(parts):
        spot = pl.multiple_of(lax.rem(meta[1] - k + spans, spans) * block, block)
        g_ref[pl.ds(spot, block), :] = part[...]
    pltpu.make_async_copy(kbuf, kbuf, sems.at[0]).wait()
    pltpu.make_async_copy(vbuf, vbuf, sems.at[1]).wait()
    heads = [slice(head * HD, (head + 1) * HD) for head in range(width // HD)]

    def query_tile(t, carry):
        base = pl.multiple_of(t * qt, qt)
        first = me * tok + base
        queries = first + lax.broadcasted_iota(I32, (1, qt), 1)
        starts = doc_start(meta, queries, docs)
        here = pl.ds(base, qt)
        deltas = []
        for cols in heads:
            product = g_ref[here, cols].astype(F32) * wide_ref[here, cols]
            deltas.append(jnp.sum(jnp.transpose(product), axis=0, keepdims=True))
        acc[...] = jnp.zeros_like(acc)

        def visit(spots, rows, state, masked):
            seen = seen_rows(spots[0], rows, table, starts, queries) if masked else None
            for head, cols in enumerate(heads):
                q, grad = q_ref[here, cols], g_ref[here, cols]
                k = rows_of(kbuf, spots, rows, cols)
                probs = jnp.exp2(mm(k, q, NT) * factor - log_ref[head : head + 1, here])
                if masked:
                    probs = hide(probs, seen, 0.0)
                slopes = probs * (mm(rows_of(vbuf, spots, rows, cols), grad, NT) - deltas[head])
                slopes = slopes.astype(BF)
                d_values = mm(probs.astype(BF), grad, NN)
                d_keys = mm(slopes, q, NN)
                for j, at in enumerate(spots):
                    part = slice(j * rows, (j + 1) * rows)
                    dv_acc[pl.ds(at, rows), cols] += d_values[part]
                    dk_acc[pl.ds(at, rows), cols] += d_keys[part]
                acc[head] += mm(k, slopes, TN)
            return state

        visit_keys(visit, jnp.int32(0), meta, first, qt, kt, docs, picks, blocks)
        for head, cols in enumerate(heads):
            dq_ref[here, cols] = (jnp.transpose(acc[head]) * scale).astype(BF)
        return carry

    lax.fori_loop(0, tok // qt, query_tile, 0)

    depth = stage.shape[1]

    def put(which, m):
        side, at = reduce_place(n, which, m)
        out = outs[which][side].at[at * tok : (at + 1) * tok]
        return pltpu.make_async_copy(stage.at[which, m % depth], out, out_sems.at[which, m % depth])

    for m in range(n):
        at = pl.ds(pl.multiple_of(lax.bitwise_xor(me, m) * tok, tok), tok)
        for which in range(2):
            if m >= depth:
                put(which, m - depth).wait()
            rows = dk_acc[at, :] * scale if which == 0 else dv_acc[at, :]
            stage[which, m % depth] = rows.astype(BF)
            put(which, m).start()
    for m in range(max(n - depth, 0), n):
        for which in range(2):
            put(which, m).wait()


def attend_back(meta, q, grads, wide, logs, keys, values, docs, picks):
    n = len(keys)
    tok, width = q.shape
    qt, kt = 512, 512
    got = pl.pallas_call(
        functools.partial(attend_back_kernel, (n, docs, picks, qt, kt, len(grads))),
        in_specs=[SMEM] + [VMEM] * (3 + len(grads)) + [ANY] * (2 * n),
        out_specs=[VMEM] + [ANY] * 4,
        out_shape=[jax.ShapeDtypeStruct((tok, width), BF)]
        + [jax.ShapeDtypeStruct((n * tok // 2, width), BF)] * 4,
        scratch_shapes=[
            pltpu.VMEM((n * tok, width), BF),
            pltpu.VMEM((n * tok, width), BF),
            pltpu.VMEM((n * tok, width), F32),
            pltpu.VMEM((n * tok, width), F32),
            pltpu.VMEM((tok, width), BF),
            pltpu.VMEM((width // HD, HD, qt), F32),
            pltpu.VMEM((2, 4, tok, width), BF),
            pltpu.SMEM((n * tok // MEMB,), I32),
            pltpu.SMEM((picks,), I32),
            pltpu.SemaphoreType.DMA((2,)),
            pltpu.SemaphoreType.DMA((2, 4)),
        ],
        compiler_params=params(),
        cost_estimate=QUICK,
        name="attend_back",
    )(meta, q, wide, logs, *grads, *keys, *values)
    return got[0], got[1:3], got[3:5]


def mix_kernel(first, meta, x_ref, gain_ref, wo_ref, *refs):
    heads, (mixed_ref, left_ref, right_ref) = refs[:-3], refs[-3:]
    spans, qw = len(heads), heads[0].shape[1]
    mixed = x_ref[...].astype(F32)
    for k, head in enumerate(heads):
        mixed = mixed + mm(head[...], wo_ref[lax.rem(meta[1] - k + spans, spans), first:], NN)
    mixed_ref[...] = mixed
    _, _, normed = norm_rows(mixed, gain_ref[1:2, :])
    normed = normed.astype(BF)
    half = normed.shape[1] // 2
    left_ref[...] = normed[:, :half]
    right_ref[...] = normed[:, half:]


def mix(meta, x, gains, weights, heads):
    block, d = heads[0].shape[0], x.shape[1]
    whole = lambda a: pl.BlockSpec(a.shape, lambda i, meta: (0, 0))
    shape = lambda w, t: jax.ShapeDtypeStruct((block, w), t)
    outs = [shape(d, F32), shape(d // 2, BF), shape(d // 2, BF)]
    return pl.pallas_call(
        functools.partial(mix_kernel, weights.shape[1] - heads[0].shape[1]),
        grid_spec=pltpu.PrefetchScalarGridSpec(
            num_scalar_prefetch=1,
            grid=(1,),
            in_specs=[pl.BlockSpec((block, d), lambda i, meta: (meta[1], 0)), whole(gains), VMEM]
            + [whole(h) for h in heads],
            out_specs=[whole(o) for o in outs],
        ),
        out_shape=outs,
        compiler_params=params(),
        cost_estimate=QUICK,
        name="mix",
    )(meta, x, gains, weights, *heads)


def feed_kernel(cfg, meta, w_ref, g_ref, *refs):
    n, spans, fs = cfg
    pieces = refs[: 2 * n]
    normed_ref, hidden_ref, inner_ref = refs[2 * n : 2 * n + 3]
    backs = (refs[2 * n + 3 : 2 * n + 5], refs[2 * n + 5 : 2 * n + 7])
    feeds = refs[2 * n + 7 : 2 * n + 9]
    rows, stage, feed, w, sem, out_sem = refs[2 * n + 9 :]
    step, units = pl.program_id(0), spans * fs
    block, d = rows.shape[1:]
    tile, half = g_ref.shape[0], d // 2
    per = tile // block

    @pl.when(step == 0)
    def _():
        for m in range(n):
            spot = gather_place(n, m)
            pltpu.make_async_copy(pieces[m], rows.at[spot, :, :half], sem.at[spot // per]).start()
            pltpu.make_async_copy(pieces[n + m], rows.at[spot, :, half:], sem.at[spot // per]).start()
        for t in range(spans):
            for kind, first in enumerate((0, units, 2 * units)):
                w[first + t * fs : first + (t + 1) * fs] = w_ref[t, kind * fs : (kind + 1) * fs]

    these = pl.ds(step * per, per)
    pltpu.make_async_copy(rows.at[these], rows.at[these], sem.at[step]).wait()
    normed = rows[these].reshape(tile, d)
    normed_ref[...] = normed
    inner = mm(normed, w[: 2 * units], NT)
    gate, up = inner[:, :units], inner[:, units:]
    sigma = jax.nn.sigmoid(gate)
    silu = gate * sigma
    hidden = (silu * up).astype(BF)
    hidden_ref[...] = hidden
    d_hidden = mm(g_ref[...], w[2 * units :], NT).astype(BF).astype(F32)
    d_gate = (d_hidden * up * (sigma * (1.0 + gate * (1.0 - sigma)))).astype(BF)
    d_inner = jnp.concatenate([d_gate, (d_hidden * silu).astype(BF)], axis=1)
    inner_ref[...] = d_inner
    stage[these] = mm(d_inner, w[: 2 * units], NN).astype(BF).reshape(per, block, d)
    feed[these] = mm(hidden, w[2 * units :], NN).astype(BF).reshape(per, block, d)
    for part in range(per):
        at = step * per + part
        for m in range(n):

            @pl.when(at == gather_place(n, m))
            def _(at=at, m=m):
                for route, cols in enumerate((slice(0, half), slice(half, d))):
                    side, spot = reduce_place(n, route, m)
                    there = backs[route][side].at[spot * block : (spot + 1) * block]
                    pltpu.make_async_copy(stage.at[at, :, cols], there, out_sem).start()
                side, spot = reduce_place(n, 0, m)
                there = feeds[side].at[spot * block : (spot + 1) * block]
                pltpu.make_async_copy(feed.at[at], there, out_sem).start()

    @pl.when(step == pl.num_programs(0) - 1)
    def _():
        pltpu.make_async_copy(stage, stage, out_sem).wait()
        pltpu.make_async_copy(feed, feed, out_sem).wait()


def feed_forward(meta, weights, grads, pieces, fs):
    n = len(pieces) // 2
    rows, d = grads.shape
    block = rows // n
    spans = weights.shape[0]
    units = spans * fs
    tile = min(512, rows)
    turned = lambda w: pl.BlockSpec((tile, w), lambda i, meta: (i, 0))
    shape = lambda w: jax.ShapeDtypeStruct((rows, w), BF)
    got = pl.pallas_call(
        functools.partial(feed_kernel, (n, spans, fs)),
        grid_spec=pltpu.PrefetchScalarGridSpec(
            num_scalar_prefetch=1,
            grid=(rows // tile,),
            in_specs=[VMEM, turned(d)] + [ANY] * (2 * n),
            out_specs=[turned(d), turned(units), turned(2 * units)] + [ANY] * 6,
            scratch_shapes=[
                pltpu.VMEM((n, block, d), BF),
                pltpu.VMEM((n, block, d), BF),
                pltpu.VMEM((n, block, d), BF),
                pltpu.VMEM((3 * units, d), BF),
                pltpu.SemaphoreType.DMA((rows // tile,)),
                pltpu.SemaphoreType.DMA,
            ],
        ),
        out_shape=[shape(d), shape(units), shape(2 * units)]
        + [jax.ShapeDtypeStruct((rows // 2, d // 2), BF)] * 4
        + [jax.ShapeDtypeStruct((rows // 2, d), BF)] * 2,
        compiler_params=params(),
        cost_estimate=QUICK,
        name="feed_forward",
    )(meta, weights, grads, *pieces)
    return got[:3], (got[3:5], got[5:7]), got[7:]


def branch_kernel(cfg, meta, left_a, left_b, right_a, right_b, mixed_ref, g_ref, gain_ref, wo_ref, *refs):
    first, n, spans = cfg
    heads, (mixed_out, gain_out), parts = refs[:spans], refs[spans : spans + 2], refs[spans + 2 : 2 * spans + 2]
    sides, (outer, sem) = refs[2 * spans + 2 : 2 * spans + 4], refs[2 * spans + 4 :]
    qw, out_rows = parts[0].shape[1], outer.shape[1] // n
    total = lambda a, b: a[...].astype(F32) + b[...].astype(F32)
    grad = jnp.concatenate([total(left_a, left_b), total(right_a, right_b)], axis=1)
    gain = gain_ref[1:2, :]
    unit, inverse, _ = norm_rows(mixed_ref[...], gain)
    gain_out[...] = jnp.sum(grad * unit, axis=0, keepdims=True)
    d_mixed = g_ref[...].astype(F32) + norm_back(grad, unit, inverse, gain)
    mixed_out[...] = d_mixed
    branch = d_mixed.astype(BF)
    for k, part in enumerate(parts):
        part[...] = mm(branch, wo_ref[lax.rem(meta[1] + k, spans), first:], NT).astype(BF)
    for k in range(spans):
        if outer.shape[1] > qw:
            outer[k, qw:] = jnp.zeros((outer.shape[1] - qw, outer.shape[2]), BF)
        outer[k, :qw] = mm(heads[(spans - k) % spans][...], branch, TN).astype(BF)
        spread(meta, outer.at[k], sides, n, 0, out_rows, sem, k * out_rows, spans * out_rows)
    pltpu.make_async_copy(outer, outer, sem).wait()


def branch_back(meta, pairs, mixed, grads, gains, weights, heads, n, first):
    block, d = mixed.shape
    spans, qw = weights.shape[0], weights.shape[1] - first
    out_rows = share_rows(qw, n)
    whole = lambda a: pl.BlockSpec(a.shape, lambda i, meta: (0, 0))
    terms = [*pairs[0], *pairs[1]]
    shape = jax.ShapeDtypeStruct
    outs = [shape((block, d), F32), shape((1, d), F32)] + [shape((block, qw), BF)] * spans
    got = pl.pallas_call(
        functools.partial(branch_kernel, (first, n, spans)),
        grid_spec=pltpu.PrefetchScalarGridSpec(
            num_scalar_prefetch=1,
            grid=(1,),
            in_specs=[whole(t) for t in terms]
            + [whole(mixed), pl.BlockSpec((block, d), lambda i, meta: (meta[1], 0)), whole(gains), VMEM]
            + [whole(h) for h in heads],
            out_specs=[whole(o) for o in outs] + [ANY] * 2,
            scratch_shapes=[pltpu.VMEM((spans, n * out_rows, d), BF), pltpu.SemaphoreType.DMA],
        ),
        out_shape=outs + [shape((n // 2 * spans * out_rows, d), BF)] * 2,
        compiler_params=params(),
        cost_estimate=QUICK,
        name="branch_back",
    )(meta, *terms, mixed, grads, gains, weights, *heads)
    return got[0], got[1], got[2 : 2 + spans], got[2 + spans :]


def place_kernel(n, meta, *refs):
    pieces, out = refs[:n], refs[n]
    rows = out.shape[0] // n
    for k, piece in enumerate(pieces):
        block = lax.rem(meta[1] - k + n, n)
        out[pl.ds(pl.multiple_of(block * rows, rows), rows), :] = piece[:rows, :].astype(out.dtype)


def place(meta, pieces, rows, kind=BF):
    n, d = len(pieces), pieces[0].shape[1]
    return pl.pallas_call(
        functools.partial(place_kernel, n),
        in_specs=[SMEM] + [VMEM] * n,
        out_specs=VMEM,
        out_shape=jax.ShapeDtypeStruct((n * rows, d), kind),
        compiler_params=params(),
        cost_estimate=QUICK,
        name="place",
    )(meta, *pieces)


def norm_back(grad_normed, unit_rows, inverse, gain_row):
    scaled = grad_normed * gain_row
    return inverse * (scaled - unit_rows * jnp.mean(scaled * unit_rows, axis=-1, keepdims=True))


def feed_grads_kernel(cfg, hidden, d_inner, normed, grads, out):
    spans, fs = cfg
    units = spans * fs
    pairs = [(d_inner.at[:, :units], normed), (d_inner.at[:, units:], normed), (hidden, grads)]
    for kind, (left, right) in enumerate(pairs):
        product = mm(left[...], right[...], TN).astype(BF)
        for t in range(spans):
            out[t, kind * fs : (kind + 1) * fs] = product[t * fs : (t + 1) * fs]


def feed_grads(hidden, d_inner, normed, grads, fs):
    (rows, units), d = hidden.shape, normed.shape[1]
    return pl.pallas_call(
        functools.partial(feed_grads_kernel, (units // fs, fs)),
        in_specs=[VMEM] * 4,
        out_specs=VMEM,
        out_shape=jax.ShapeDtypeStruct((units // fs, 3 * fs, d), BF),
        compiler_params=params(),
        cost_estimate=QUICK,
        name="feed_grads",
    )(hidden, d_inner, normed, grads)


def share_rows(rows, n):
    return -(-rows // (16 * n)) * 16


def spread(meta, stage, sides, n, route, rows, sem, base=0, total=None):
    for m in range(n):
        at = pl.ds(pl.multiple_of(lax.bitwise_xor(meta[0], m) * rows, rows), rows)
        side, spot = reduce_place(n, route, m)
        first = spot * (total or rows) + base
        pltpu.make_async_copy(stage.at[at], sides[side].at[first : first + rows], sem).start()


def both(pair):
    return (pair[0][...].astype(F32) + pair[1][...].astype(F32)).astype(BF)


def late_kernel(cfg, meta, dq, dk_a, dk_b, dv_a, dv_b, normed, *refs):
    n, qw = cfg
    sides, (stage, sem) = refs[:2], refs[2:]
    used = 3 * qw
    if stage.shape[0] > used:
        stage[used:] = jnp.zeros((stage.shape[0] - used, stage.shape[1]), BF)
    for at, left in enumerate((dq[...], both((dk_a, dk_b)), both((dv_a, dv_b)))):
        stage[at * qw : (at + 1) * qw] = mm(left, normed[...], TN).astype(BF)
    spread(meta, stage, sides, n, 0, stage.shape[0] // n, sem)
    pltpu.make_async_copy(stage, stage, sem).wait()


def late_grads(meta, dq, dk, dv, normed, n):
    (tok, qw), d = dq.shape, normed.shape[1]
    rows = share_rows(3 * qw, n)
    return pl.pallas_call(
        functools.partial(late_kernel, (n, qw)),
        in_specs=[SMEM] + [VMEM] * 6,
        out_specs=[ANY] * 2,
        out_shape=[jax.ShapeDtypeStruct((n * rows // 2, d), BF)] * 2,
        scratch_shapes=[pltpu.VMEM((n * rows, d), BF), pltpu.SemaphoreType.DMA],
        compiler_params=params(),
        cost_estimate=QUICK,
        name="late_grads",
    )(meta, dq, *dk, *dv, normed)


def soap_kernel(cfg, meta, held, early, late, weight_ref, first_ref, second_ref, average_ref, stat_ref, basis_ref,
                weight_out, first_out, second_out, average_out, stat_out, turned_out, grads, wide, sem):
    n, late_panels, out_panels, pf, cap, rows, out_rows, group = cfg
    slots, panel, width = weight_ref.shape
    me, step = meta[0], pl.program_id(0)
    inner_panels = late_panels - out_panels

    def fetch(slot, source, share, base):
        grain = min(share, panel)
        for part in range(panel // grain):
            row = source * panel + part * grain
            at = gather_place(n, lax.bitwise_xor(me, row // share)) * (rows + out_rows) + base + row % share
            there = grads.at[slot, part * grain : (part + 1) * grain]
            pltpu.make_async_copy(late.at[pl.ds(pl.multiple_of(at, grain), grain)], there, sem).start()

    @pl.when(step == 0)
    def _():
        for slot in range(slots):
            source = held[slot]

            @pl.when(source < 0)
            def _(slot=slot):
                grads[slot] = jnp.zeros((panel, grads.shape[2]), BF)

            @pl.when((source >= 0) & (source < inner_panels))
            def _(slot=slot, source=source):
                fetch(slot, source, rows, 0)

            @pl.when((source >= inner_panels) & (source < late_panels))
            def _(slot=slot, source=source):
                fetch(slot, source - inner_panels, out_rows, rows)

            @pl.when(source >= late_panels)
            def _(slot=slot, source=source):
                kind, unit = (source - late_panels) // pf, (source - late_panels) % pf
                spot = (unit // cap) * 3 * cap + kind * cap + unit % cap
                pltpu.make_async_copy(early.at[spot], grads.at[slot], sem).start()

        for slot in range(slots):

            @pl.when(held[slot] >= 0)
            def _(slot=slot):
                pltpu.make_async_copy(grads.at[slot], grads.at[slot], sem).wait()

    high = functools.partial(lax.dot_general, precision=HIGH, preferred_element_type=F32)
    cols = pl.ds(pl.multiple_of(step * width, width), width)

    def parts(value):
        top = value.astype(BF)
        return top, (value - top.astype(F32)).astype(BF)

    for low in range(0, slots, group):
        count = min(group, slots - low)
        size = count * panel
        slot_range = slice(low, low + count)
        diagonal = wide.at[low // group]

        @pl.when(step == 0)
        def _(low=low, count=count, diagonal=diagonal):
            diagonal[...] = jnp.zeros_like(diagonal)
            for j in range(count):
                at = slice(j * panel, (j + 1) * panel)
                diagonal[at, at] = basis_ref[low + j]
                stat_out[low + j] = BETA_TWO * stat_ref[low + j]

        grad = grads[slot_range, :, cols].reshape(size, width)
        square = mm(grad, grad, NT)
        for j in range(count):
            at = slice(j * panel, (j + 1) * panel)
            stat_out[low + j] += (1.0 - BETA_TWO) * square[at, at]
        top, rest = parts(diagonal[:size, :size])
        flat = lambda ref, slot_range=slot_range, size=size: ref[slot_range].reshape(size, width)
        rotated = mm(top, grad, TN) + mm(rest, grad, TN)
        first = BETA_ONE * flat(first_ref) + (1.0 - BETA_ONE) * rotated
        second = BETA_TWO * flat(second_ref) + (1.0 - BETA_TWO) * rotated * rotated
        direction = (first / (1.0 - BETA_ONE**STEP)) / (
            jnp.sqrt(second / (1.0 - BETA_TWO**STEP)) + ADAM_EPSILON
        )
        high_part, low_part = parts(direction)
        update = mm(top, high_part, NN) + (mm(top, low_part, NN) + mm(rest, high_part, NN))
        weight = flat(weight_ref)
        new_weight = weight - RATE * (update + WEIGHT_DECAY * weight)
        average = AVERAGE_DECAY * flat(average_ref) + (1.0 - AVERAGE_DECAY) * new_weight
        shape = (count, panel, width)
        first_out[slot_range] = first.reshape(shape)
        second_out[slot_range] = second.reshape(shape)
        weight_out[slot_range] = new_weight.reshape(shape)
        average_out[slot_range] = average.reshape(shape)

        @pl.when(step == pl.num_programs(0) - 1)
        def _(low=low, count=count):
            for j in range(count):
                turned_out[low + j] = high(stat_out[low + j], basis_ref[low + j], NN)


def soap(meta, held, early, late, n, weight, first, second, average, stat, basis, late_panels, out_panels, pf, cap, rows):
    slots, panel, d = weight.shape
    width, group = 256, 8
    out_rows = late.shape[0] // n - rows
    big = pl.BlockSpec((slots, panel, width), lambda i, meta, held: (0, 0, i))
    small = pl.BlockSpec((slots, panel, panel), lambda i, meta, held: (0, 0, 0))
    shape = jax.ShapeDtypeStruct
    return pl.pallas_call(
        functools.partial(soap_kernel, (n, late_panels, out_panels, pf, cap, rows, out_rows, group)),
        grid_spec=pltpu.PrefetchScalarGridSpec(
            num_scalar_prefetch=2,
            grid=(d // width,),
            in_specs=[ANY] * 2 + [big] * 4 + [small] * 2,
            out_specs=[big] * 4 + [small] * 2,
            scratch_shapes=[
                pltpu.VMEM((slots, panel, d), BF),
                pltpu.VMEM((-(-slots // group), group * panel, group * panel), F32),
                pltpu.SemaphoreType.DMA,
            ],
        ),
        out_shape=[shape((slots, panel, d), F32)] * 4 + [shape((slots, panel, panel), F32)] * 2,
        compiler_params=params(),
        cost_estimate=QUICK,
        name="soap",
    )(meta, held, early, late, weight, first, second, average, stat, basis)


def orthonormal_kernel(columns_ref, out_ref):
    size = columns_ref.shape[0]
    out_ref[...] = columns_ref[...]
    for i in range(size):
        vector = out_ref[i]
        vector = vector * lax.rsqrt(jnp.sum(vector * vector, axis=0, keepdims=True))
        out_ref[i] = vector
        if i < size - 1:
            rest = out_ref[i + 1 :]
            out_ref[i + 1 :] = rest - jnp.sum(rest * vector[None], axis=1, keepdims=True) * vector[None]


def orthonormal(matrix):
    columns = jnp.transpose(matrix, (2, 1, 0))
    found = pl.pallas_call(
        orthonormal_kernel,
        in_specs=[VMEM],
        out_specs=VMEM,
        out_shape=jax.ShapeDtypeStruct(columns.shape, F32),
        compiler_params=params(),
        name="orthonormal",
    )(columns)
    return jnp.transpose(found, (2, 1, 0))


def adam_gain(gradient, weight, first_state, second):
    new_first = BETA_ONE * first_state + (1.0 - BETA_ONE) * gradient
    new_second = BETA_TWO * second + (1.0 - BETA_TWO) * gradient * gradient
    direction = (
        new_first
        / (1.0 - BETA_ONE**STEP)
        / (jnp.sqrt(new_second / (1.0 - BETA_TWO**STEP)) + ADAM_EPSILON)
    )
    return (weight - GAIN_RATE * direction, new_first, new_second)


def back_kernel(meta, x_ref, dq, dk_a, dk_b, dv_a, dv_b, wq, wk, wv, out, gain_out):
    total = mm(dq[...], wq[...], NN) + mm(both((dk_a, dk_b)), wk[...], NN)
    total = total + mm(both((dv_a, dv_b)), wv[...], NN)
    out[...] = total.astype(BF)
    unit, _, _ = norm_rows(x_ref[...].astype(F32), 1.0)
    share = jnp.sum(total * unit, axis=0, keepdims=True)

    @pl.when(pl.program_id(0) == 0)
    def _():
        gain_out[...] = share

    @pl.when(pl.program_id(0) > 0)
    def _():
        gain_out[...] += share


def back_in(meta, x, dq, dk, dv, wq, wk, wv, n, low, high):
    tok, (qw, d) = dq.shape[0], wq.shape
    tile = tok // n
    rows = lambda w: pl.BlockSpec((tile, w), lambda i, meta: ((meta[1] - i - low + n) % n, 0))
    whole = pl.BlockSpec((qw, d), lambda i, meta: (0, 0))
    return pl.pallas_call(
        back_kernel,
        grid_spec=pltpu.PrefetchScalarGridSpec(
            num_scalar_prefetch=1,
            grid=(high - low,),
            in_specs=[rows(d)] + [rows(qw)] * 5 + [whole] * 3,
            out_specs=[pl.BlockSpec((tile, d), lambda i, meta: (i, 0)), pl.BlockSpec((1, d), lambda i, meta: (0, 0))],
        ),
        out_shape=[jax.ShapeDtypeStruct(((high - low) * tile, d), BF), jax.ShapeDtypeStruct((1, d), F32)],
        compiler_params=params(),
        cost_estimate=QUICK,
        name="back_in",
    )(meta, x, dq, *dk, *dv, wq, wk, wv)


def shards(
    tokens,
    cotangent,
    lengths,
    retrieve,
    owners,
    masters,
    first_moment,
    second_moment,
    averaged,
    statistics,
    bases,
    gains,
    gain_first,
    gain_second,
):
    tok, d = tokens.shape
    n_seq, n_tp = lax.axis_size("seq"), lax.axis_size("tp")
    me, z = lax.axis_index("seq"), lax.axis_index("tp")
    qw, ff = H // n_tp * HD, FF // n_tp
    slots_dev, panel = masters.shape[1:3]
    split = (slots_dev + 1) // 2
    docs, picks = lengths.shape[0], retrieve.shape[1]
    recalled = lax.dynamic_index_in_dim(retrieve, me, 0, keepdims=False)
    meta = jnp.concatenate([jnp.stack([me, z]).astype(I32), lengths, recalled])
    block = tok // n_tp
    pq, pf = qw // panel, ff // panel
    cap = -(-pf // n_seq)
    fs = cap * panel
    slot_ids = me * slots_dev + jnp.arange(slots_dev, dtype=I32)
    panel_ids = jnp.arange(1, owners.shape[0] + 1, dtype=I32)
    held = jnp.sum(jnp.where(slot_ids[:, None] == owners[None, :], panel_ids[None, :], 0), axis=1) - 1

    def mine(rows):
        return lax.dynamic_slice_in_dim(rows, z * block, block, 0)

    def whole_tp(rows):
        return lax.all_gather(rows, "tp", axis=0, tiled=True)

    def whole_seq(rows):
        return lax.all_gather(rows, "seq", axis=0, tiled=True)

    own = masters[0].astype(BF)
    pieces, _ = gather_seq([own[:split], own[split:]], n_seq)
    pieces = list(zip(*pieces, strict=True))
    q, k, v, normed_one, inner, share = project_in(
        meta, owners, tokens, gains, pieces, pq, pf, cap, slots_dev, split
    )
    (keys, values), _ = gather_seq([k, v], n_seq)
    weights = whole_tp(share).reshape(n_tp, -1, d)
    own_grads, keys[n_seq - 2], values[n_seq - 2] = pin(mine(cotangent), keys[n_seq - 2], values[n_seq - 2])
    grads_all = direct_pieces(own_grads, n_seq)
    turned_heads, wide, logs = attend(meta, q, keys, values, docs, picks, block)
    turned_heads, grads_all = pin(turned_heads, grads_all)
    heads = trade_tp(turned_heads, n_tp)
    mixed, left, right = mix(meta, tokens, gains, weights, heads)
    left, grads_all = pin(left, grads_all)
    grads_all = core_gather(jnp.concatenate(grads_all, axis=0), n_seq)
    (left, right), _ = gather_seq([left, right], n_seq)
    (normed_two, hidden, d_inner), pairs, feed = feed_forward(meta, weights, grads_all, left + right, fs)

    last = len(routes(n_seq)[0])
    inner_rows, out_rows = share_rows(3 * qw, n_seq), share_rows(qw, n_seq)
    feed_sums_in = (hidden, d_inner, normed_two, grads_all)
    for at in range(last + 1):
        pairs = reduce_levels(pairs, n_seq, at)
        if at == last - 1:
            pairs, feed, feed_sums = pin(pairs, (feed[0], swap(feed[1], n_seq, 1)), feed_sums)
            feed = plus(*feed)
        elif at == 0:
            pairs, feed, feed_sums_in = pin(pairs, feed, feed_sums_in)
            feed_sums = feed_grads(*feed_sums_in, fs)
    d_mixed, grad_gain_two, d_heads, outer = branch_back(
        meta, pairs, mixed, cotangent, gains, weights, heads, n_seq, 3 * fs
    )
    d_heads = trade_tp(d_heads, n_tp)
    outer = plus(outer[0], swap(outer[1], n_seq, 1))

    size = n_tp * out_rows
    parts = {}
    for m in range(0, n_seq, 2):
        at = reduce_place(n_seq, 0, m)[1]
        parts[m] = jnp.concatenate([feed[at * block : (at + 1) * block], outer[at * size : (at + 1) * size]], axis=0)
    d_heads, parts, feed_sums = pin(d_heads, parts, feed_sums)
    parts = [swap(part, n_seq, m) if m else part for m, part in parts.items()]
    feed_sums = lax.psum_scatter(feed_sums.reshape(-1, d), "tp", scatter_dimension=0, tiled=True)
    dq, *pairs = attend_back(meta, q, d_heads, wide, logs, keys, values, docs, picks)
    parts, dq, pairs = pin(parts, dq, pairs)
    pairs = reduce_levels(pairs, n_seq, 0)
    total = sum(part.astype(F32) for part in parts)
    output = (mixed + total[:block]).astype(BF)
    outer = [total[block + k * out_rows : block + (k + 1) * out_rows].astype(BF) for k in range(n_tp)]
    outputs = [output]
    for at in range(last + 1):
        if at:
            pairs = reduce_levels(pairs, n_seq, at)
            while len(outputs) < n_tp and (at == last or len(outputs) < 1 + 2 * at):
                outputs.append(ring(outputs[-1], n_tp, 1))
        pairs, outputs, feed_sums, dq = pin(pairs, outputs, feed_sums, dq)
        if at == min(1, last):
            pairs, outer, held = pin(pairs, outer, held)
    dk, dv = pairs
    output = place(meta, outputs, block)
    early = whole_seq(feed_sums).reshape(-1, panel, d)

    inputs = (meta, tokens, dq, dk, dv, inner[0], inner[1], inner[2], n_tp)
    total, gain_a = back_in(*inputs, n_tp - 1, n_tp)
    total, lefts = pin(total, (dq, dk, dv))
    back_rest, gain_b = back_in(meta, tokens, *lefts, *inputs[5:], 0, n_tp - 1)
    gain_total = jnp.concatenate([gain_a + gain_b, grad_gain_two], axis=0)
    late = late_grads(meta, *lefts, normed_one, n_seq)

    def advance(late, step):
        if step == 1:
            late = plus(late[0], swap(late[1], n_seq, 1))
        elif step == 2:
            parts = direct_reduce(late, n_seq, inner_rows)
            late = sum(part.astype(F32) for part in parts).astype(BF)
            late = jnp.concatenate([late, outer], axis=0)
        elif step == 3:
            late = direct_gather(late, n_seq)
        elif step == 4:
            late = core_gather(late, n_seq)
        return late

    steps = max(2 * (n_tp - 1), 6)
    gain_steps = sum_steps(n_seq, n_tp)
    gather = []
    for step in range(steps):
        if step < n_tp - 1:
            k = n_tp - 2 - step
            came = ring(total, n_tp, -1)
            late = advance(late, step)
            if step == 0:
                outer = trade_tp(outer, n_tp)
            if step == 1:
                came, output = pin(came, output)
            for _ in range(min(len(gain_steps), 2 if 0 < step else 0)):
                gain_total = gain_steps.pop(0)(gain_total)
            came, late, back_rest, outer, held, gain_total = pin(came, late, back_rest, outer, held, gain_total)
            if step == 0:
                outer = sum(part.astype(F32) for part in outer).astype(BF)
            part = back_rest[k * block : (k + 1) * block]
            if k:
                total = plus(part, came)
                total, late, gain_total = pin(total, late, gain_total)
                continue
            d_normed_one = part.astype(F32) + came.astype(F32)
            unit_one, inverse_one, _ = norm_rows(mine(tokens).astype(F32), gains[0])
            grad_here = d_mixed + norm_back(d_normed_one, unit_one, inverse_one, gains[0])
            gather.append(grad_here.astype(BF))
            continue
        if len(gather) < n_tp:
            gather.append(ring(gather[-1], n_tp, 1))
        for _ in range(min(len(gain_steps), 1)):
            gain_total = gain_steps.pop(0)(gain_total)
        late = advance(late, step)
        if step == steps - 2:
            new_weight, new_first, new_second, new_average, new_stat, turned_basis = soap(
                meta, held, early, late, n_seq, masters[0], first_moment[0], second_moment[0], averaged[0],
                statistics[0], bases[0], 4 * pq, pq, pf, cap, inner_rows,
            )
            gather[-1], turned_basis, gain_total = pin(gather[-1], turned_basis, gain_total)
        elif step == steps - 1:
            new_basis = orthonormal(turned_basis)
            gather, new_basis, gain_total = pin(gather, new_basis, gain_total)
        else:
            gather[-1], late, gain_total = pin(gather[-1], late, gain_total)
    for step in gain_steps:
        gain_total = step(gain_total)
    grad_input = place(meta, gather, block, F32)
    new_gains, new_gain_first, new_gain_second = adam_gain(gain_total, gains, gain_first, gain_second)
    return (
        output,
        grad_input,
        new_weight[None],
        new_first[None],
        new_second[None],
        new_average[None],
        new_stat[None],
        new_basis[None],
        new_gains,
        new_gain_first,
        new_gain_second,
    )


def solution(mesh):
    by_token, by_slot = P("seq", None), P("tp", "seq", None, None)
    in_specs = (by_token, by_token, P(), P(), P()) + (by_slot,) * 6 + (P(),) * 3
    out_specs = (by_token, by_token) + (by_slot,) * 6 + (P(),) * 3
    return jax.shard_map(shards, mesh=mesh, in_specs=in_specs, out_specs=out_specs, check_vma=False)
```

```python
import functools

import jax
import jax.numpy as jnp
from jax import lax
from jax.experimental import pallas as pl
from jax.experimental.pallas import tpu as pltpu
from jax.sharding import PartitionSpec as P

H = 8
HD = 128
FF = 2816
MEMB = 128
STEP = 10

EPSILON = 1e-06
RATE = 0.02
GAIN_RATE = 0.5
BETA_ONE = 0.9
BETA_TWO = 0.95
ADAM_EPSILON = 1e-08
WEIGHT_DECAY = 0.01
AVERAGE_DECAY = 0.8
NEGATIVE = -1e30
START_TOP = -1e29
LOG2E = 1.4426950408889634

BF = jnp.bfloat16
F32 = jnp.float32
I32 = jnp.int32
HIGH = lax.Precision.HIGHEST
ANY = pl.BlockSpec(memory_space=pl.ANY)
SMEM = pl.BlockSpec(memory_space=pltpu.SMEM)
VMEM = pl.BlockSpec(memory_space=pltpu.VMEM)
VMEM_BYTES = 58 * 2**20

NT = (((1,), (1,)), ((), ()))
NN = (((1,), (0,)), ((), ()))
TN = (((0,), (0,)), ((), ()))


def mm(left, right, dims):
    return lax.dot_general(left, right, dims, preferred_element_type=F32)


QUICK = pl.CostEstimate(flops=1000, bytes_accessed=1000, transcendentals=0)


def params(**more):
    return pltpu.CompilerParams(vmem_limit_bytes=VMEM_BYTES, **more)


def pin(*values):
    return lax.optimization_barrier(values)


def routes(count):
    bits = []
    bit = 2
    while bit < count:
        bits.append(bit)
        bit *= 2
    return bits, bits[::-1]


def swap(value, count, bit):
    return lax.ppermute(value, "seq", [(i, i ^ bit) for i in range(count)])


def gather_seq(owns, count, beside=None):
    orders = routes(count)
    held = [{0: own} for own in owns]
    hops = len(orders[0])
    for stage in range(hops + 1):
        for i, pieces in enumerate(held):
            order = orders[i % 2]
            come = {}
            for m, piece in pieces.items():
                if m & 1 or bin(m).count("1") != stage:
                    continue
                for bit in order:
                    if all(other == bit or not m & other for other in order[order.index(bit) :]) and not m & bit:
                        come[m | bit] = swap(piece, count, bit)
                come[m | 1] = swap(piece, count, 1)
            pieces.update(come)
        if stage < hops:
            held, beside = pin(held, beside)
    return [[pieces[m] for m in range(count)] for pieces in held], beside


def plus(left, right):
    return (left.astype(F32) + right.astype(F32)).astype(left.dtype)


def reduce_bits(count, route):
    return [1, *routes(count)[route][::-1]]


def reduce_place(count, route, m):
    bits = reduce_bits(count, route)
    block = 0
    for bit in bits[1:]:
        block = 2 * block + bool(m & bit)
    return int(bool(m & bits[0])), block


def reduce_level(pair, count, route, at):
    keep, send = pair
    bits = reduce_bits(count, route)
    came = swap(send, count, bits[at])
    if at == len(bits) - 1:
        return keep, came
    half = keep.shape[0] // 2
    return plus(keep[:half], came[:half]), plus(keep[half:], came[half:])


def reduce_levels(pairs, count, at):
    return [reduce_level(pair, count, i % 2, at) for i, pair in enumerate(pairs)]


def direct_reduce(rows, count, sizes):
    parts = []
    for m in range(0, count, 2):
        at = reduce_place(count, 0, m)[1]
        part = rows[at * sizes : (at + 1) * sizes]
        parts.append(swap(part, count, m) if m else part)
    return parts


def direct_pieces(rows, count):
    return [swap(rows, count, m) if m else rows for m in range(0, count, 2)]


def direct_gather(rows, count):
    return jnp.concatenate(direct_pieces(rows, count), axis=0)


def core_gather(rows, count):
    return jnp.concatenate([rows, swap(rows, count, 1)], axis=0)


def gather_place(count, distance):
    return distance // 2 + (count // 2) * (distance % 2)


def ring(value, count, step):
    return lax.ppermute(value, "tp", [(i, (i + step) % count) for i in range(count)])


def trade_tp(parts, count):
    return [parts[0]] + [ring(parts[k], count, k) for k in range(1, count)]


def gather_tp(own, count):
    pieces = [own]
    for _ in range(count - 1):
        pieces.append(ring(pieces[-1], count, 1))
    return pieces


def reduce_tp(parts, count):
    total = parts[count - 1]
    for k in range(count - 2, -1, -1):
        came = ring(total, count, -1)
        if k == 0:
            return parts[0], came
        total = plus(parts[k], came)
    return None


def sum_steps(n_seq, n_tp):
    steps = []
    for axis, count in (("seq", n_seq), ("tp", n_tp)):
        bit = 1
        while bit < count:
            pairs = [(i, i ^ bit) for i in range(count)]
            steps.append(lambda v, axis=axis, pairs=pairs: v + lax.ppermute(v, axis, pairs))
            bit *= 2
    return steps


def panel_copies(owners_ref, me, first, amount, slots_dev, split, pieces, view, sem, back):
    def one(i, carry):
        slot = owners_ref[first + i]
        spot = lax.bitwise_xor(slot // slots_dev, me)
        row = slot % slots_dev
        for m, (low, high) in enumerate(pieces):
            for ref, base, size in ((low, 0, split), (high, split, slots_dev - split)):

                @pl.when((spot == m) & (row >= base) & (row < base + size))
                def _(ref=ref, base=base):
                    there = ref.at[row - base]
                    source, target = (view(i), there) if back else (there, view(i))
                    pltpu.make_async_copy(source, target, sem).start()

        return carry

    lax.fori_loop(0, amount, one, 0)


def norm_rows(rows, gain):
    inverse = lax.rsqrt(jnp.mean(rows * rows, axis=-1, keepdims=True) + EPSILON)
    unit = rows * inverse
    return unit, inverse, unit * gain


def project_kernel(cfg, meta, owners, x_ref, gain_ref, *refs):
    n, pq, pf, cap, slots_dev, split = cfg
    pieces = list(zip(refs[:n], refs[n : 2 * n], strict=True))
    outs = refs[2 * n : 2 * n + 3]
    normed_ref, inner, share, sems = refs[2 * n + 3 :]
    me, panel, d = meta[0], inner.shape[1], x_ref.shape[1]
    mine = jnp.clip(pf - me * cap, 0, cap)

    @pl.when(pl.program_id(0) == 0)
    def _():
        copies = functools.partial(panel_copies, owners, me)
        copies(0, 3 * pq, slots_dev, split, pieces, lambda i: inner.at[i], sems.at[0], False)
        copies(3 * pq, pq, slots_dev, split, pieces, lambda i: share.at[3 * cap + i], sems.at[1], False)
        for kind in range(3):
            for j in range(cap):

                @pl.when(j >= mine)
                def _(at=kind * cap + j):
                    share[at] = jnp.zeros(share.shape[1:], BF)

            copies(
                4 * pq + kind * pf + me * cap, mine, slots_dev, split, pieces,
                lambda i, kind=kind: share.at[kind * cap + i], sems.at[1], False,
            )

    _, _, normed = norm_rows(x_ref[...].astype(F32), gain_ref[0:1, :])
    normed = normed.astype(BF)
    normed_ref[...] = normed

    @pl.when(pl.program_id(0) == 0)
    def _():
        pltpu.make_async_copy(inner, inner, sems.at[0]).wait()

    for at in range(3):
        w = inner[at * pq : (at + 1) * pq].reshape(pq * panel, d)
        outs[at][...] = mm(normed, w, NT).astype(BF)

    @pl.when(pl.program_id(0) == pl.num_programs(0) - 1)
    def _():
        def finish(i, c):
            pltpu.make_async_copy(share.at[0], share.at[0], sems.at[1]).wait()
            return c

        lax.fori_loop(0, 3 * mine + pq, finish, 0)


def project_in(meta, owners, x, gains, pieces, pq, pf, cap, slots_dev, split):
    n = len(pieces)
    tok, d = x.shape
    panel = pieces[0][0].shape[1]
    qw = pq * panel
    tile = 256
    out = lambda w: pl.BlockSpec((tile, w), lambda i: (i, 0))
    whole = lambda count: pl.BlockSpec((count, panel, d), lambda i: (0, 0, 0))
    shape = lambda *dims: jax.ShapeDtypeStruct(dims, BF)
    q, k, v, normed, inner, share = pl.pallas_call(
        functools.partial(project_kernel, (n, pq, pf, cap, slots_dev, split)),
        grid=(tok // tile,),
        in_specs=[SMEM, SMEM, out(d), pl.BlockSpec(gains.shape, lambda i: (0, 0))] + [ANY] * (2 * n),
        out_specs=[out(qw)] * 3 + [out(d), whole(3 * pq), whole(3 * cap + pq)],
        out_shape=[shape(tok, qw)] * 3 + [shape(tok, d), shape(3 * pq, panel, d), shape(3 * cap + pq, panel, d)],
        scratch_shapes=[pltpu.SemaphoreType.DMA((2,))],
        compiler_params=params(),
        cost_estimate=QUICK,
        name="project",
    )(meta, owners, x, gains, *[p[0] for p in pieces], *[p[1] for p in pieces])
    return q, k, v, normed, inner.reshape(3, qw, d), share.reshape(-1, d)


def doc_start(meta, positions, docs):
    start = jnp.int32(0)
    found = jnp.zeros_like(positions)
    for at in range(docs):
        found = jnp.where(positions >= start, start, found)
        start = start + meta[2 + at]
    return found


def load_pieces(me, pieces, buffer, sem, tok):
    for m, piece in enumerate(pieces):
        owner = lax.bitwise_xor(me, m)
        at = pl.multiple_of(owner * tok, tok)
        pltpu.make_async_copy(piece, buffer.at[pl.ds(at, tok)], sem).start()


def member_table(meta, table, docs, picks, blocks):
    def clear(i, c):
        table[i] = 0
        return c

    lax.fori_loop(0, blocks, clear, 0)
    for e in range(picks):
        table[meta[2 + docs + e]] = 1


def memory_list(meta, blocks_ref, docs, picks, limit):
    count = jnp.int32(0)
    for e in range(picks):
        block = meta[2 + docs + e]
        fresh = (block + 1) * MEMB <= limit
        for other in range(e):
            fresh = fresh & (meta[2 + docs + other] != block)

        @pl.when(fresh)
        def _(count=count, block=block):
            blocks_ref[count] = block

        count = count + fresh.astype(I32)
    return count


def seen_rows(at, rows, table, starts, queries):
    row = lax.broadcasted_iota(I32, (MEMB, queries.shape[1]), 0)
    seen = []
    for b in range(rows // MEMB):
        base = at + b * MEMB
        lowest = starts * (1 - table[base // MEMB]) - base
        seen.append((row >= lowest) & (row <= queries - base))
    return seen


def hide(scores, seen, fill):
    kept = [jnp.where(mask, scores[b * MEMB : (b + 1) * MEMB], fill) for b, mask in enumerate(seen)]
    return jnp.concatenate(kept, axis=0)


def rows_of(buffer, spots, rows, cols):
    parts = [buffer[pl.ds(at, rows), cols] for at in spots]
    return parts[0] if len(parts) == 1 else jnp.concatenate(parts, axis=0)


def visit_keys(visit, state, meta, first, qt, kt, docs, picks, blocks):
    low = doc_start(meta, first, docs) // kt
    high = (first + qt - 1) // kt + 1
    clear = jnp.clip((doc_start(meta, first + qt - 1, docs) + kt - 1) // kt, low, high)
    full = jnp.clip(first // kt, clear, high)
    count = memory_list(meta, blocks, docs, picks, low * kt)

    def dense(masked):
        return lambda i, state: visit([pl.multiple_of(i * kt, kt)], kt, state, masked)

    def memory(together, base):
        def go(i, state):
            spots = [pl.multiple_of(blocks[base + i * together + j] * MEMB, MEMB) for j in range(together)]
            return visit(spots, MEMB, state, False)

        return go

    state = lax.fori_loop(low, clear, dense(True), state)
    state = lax.fori_loop(clear, full, dense(False), state)
    state = lax.fori_loop(full, high, dense(True), state)
    state = lax.fori_loop(0, count // 4, memory(4, 0), state)
    return lax.fori_loop(0, count % 4, memory(1, count // 4 * 4), state)


def attend_kernel(cfg, meta, q_ref, *refs):
    n, docs, picks, qt, kt, block = cfg
    keys, values = refs[:n], refs[n : 2 * n]
    turns, refs = refs[2 * n : 2 * n + q_ref.shape[0] // block], refs[2 * n + q_ref.shape[0] // block :]
    wide_ref, log_ref, kbuf, vbuf, acc, table, blocks, sems = refs
    tok, width = q_ref.shape
    me = meta[0]
    factor = HD**-0.5 * LOG2E
    load_pieces(me, keys, kbuf, sems.at[0], tok)
    load_pieces(me, values, vbuf, sems.at[1], tok)
    member_table(meta, table, docs, picks, kbuf.shape[0] // MEMB)
    pltpu.make_async_copy(kbuf, kbuf, sems.at[0]).wait()
    pltpu.make_async_copy(vbuf, vbuf, sems.at[1]).wait()
    heads = [slice(head * HD, (head + 1) * HD) for head in range(width // HD)]
    spans = tok // block

    def query_tile(t, carry):
        base = pl.multiple_of(t * qt, qt)
        first = me * tok + base
        queries = first + lax.broadcasted_iota(I32, (1, qt), 1)
        starts = doc_start(meta, queries, docs)
        acc[...] = jnp.zeros_like(acc)

        def visit(spots, rows, state, masked):
            seen = seen_rows(spots[0], rows, table, starts, queries) if masked else None
            result = []
            for head, cols in enumerate(heads):
                top, total = state[head]
                scores = mm(rows_of(kbuf, spots, rows, cols), q_ref[pl.ds(base, qt), cols], NT)
                if masked:
                    scores = hide(scores, seen, NEGATIVE)
                new_top = jnp.maximum(top, jnp.max(scores, axis=0, keepdims=True))
                fade = jnp.exp2((top - new_top) * factor)
                probs = jnp.exp2((scores - new_top) * factor)
                total = total * fade + jnp.sum(probs, axis=0, keepdims=True)
                product = mm(rows_of(vbuf, spots, rows, cols), probs.astype(BF), TN)
                acc[head] = acc[head] * fade + product
                result.append((new_top, total))
            return tuple(result)

        state = tuple((jnp.full((1, qt), START_TOP, F32), jnp.zeros((1, qt), F32)) for _ in heads)
        state = visit_keys(visit, state, meta, first, qt, kt, docs, picks, blocks)
        for head, cols in enumerate(heads):
            top, total = state[head]
            rows = jnp.transpose(acc[head] * (1.0 / total))
            wide_ref[pl.ds(base, qt), cols] = rows
            rows = rows.astype(BF)
            size = min(block, qt)
            inside = pl.ds(pl.multiple_of(lax.rem(base, block), size), size)
            for part in range(max(qt // block, 1)):
                spot = lax.rem(base // block + part - meta[1] + spans, spans)
                for k, turn in enumerate(turns):

                    @pl.when(spot == k)
                    def _(turn=turn, part=part, rows=rows, cols=cols):
                        turn[inside, cols] = rows[part * size : (part + 1) * size]

            log_ref[head : head + 1, pl.ds(base, qt)] = top * factor + jnp.log2(total)
        return carry

    lax.fori_loop(0, tok // qt, query_tile, 0)


def attend(meta, q, keys, values, docs, picks, block):
    n = len(keys)
    tok, width = q.shape
    qt, kt = 512, 1024
    *turns, wide, logs = pl.pallas_call(
        functools.partial(attend_kernel, (n, docs, picks, qt, kt, block)),
        in_specs=[SMEM, VMEM] + [ANY] * (2 * n),
        out_specs=[VMEM] * (2 + tok // block),
        out_shape=[jax.ShapeDtypeStruct((block, width), BF)] * (tok // block)
        + [
            jax.ShapeDtypeStruct((tok, width), F32),
            jax.ShapeDtypeStruct((width // HD, tok), F32),
        ],
        scratch_shapes=[
            pltpu.VMEM((n * tok, width), BF),
            pltpu.VMEM((n * tok, width), BF),
            pltpu.VMEM((width // HD, HD, qt), F32),
            pltpu.SMEM((n * tok // MEMB,), I32),
            pltpu.SMEM((picks,), I32),
            pltpu.SemaphoreType.DMA((2,)),
        ],
        compiler_params=params(),
        cost_estimate=QUICK,
        name="attend",
    )(meta, q, *keys, *values)
    return turns, wide, logs


def attend_back_kernel(cfg, meta, q_ref, wide_ref, log_ref, *refs):
    n, docs, picks, qt, kt, spans = cfg
    parts, refs = refs[:spans], refs[spans:]
    keys, values = refs[:n], refs[n : 2 * n]
    dq_ref = refs[2 * n]
    outs = (refs[2 * n + 1 : 2 * n + 3], refs[2 * n + 3 : 2 * n + 5])
    kbuf, vbuf, dk_acc, dv_acc, g_ref, acc, stage, table, blocks, sems, out_sems = refs[2 * n + 5 :]
    tok, width = q_ref.shape
    me = meta[0]
    block = tok // spans
    scale = HD**-0.5
    factor = scale * LOG2E
    load_pieces(me, keys, kbuf, sems.at[0], tok)
    load_pieces(me, values, vbuf, sems.at[1], tok)
    member_table(meta, table, docs, picks, kbuf.shape[0] // MEMB)

    def clear(i, c):
        at = pl.ds(pl.multiple_of(i * 256, 256), 256)
        dk_acc[at, :] = jnp.zeros((256, width), F32)
        dv_acc[at, :] = jnp.zeros((256, width), F32)
        return c

    lax.fori_loop(0, kbuf.shape[0] // 256, clear, 0)
    for k, part in enumerate(parts):
        spot = pl.multiple_of(lax.rem(meta[1] - k + spans, spans) * block, block)
        g_ref[pl.ds(spot, block), :] = part[...]
    pltpu.make_async_copy(kbuf, kbuf, sems.at[0]).wait()
    pltpu.make_async_copy(vbuf, vbuf, sems.at[1]).wait()
    heads = [slice(head * HD, (head + 1) * HD) for head in range(width // HD)]

    def query_tile(t, carry):
        base = pl.multiple_of(t * qt, qt)
        first = me * tok + base
        queries = first + lax.broadcasted_iota(I32, (1, qt), 1)
        starts = doc_start(meta, queries, docs)
        here = pl.ds(base, qt)
        deltas = []
        for cols in heads:
            product = g_ref[here, cols].astype(F32) * wide_ref[here, cols]
            deltas.append(jnp.sum(jnp.transpose(product), axis=0, keepdims=True))
        acc[...] = jnp.zeros_like(acc)

        def visit(spots, rows, state, masked):
            seen = seen_rows(spots[0], rows, table, starts, queries) if masked else None
            for head, cols in enumerate(heads):
                q, grad = q_ref[here, cols], g_ref[here, cols]
                k = rows_of(kbuf, spots, rows, cols)
                probs = jnp.exp2(mm(k, q, NT) * factor - log_ref[head : head + 1, here])
                if masked:
                    probs = hide(probs, seen, 0.0)
                slopes = probs * (mm(rows_of(vbuf, spots, rows, cols), grad, NT) - deltas[head])
                slopes = slopes.astype(BF)
                d_values = mm(probs.astype(BF), grad, NN)
                d_keys = mm(slopes, q, NN)
                for j, at in enumerate(spots):
                    part = slice(j * rows, (j + 1) * rows)
                    dv_acc[pl.ds(at, rows), cols] += d_values[part]
                    dk_acc[pl.ds(at, rows), cols] += d_keys[part]
                acc[head] += mm(k, slopes, TN)
            return state

        visit_keys(visit, jnp.int32(0), meta, first, qt, kt, docs, picks, blocks)
        for head, cols in enumerate(heads):
            dq_ref[here, cols] = (jnp.transpose(acc[head]) * scale).astype(BF)
        return carry

    lax.fori_loop(0, tok // qt, query_tile, 0)

    depth = stage.shape[1]

    def put(which, m):
        side, at = reduce_place(n, which, m)
        out = outs[which][side].at[at * tok : (at + 1) * tok]
        return pltpu.make_async_copy(stage.at[which, m % depth], out, out_sems.at[which, m % depth])

    for m in range(n):
        at = pl.ds(pl.multiple_of(lax.bitwise_xor(me, m) * tok, tok), tok)
        for which in range(2):
            if m >= depth:
                put(which, m - depth).wait()
            rows = dk_acc[at, :] * scale if which == 0 else dv_acc[at, :]
            stage[which, m % depth] = rows.astype(BF)
            put(which, m).start()
    for m in range(max(n - depth, 0), n):
        for which in range(2):
            put(which, m).wait()


def attend_back(meta, q, grads, wide, logs, keys, values, docs, picks):
    n = len(keys)
    tok, width = q.shape
    qt, kt = 512, 512
    got = pl.pallas_call(
        functools.partial(attend_back_kernel, (n, docs, picks, qt, kt, len(grads))),
        in_specs=[SMEM] + [VMEM] * (3 + len(grads)) + [ANY] * (2 * n),
        out_specs=[VMEM] + [ANY] * 4,
        out_shape=[jax.ShapeDtypeStruct((tok, width), BF)]
        + [jax.ShapeDtypeStruct((n * tok // 2, width), BF)] * 4,
        scratch_shapes=[
            pltpu.VMEM((n * tok, width), BF),
            pltpu.VMEM((n * tok, width), BF),
            pltpu.VMEM((n * tok, width), F32),
            pltpu.VMEM((n * tok, width), F32),
            pltpu.VMEM((tok, width), BF),
            pltpu.VMEM((width // HD, HD, qt), F32),
            pltpu.VMEM((2, 4, tok, width), BF),
            pltpu.SMEM((n * tok // MEMB,), I32),
            pltpu.SMEM((picks,), I32),
            pltpu.SemaphoreType.DMA((2,)),
            pltpu.SemaphoreType.DMA((2, 4)),
        ],
        compiler_params=params(),
        cost_estimate=QUICK,
        name="attend_back",
    )(meta, q, wide, logs, *grads, *keys, *values)
    return got[0], got[1:3], got[3:5]


def mix_kernel(first, meta, x_ref, gain_ref, wo_ref, *refs):
    heads, (mixed_ref, left_ref, right_ref) = refs[:-3], refs[-3:]
    spans, qw = len(heads), heads[0].shape[1]
    mixed = x_ref[...].astype(F32)
    for k, head in enumerate(heads):
        mixed = mixed + mm(head[...], wo_ref[lax.rem(meta[1] - k + spans, spans), first:], NN)
    mixed_ref[...] = mixed
    _, _, normed = norm_rows(mixed, gain_ref[1:2, :])
    normed = normed.astype(BF)
    half = normed.shape[1] // 2
    left_ref[...] = normed[:, :half]
    right_ref[...] = normed[:, half:]


def mix(meta, x, gains, weights, heads):
    block, d = heads[0].shape[0], x.shape[1]
    whole = lambda a: pl.BlockSpec(a.shape, lambda i, meta: (0, 0))
    shape = lambda w, t: jax.ShapeDtypeStruct((block, w), t)
    outs = [shape(d, F32), shape(d // 2, BF), shape(d // 2, BF)]
    return pl.pallas_call(
        functools.partial(mix_kernel, weights.shape[1] - heads[0].shape[1]),
        grid_spec=pltpu.PrefetchScalarGridSpec(
            num_scalar_prefetch=1,
            grid=(1,),
            in_specs=[pl.BlockSpec((block, d), lambda i, meta: (meta[1], 0)), whole(gains), VMEM]
            + [whole(h) for h in heads],
            out_specs=[whole(o) for o in outs],
        ),
        out_shape=outs,
        compiler_params=params(),
        cost_estimate=QUICK,
        name="mix",
    )(meta, x, gains, weights, *heads)


def feed_kernel(cfg, meta, w_ref, g_ref, *refs):
    n, spans, fs = cfg
    pieces = refs[: 2 * n]
    normed_ref, hidden_ref, inner_ref = refs[2 * n : 2 * n + 3]
    backs = (refs[2 * n + 3 : 2 * n + 5], refs[2 * n + 5 : 2 * n + 7])
    feeds = refs[2 * n + 7 : 2 * n + 9]
    rows, stage, feed, w, sem, out_sem = refs[2 * n + 9 :]
    step, units = pl.program_id(0), spans * fs
    block, d = rows.shape[1:]
    tile, half = g_ref.shape[0], d // 2
    per = tile // block

    @pl.when(step == 0)
    def _():
        for m in range(n):
            spot = gather_place(n, m)
            pltpu.make_async_copy(pieces[m], rows.at[spot, :, :half], sem.at[spot // per]).start()
            pltpu.make_async_copy(pieces[n + m], rows.at[spot, :, half:], sem.at[spot // per]).start()
        for t in range(spans):
            for kind, first in enumerate((0, units, 2 * units)):
                w[first + t * fs : first + (t + 1) * fs] = w_ref[t, kind * fs : (kind + 1) * fs]

    these = pl.ds(step * per, per)
    pltpu.make_async_copy(rows.at[these], rows.at[these], sem.at[step]).wait()
    normed = rows[these].reshape(tile, d)
    normed_ref[...] = normed
    inner = mm(normed, w[: 2 * units], NT)
    gate, up = inner[:, :units], inner[:, units:]
    sigma = jax.nn.sigmoid(gate)
    silu = gate * sigma
    hidden = (silu * up).astype(BF)
    hidden_ref[...] = hidden
    d_hidden = mm(g_ref[...], w[2 * units :], NT).astype(BF).astype(F32)
    d_gate = (d_hidden * up * (sigma * (1.0 + gate * (1.0 - sigma)))).astype(BF)
    d_inner = jnp.concatenate([d_gate, (d_hidden * silu).astype(BF)], axis=1)
    inner_ref[...] = d_inner
    stage[these] = mm(d_inner, w[: 2 * units], NN).astype(BF).reshape(per, block, d)
    feed[these] = mm(hidden, w[2 * units :], NN).astype(BF).reshape(per, block, d)
    for part in range(per):
        at = step * per + part
        for m in range(n):

            @pl.when(at == gather_place(n, m))
            def _(at=at, m=m):
                for route, cols in enumerate((slice(0, half), slice(half, d))):
                    side, spot = reduce_place(n, route, m)
                    there = backs[route][side].at[spot * block : (spot + 1) * block]
                    pltpu.make_async_copy(stage.at[at, :, cols], there, out_sem).start()
                side, spot = reduce_place(n, 0, m)
                there = feeds[side].at[spot * block : (spot + 1) * block]
                pltpu.make_async_copy(feed.at[at], there, out_sem).start()

    @pl.when(step == pl.num_programs(0) - 1)
    def _():
        pltpu.make_async_copy(stage, stage, out_sem).wait()
        pltpu.make_async_copy(feed, feed, out_sem).wait()


def feed_forward(meta, weights, grads, pieces, fs):
    n = len(pieces) // 2
    rows, d = grads.shape
    block = rows // n
    spans = weights.shape[0]
    units = spans * fs
    tile = min(512, rows)
    turned = lambda w: pl.BlockSpec((tile, w), lambda i, meta: (i, 0))
    shape = lambda w: jax.ShapeDtypeStruct((rows, w), BF)
    got = pl.pallas_call(
        functools.partial(feed_kernel, (n, spans, fs)),
        grid_spec=pltpu.PrefetchScalarGridSpec(
            num_scalar_prefetch=1,
            grid=(rows // tile,),
            in_specs=[VMEM, turned(d)] + [ANY] * (2 * n),
            out_specs=[turned(d), turned(units), turned(2 * units)] + [ANY] * 6,
            scratch_shapes=[
                pltpu.VMEM((n, block, d), BF),
                pltpu.VMEM((n, block, d), BF),
                pltpu.VMEM((n, block, d), BF),
                pltpu.VMEM((3 * units, d), BF),
                pltpu.SemaphoreType.DMA((rows // tile,)),
                pltpu.SemaphoreType.DMA,
            ],
        ),
        out_shape=[shape(d), shape(units), shape(2 * units)]
        + [jax.ShapeDtypeStruct((rows // 2, d // 2), BF)] * 4
        + [jax.ShapeDtypeStruct((rows // 2, d), BF)] * 2,
        compiler_params=params(),
        cost_estimate=QUICK,
        name="feed_forward",
    )(meta, weights, grads, *pieces)
    return got[:3], (got[3:5], got[5:7]), got[7:]


def branch_kernel(cfg, meta, left_a, left_b, right_a, right_b, mixed_ref, g_ref, gain_ref, wo_ref, *refs):
    first, n, spans = cfg
    heads, (mixed_out, gain_out), parts = refs[:spans], refs[spans : spans + 2], refs[spans + 2 : 2 * spans + 2]
    sides, (outer, sem) = refs[2 * spans + 2 : 2 * spans + 4], refs[2 * spans + 4 :]
    qw, out_rows = parts[0].shape[1], outer.shape[1] // n
    total = lambda a, b: a[...].astype(F32) + b[...].astype(F32)
    grad = jnp.concatenate([total(left_a, left_b), total(right_a, right_b)], axis=1)
    gain = gain_ref[1:2, :]
    unit, inverse, _ = norm_rows(mixed_ref[...], gain)
    gain_out[...] = jnp.sum(grad * unit, axis=0, keepdims=True)
    d_mixed = g_ref[...].astype(F32) + norm_back(grad, unit, inverse, gain)
    mixed_out[...] = d_mixed
    branch = d_mixed.astype(BF)
    for k, part in enumerate(parts):
        part[...] = mm(branch, wo_ref[lax.rem(meta[1] + k, spans), first:], NT).astype(BF)
    for k in range(spans):
        if outer.shape[1] > qw:
            outer[k, qw:] = jnp.zeros((outer.shape[1] - qw, outer.shape[2]), BF)
        outer[k, :qw] = mm(heads[(spans - k) % spans][...], branch, TN).astype(BF)
        spread(meta, outer.at[k], sides, n, 0, out_rows, sem, k * out_rows, spans * out_rows)
    pltpu.make_async_copy(outer, outer, sem).wait()


def branch_back(meta, pairs, mixed, grads, gains, weights, heads, n, first):
    block, d = mixed.shape
    spans, qw = weights.shape[0], weights.shape[1] - first
    out_rows = share_rows(qw, n)
    whole = lambda a: pl.BlockSpec(a.shape, lambda i, meta: (0, 0))
    terms = [*pairs[0], *pairs[1]]
    shape = jax.ShapeDtypeStruct
    outs = [shape((block, d), F32), shape((1, d), F32)] + [shape((block, qw), BF)] * spans
    got = pl.pallas_call(
        functools.partial(branch_kernel, (first, n, spans)),
        grid_spec=pltpu.PrefetchScalarGridSpec(
            num_scalar_prefetch=1,
            grid=(1,),
            in_specs=[whole(t) for t in terms]
            + [whole(mixed), pl.BlockSpec((block, d), lambda i, meta: (meta[1], 0)), whole(gains), VMEM]
            + [whole(h) for h in heads],
            out_specs=[whole(o) for o in outs] + [ANY] * 2,
            scratch_shapes=[pltpu.VMEM((spans, n * out_rows, d), BF), pltpu.SemaphoreType.DMA],
        ),
        out_shape=outs + [shape((n // 2 * spans * out_rows, d), BF)] * 2,
        compiler_params=params(),
        cost_estimate=QUICK,
        name="branch_back",
    )(meta, *terms, mixed, grads, gains, weights, *heads)
    return got[0], got[1], got[2 : 2 + spans], got[2 + spans :]


def place_kernel(n, meta, *refs):
    pieces, out = refs[:n], refs[n]
    rows = out.shape[0] // n
    for k, piece in enumerate(pieces):
        block = lax.rem(meta[1] - k + n, n)
        out[pl.ds(pl.multiple_of(block * rows, rows), rows), :] = piece[:rows, :].astype(out.dtype)


def place(meta, pieces, rows, kind=BF):
    n, d = len(pieces), pieces[0].shape[1]
    return pl.pallas_call(
        functools.partial(place_kernel, n),
        in_specs=[SMEM] + [VMEM] * n,
        out_specs=VMEM,
        out_shape=jax.ShapeDtypeStruct((n * rows, d), kind),
        compiler_params=params(),
        cost_estimate=QUICK,
        name="place",
    )(meta, *pieces)


def norm_back(grad_normed, unit_rows, inverse, gain_row):
    scaled = grad_normed * gain_row
    return inverse * (scaled - unit_rows * jnp.mean(scaled * unit_rows, axis=-1, keepdims=True))


def feed_grads_kernel(cfg, hidden, d_inner, normed, grads, out):
    spans, fs = cfg
    units = spans * fs
    pairs = [(d_inner.at[:, :units], normed), (d_inner.at[:, units:], normed), (hidden, grads)]
    for kind, (left, right) in enumerate(pairs):
        product = mm(left[...], right[...], TN).astype(BF)
        for t in range(spans):
            out[t, kind * fs : (kind + 1) * fs] = product[t * fs : (t + 1) * fs]


def feed_grads(hidden, d_inner, normed, grads, fs):
    (rows, units), d = hidden.shape, normed.shape[1]
    return pl.pallas_call(
        functools.partial(feed_grads_kernel, (units // fs, fs)),
        in_specs=[VMEM] * 4,
        out_specs=VMEM,
        out_shape=jax.ShapeDtypeStruct((units // fs, 3 * fs, d), BF),
        compiler_params=params(),
        cost_estimate=QUICK,
        name="feed_grads",
    )(hidden, d_inner, normed, grads)


def share_rows(rows, n):
    return -(-rows // (16 * n)) * 16


def spread(meta, stage, sides, n, route, rows, sem, base=0, total=None):
    for m in range(n):
        at = pl.ds(pl.multiple_of(lax.bitwise_xor(meta[0], m) * rows, rows), rows)
        side, spot = reduce_place(n, route, m)
        first = spot * (total or rows) + base
        pltpu.make_async_copy(stage.at[at], sides[side].at[first : first + rows], sem).start()


def both(pair):
    return (pair[0][...].astype(F32) + pair[1][...].astype(F32)).astype(BF)


def late_kernel(cfg, meta, dq, dk_a, dk_b, dv_a, dv_b, normed, *refs):
    n, qw = cfg
    sides, (stage, sem) = refs[:2], refs[2:]
    used = 3 * qw
    if stage.shape[0] > used:
        stage[used:] = jnp.zeros((stage.shape[0] - used, stage.shape[1]), BF)
    for at, left in enumerate((dq[...], both((dk_a, dk_b)), both((dv_a, dv_b)))):
        stage[at * qw : (at + 1) * qw] = mm(left, normed[...], TN).astype(BF)
    spread(meta, stage, sides, n, 0, stage.shape[0] // n, sem)
    pltpu.make_async_copy(stage, stage, sem).wait()


def late_grads(meta, dq, dk, dv, normed, n):
    (tok, qw), d = dq.shape, normed.shape[1]
    rows = share_rows(3 * qw, n)
    return pl.pallas_call(
        functools.partial(late_kernel, (n, qw)),
        in_specs=[SMEM] + [VMEM] * 6,
        out_specs=[ANY] * 2,
        out_shape=[jax.ShapeDtypeStruct((n * rows // 2, d), BF)] * 2,
        scratch_shapes=[pltpu.VMEM((n * rows, d), BF), pltpu.SemaphoreType.DMA],
        compiler_params=params(),
        cost_estimate=QUICK,
        name="late_grads",
    )(meta, dq, *dk, *dv, normed)


def soap_kernel(cfg, meta, held, early, late, weight_ref, first_ref, second_ref, average_ref, stat_ref, basis_ref,
                weight_out, first_out, second_out, average_out, stat_out, turned_out, grads, wide, sem):
    n, late_panels, out_panels, pf, cap, rows, out_rows, group = cfg
    slots, panel, width = weight_ref.shape
    me, step = meta[0], pl.program_id(0)
    inner_panels = late_panels - out_panels

    def fetch(slot, source, share, base):
        grain = min(share, panel)
        for part in range(panel // grain):
            row = source * panel + part * grain
            at = gather_place(n, lax.bitwise_xor(me, row // share)) * (rows + out_rows) + base + row % share
            there = grads.at[slot, part * grain : (part + 1) * grain]
            pltpu.make_async_copy(late.at[pl.ds(pl.multiple_of(at, grain), grain)], there, sem).start()

    @pl.when(step == 0)
    def _():
        for slot in range(slots):
            source = held[slot]

            @pl.when(source < 0)
            def _(slot=slot):
                grads[slot] = jnp.zeros((panel, grads.shape[2]), BF)

            @pl.when((source >= 0) & (source < inner_panels))
            def _(slot=slot, source=source):
                fetch(slot, source, rows, 0)

            @pl.when((source >= inner_panels) & (source < late_panels))
            def _(slot=slot, source=source):
                fetch(slot, source - inner_panels, out_rows, rows)

            @pl.when(source >= late_panels)
            def _(slot=slot, source=source):
                kind, unit = (source - late_panels) // pf, (source - late_panels) % pf
                spot = (unit // cap) * 3 * cap + kind * cap + unit % cap
                pltpu.make_async_copy(early.at[spot], grads.at[slot], sem).start()

        for slot in range(slots):

            @pl.when(held[slot] >= 0)
            def _(slot=slot):
                pltpu.make_async_copy(grads.at[slot], grads.at[slot], sem).wait()

    high = functools.partial(lax.dot_general, precision=HIGH, preferred_element_type=F32)
    cols = pl.ds(pl.multiple_of(step * width, width), width)

    def parts(value):
        top = value.astype(BF)
        return top, (value - top.astype(F32)).astype(BF)

    for low in range(0, slots, group):
        count = min(group, slots - low)
        size = count * panel
        slot_range = slice(low, low + count)
        diagonal = wide.at[low // group]

        @pl.when(step == 0)
        def _(low=low, count=count, diagonal=diagonal):
            diagonal[...] = jnp.zeros_like(diagonal)
            for j in range(count):
                at = slice(j * panel, (j + 1) * panel)
                diagonal[at, at] = basis_ref[low + j]
                stat_out[low + j] = BETA_TWO * stat_ref[low + j]

        grad = grads[slot_range, :, cols].reshape(size, width)
        square = mm(grad, grad, NT)
        for j in range(count):
            at = slice(j * panel, (j + 1) * panel)
            stat_out[low + j] += (1.0 - BETA_TWO) * square[at, at]
        top, rest = parts(diagonal[:size, :size])
        flat = lambda ref, slot_range=slot_range, size=size: ref[slot_range].reshape(size, width)
        rotated = mm(top, grad, TN) + mm(rest, grad, TN)
        first = BETA_ONE * flat(first_ref) + (1.0 - BETA_ONE) * rotated
        second = BETA_TWO * flat(second_ref) + (1.0 - BETA_TWO) * rotated * rotated
        direction = (first / (1.0 - BETA_ONE**STEP)) / (
            jnp.sqrt(second / (1.0 - BETA_TWO**STEP)) + ADAM_EPSILON
        )
        high_part, low_part = parts(direction)
        update = mm(top, high_part, NN) + (mm(top, low_part, NN) + mm(rest, high_part, NN))
        weight = flat(weight_ref)
        new_weight = weight - RATE * (update + WEIGHT_DECAY * weight)
        average = AVERAGE_DECAY * flat(average_ref) + (1.0 - AVERAGE_DECAY) * new_weight
        shape = (count, panel, width)
        first_out[slot_range] = first.reshape(shape)
        second_out[slot_range] = second.reshape(shape)
        weight_out[slot_range] = new_weight.reshape(shape)
        average_out[slot_range] = average.reshape(shape)

        @pl.when(step == pl.num_programs(0) - 1)
        def _(low=low, count=count):
            for j in range(count):
                turned_out[low + j] = high(stat_out[low + j], basis_ref[low + j], NN)


def soap(meta, held, early, late, n, weight, first, second, average, stat, basis, late_panels, out_panels, pf, cap, rows):
    slots, panel, d = weight.shape
    width, group = 256, 8
    out_rows = late.shape[0] // n - rows
    big = pl.BlockSpec((slots, panel, width), lambda i, meta, held: (0, 0, i))
    small = pl.BlockSpec((slots, panel, panel), lambda i, meta, held: (0, 0, 0))
    shape = jax.ShapeDtypeStruct
    return pl.pallas_call(
        functools.partial(soap_kernel, (n, late_panels, out_panels, pf, cap, rows, out_rows, group)),
        grid_spec=pltpu.PrefetchScalarGridSpec(
            num_scalar_prefetch=2,
            grid=(d // width,),
            in_specs=[ANY] * 2 + [big] * 4 + [small] * 2,
            out_specs=[big] * 4 + [small] * 2,
            scratch_shapes=[
                pltpu.VMEM((slots, panel, d), BF),
                pltpu.VMEM((-(-slots // group), group * panel, group * panel), F32),
                pltpu.SemaphoreType.DMA,
            ],
        ),
        out_shape=[shape((slots, panel, d), F32)] * 4 + [shape((slots, panel, panel), F32)] * 2,
        compiler_params=params(),
        cost_estimate=QUICK,
        name="soap",
    )(meta, held, early, late, weight, first, second, average, stat, basis)


def orthonormal_kernel(columns_ref, out_ref):
    size = columns_ref.shape[0]
    out_ref[...] = columns_ref[...]
    for i in range(size):
        vector = out_ref[i]
        vector = vector * lax.rsqrt(jnp.sum(vector * vector, axis=0, keepdims=True))
        out_ref[i] = vector
        if i < size - 1:
            rest = out_ref[i + 1 :]
            out_ref[i + 1 :] = rest - jnp.sum(rest * vector[None], axis=1, keepdims=True) * vector[None]


def orthonormal(matrix):
    columns = jnp.transpose(matrix, (2, 1, 0))
    found = pl.pallas_call(
        orthonormal_kernel,
        in_specs=[VMEM],
        out_specs=VMEM,
        out_shape=jax.ShapeDtypeStruct(columns.shape, F32),
        compiler_params=params(),
        name="orthonormal",
    )(columns)
    return jnp.transpose(found, (2, 1, 0))


def adam_gain(gradient, weight, first_state, second):
    new_first = BETA_ONE * first_state + (1.0 - BETA_ONE) * gradient
    new_second = BETA_TWO * second + (1.0 - BETA_TWO) * gradient * gradient
    direction = (
        new_first
        / (1.0 - BETA_ONE**STEP)
        / (jnp.sqrt(new_second / (1.0 - BETA_TWO**STEP)) + ADAM_EPSILON)
    )
    return (weight - GAIN_RATE * direction, new_first, new_second)


def back_kernel(meta, x_ref, dq, dk_a, dk_b, dv_a, dv_b, w_ref, out, gain_out):
    total = mm(dq[...], w_ref[0], NN) + mm(both((dk_a, dk_b)), w_ref[1], NN)
    total = total + mm(both((dv_a, dv_b)), w_ref[2], NN)
    out[...] = total.astype(BF)
    unit, _, _ = norm_rows(x_ref[...].astype(F32), 1.0)
    share = jnp.sum(total * unit, axis=0, keepdims=True)

    @pl.when(pl.program_id(0) == 0)
    def _():
        gain_out[...] = share

    @pl.when(pl.program_id(0) > 0)
    def _():
        gain_out[...] += share


def back_in(meta, x, dq, dk, dv, weights, n, low, high):
    tok, (_, qw, d) = dq.shape[0], weights.shape
    tile = tok // n
    rows = lambda w: pl.BlockSpec((tile, w), lambda i, meta: ((meta[1] - i - low + n) % n, 0))
    whole = pl.BlockSpec((3, qw, d), lambda i, meta: (0, 0, 0))
    return pl.pallas_call(
        back_kernel,
        grid_spec=pltpu.PrefetchScalarGridSpec(
            num_scalar_prefetch=1,
            grid=(high - low,),
            in_specs=[rows(d)] + [rows(qw)] * 5 + [whole],
            out_specs=[pl.BlockSpec((tile, d), lambda i, meta: (i, 0)), pl.BlockSpec((1, d), lambda i, meta: (0, 0))],
        ),
        out_shape=[jax.ShapeDtypeStruct(((high - low) * tile, d), BF), jax.ShapeDtypeStruct((1, d), F32)],
        compiler_params=params(),
        cost_estimate=QUICK,
        name="back_in",
    )(meta, x, dq, *dk, *dv, weights)


def shards(
    tokens,
    cotangent,
    lengths,
    retrieve,
    owners,
    masters,
    first_moment,
    second_moment,
    averaged,
    statistics,
    bases,
    gains,
    gain_first,
    gain_second,
):
    tok, d = tokens.shape
    n_seq, n_tp = lax.axis_size("seq"), lax.axis_size("tp")
    me, z = lax.axis_index("seq"), lax.axis_index("tp")
    qw, ff = H // n_tp * HD, FF // n_tp
    slots_dev, panel = masters.shape[1:3]
    split = (slots_dev + 1) // 2
    docs, picks = lengths.shape[0], retrieve.shape[1]
    recalled = lax.dynamic_index_in_dim(retrieve, me, 0, keepdims=False)
    meta = jnp.concatenate([jnp.stack([me, z]).astype(I32), lengths, recalled])
    block = tok // n_tp
    pq, pf = qw // panel, ff // panel
    cap = -(-pf // n_seq)
    fs = cap * panel
    slot_ids = me * slots_dev + jnp.arange(slots_dev, dtype=I32)
    panel_ids = jnp.arange(1, owners.shape[0] + 1, dtype=I32)
    held = jnp.sum(jnp.where(slot_ids[:, None] == owners[None, :], panel_ids[None, :], 0), axis=1) - 1

    def mine(rows):
        return lax.dynamic_slice_in_dim(rows, z * block, block, 0)

    def whole_tp(rows):
        return lax.all_gather(rows, "tp", axis=0, tiled=True)

    def whole_seq(rows):
        return lax.all_gather(rows, "seq", axis=0, tiled=True)

    own = masters[0].astype(BF)
    pieces, _ = gather_seq([own[:split], own[split:]], n_seq)
    pieces = list(zip(*pieces, strict=True))
    q, k, v, normed_one, inner, share = project_in(
        meta, owners, tokens, gains, pieces, pq, pf, cap, slots_dev, split
    )
    (keys, values), _ = gather_seq([k, v], n_seq)
    weights = whole_tp(share).reshape(n_tp, -1, d)
    own_grads, keys[n_seq - 2], values[n_seq - 2] = pin(mine(cotangent), keys[n_seq - 2], values[n_seq - 2])
    grads_all = direct_pieces(own_grads, n_seq)
    turned_heads, wide, logs = attend(meta, q, keys, values, docs, picks, block)
    turned_heads, grads_all = pin(turned_heads, grads_all)
    heads = trade_tp(turned_heads, n_tp)
    mixed, left, right = mix(meta, tokens, gains, weights, heads)
    left, grads_all = pin(left, grads_all)
    grads_all = core_gather(jnp.concatenate(grads_all, axis=0), n_seq)
    (left, right), _ = gather_seq([left, right], n_seq)
    (normed_two, hidden, d_inner), pairs, feed = feed_forward(meta, weights, grads_all, left + right, fs)

    last = len(routes(n_seq)[0])
    inner_rows, out_rows = share_rows(3 * qw, n_seq), share_rows(qw, n_seq)
    feed_sums_in = (hidden, d_inner, normed_two, grads_all)
    for at in range(last + 1):
        pairs = reduce_levels(pairs, n_seq, at)
        if at == last - 1:
            pairs, feed, feed_sums = pin(pairs, (feed[0], swap(feed[1], n_seq, 1)), feed_sums)
            feed = plus(*feed)
        elif at == 0:
            pairs, feed, feed_sums_in = pin(pairs, feed, feed_sums_in)
            feed_sums = feed_grads(*feed_sums_in, fs)
    d_mixed, grad_gain_two, d_heads, outer = branch_back(
        meta, pairs, mixed, cotangent, gains, weights, heads, n_seq, 3 * fs
    )
    d_heads = trade_tp(d_heads, n_tp)
    outer = plus(outer[0], swap(outer[1], n_seq, 1))

    size = n_tp * out_rows
    parts = {}
    for m in range(0, n_seq, 2):
        at = reduce_place(n_seq, 0, m)[1]
        parts[m] = jnp.concatenate([feed[at * block : (at + 1) * block], outer[at * size : (at + 1) * size]], axis=0)
    d_heads, parts, feed_sums = pin(d_heads, parts, feed_sums)
    parts = [swap(part, n_seq, m) if m else part for m, part in parts.items()]
    feed_sums = lax.psum_scatter(feed_sums.reshape(-1, d), "tp", scatter_dimension=0, tiled=True)
    dq, *pairs = attend_back(meta, q, d_heads, wide, logs, keys, values, docs, picks)
    parts, dq, pairs = pin(parts, dq, pairs)
    pairs = reduce_levels(pairs, n_seq, 0)
    total = sum(part.astype(F32) for part in parts)
    output = (mixed + total[:block]).astype(BF)
    outer = [total[block + k * out_rows : block + (k + 1) * out_rows].astype(BF) for k in range(n_tp)]
    outputs = [output]
    for at in range(last + 1):
        if at:
            pairs = reduce_levels(pairs, n_seq, at)
            while len(outputs) < n_tp and (at == last or len(outputs) < 1 + 2 * at):
                outputs.append(ring(outputs[-1], n_tp, 1))
        pairs, outputs, feed_sums, dq = pin(pairs, outputs, feed_sums, dq)
        if at == min(1, last):
            pairs, outer, held = pin(pairs, outer, held)
    dk, dv = pairs
    output = place(meta, outputs, block)
    early = whole_seq(feed_sums).reshape(-1, panel, d)

    inputs = (meta, tokens, dq, dk, dv, inner, n_tp)
    total, gain_a = back_in(*inputs, n_tp - 1, n_tp)
    total, lefts = pin(total, (dq, dk, dv))
    back_rest, gain_b = back_in(meta, tokens, *lefts, *inputs[5:], 0, n_tp - 1)
    gain_total = jnp.concatenate([gain_a + gain_b, grad_gain_two], axis=0)
    late = late_grads(meta, *lefts, normed_one, n_seq)

    def advance(late, step):
        if step == 1:
            late = plus(late[0], swap(late[1], n_seq, 1))
        elif step == 2:
            parts = direct_reduce(late, n_seq, inner_rows)
            late = sum(part.astype(F32) for part in parts).astype(BF)
            late = jnp.concatenate([late, outer], axis=0)
        elif step == 3:
            late = direct_gather(late, n_seq)
        elif step == 4:
            late = core_gather(late, n_seq)
        return late

    steps = max(2 * (n_tp - 1), 6)
    gain_steps = sum_steps(n_seq, n_tp)
    gather = []
    for step in range(steps):
        if step < n_tp - 1:
            k = n_tp - 2 - step
            came = ring(total, n_tp, -1)
            late = advance(late, step)
            if step == 0:
                outer = trade_tp(outer, n_tp)
            if step == 1:
                came, output = pin(came, output)
            for _ in range(min(len(gain_steps), 2 if 0 < step else 0)):
                gain_total = gain_steps.pop(0)(gain_total)
            came, late, back_rest, outer, held, gain_total = pin(came, late, back_rest, outer, held, gain_total)
            if step == 0:
                outer = sum(part.astype(F32) for part in outer).astype(BF)
            part = back_rest[k * block : (k + 1) * block]
            if k:
                total = plus(part, came)
                total, late, gain_total = pin(total, late, gain_total)
                continue
            d_normed_one = part.astype(F32) + came.astype(F32)
            unit_one, inverse_one, _ = norm_rows(mine(tokens).astype(F32), gains[0])
            grad_here = d_mixed + norm_back(d_normed_one, unit_one, inverse_one, gains[0])
            gather.append(grad_here.astype(BF))
            continue
        if len(gather) < n_tp:
            gather.append(ring(gather[-1], n_tp, 1))
        for _ in range(min(len(gain_steps), 1)):
            gain_total = gain_steps.pop(0)(gain_total)
        late = advance(late, step)
        if step == steps - 2:
            new_weight, new_first, new_second, new_average, new_stat, turned_basis = soap(
                meta, held, early, late, n_seq, masters[0], first_moment[0], second_moment[0], averaged[0],
                statistics[0], bases[0], 4 * pq, pq, pf, cap, inner_rows,
            )
            gather[-1], turned_basis, gain_total = pin(gather[-1], turned_basis, gain_total)
        elif step == steps - 1:
            new_basis = orthonormal(turned_basis)
            gather, new_basis, gain_total = pin(gather, new_basis, gain_total)
        else:
            gather[-1], late, gain_total = pin(gather[-1], late, gain_total)
    for step in gain_steps:
        gain_total = step(gain_total)
    grad_input = place(meta, gather, block, F32)
    new_gains, new_gain_first, new_gain_second = adam_gain(gain_total, gains, gain_first, gain_second)
    return (
        output,
        grad_input,
        new_weight[None],
        new_first[None],
        new_second[None],
        new_average[None],
        new_stat[None],
        new_basis[None],
        new_gains,
        new_gain_first,
        new_gain_second,
    )


def solution(mesh):
    by_token, by_slot = P("seq", None), P("tp", "seq", None, None)
    in_specs = (by_token, by_token, P(), P(), P()) + (by_slot,) * 6 + (P(),) * 3
    out_specs = (by_token, by_token) + (by_slot,) * 6 + (P(),) * 3
    return jax.shard_map(shards, mesh=mesh, in_specs=in_specs, out_specs=out_specs, check_vma=False)
```
